32 devices in a mesh: seq: 8 (over z, x), head: 4 (over y, core).
Axes of the slice: x: 2, y: 2, z: 4, core: 2. Of those that a mesh axis runs over, the one named last changes fastest.
Arguments:
- tokens: bfloat16 [8192, 1024], P('seq', 'head'), may hold values from -6 to 6
- lengths: int32 [3], replicated, may hold values from 256 to 7168, as said below
- norm1_gain: float32 [1024], replicated, may hold values from 0.25 to 1.75
- w_mixer: bfloat16 [1024, 6144], P(None, 'head'), may hold values from -0.1875 to 0.1875
- w_rates: bfloat16 [1024, 24], P(None, 'head'), may hold values from -0.1875 to 0.1875
- decay_log: float32 [8], P('head'), may hold values from -20 to -2
- rates_bias: float32 [24], P('head'), may hold values from -12 to 1
- conv_weight: float32 [4, 5120], P(None, 'head'), may hold values from -2.5 to 2.5
- out_gain: float32 [128], replicated, may hold values from 0.25 to 1.75
- w_out: bfloat16 [1024, 1024], P('head'), may hold values from -0.1875 to 0.1875
- norm2_gain: float32 [1024], replicated, may hold values from 0.25 to 1.75
- w_ffn_gate: bfloat16 [1024, 2816], P(None, 'head'), may hold values from -0.1875 to 0.1875
- w_ffn_up: bfloat16 [1024, 2816], P(None, 'head'), may hold values from -0.1875 to 0.1875
- w_ffn_down: bfloat16 [2816, 1024], P('head'), may hold values from -0.109375 to 0.109375
- out_grad: bfloat16 [8192, 1024], P('seq', 'head'), may hold values from -6 to 6
Outputs:
- output: bfloat16 [8192, 1024], P('seq', 'head')
- tokens_grad: bfloat16 [8192, 1024], P('seq', 'head')
- norm1_gain_grad: float32 [1024], replicated
- w_mixer_grad: float32 [1024, 6144], P('seq', 'head')
- w_rates_grad: float32 [1024, 24], P('seq', 'head')
- decay_log_grad: float32 [8], P('head')
- rates_bias_grad: float32 [24], P('head')
- conv_weight_grad: float32 [4, 5120], P(None, 'head')
- out_gain_grad: float32 [128], replicated
- w_out_grad: float32 [1024, 1024], P('head', 'seq')
- norm2_gain_grad: float32 [1024], replicated
- w_ffn_gate_grad: float32 [1024, 2816], P('seq', 'head')
- w_ffn_up_grad: float32 [1024, 2816], P('seq', 'head')
- w_ffn_down_grad: float32 [2816, 1024], P('head', 'seq')
The draws below stay inside these ranges and needn't reach their ends.
Inputs may be any that keep to these rules, and one draw needn't show every extreme that they name: 3 document lengths summing to 8192; the middle one is 7168; the first and the last sum to 1024, each 256 or more.
All inputs are finite; a program needn't handle non-finite values.
Results may differ from the reference program's by a relative error of at most 0.019.
Values may be sent and summed in bfloat16 or wider, within the bound.
No kernel may reach another device: no remote copies, remote signals or barrier semaphores. Data moves between devices by JAX's collectives and lax.ppermute only.
A program may use at most 192 MiB of HBM per device.

```python
import jax
import jax.numpy as jnp
from jax import lax

D = 1024
H = 8
DK = 128
DV = 128
NH = 2
FF = 2816
CONV = 4
GROUP = 64
MINLEN = 256
TOK_DEV = 1024
TOKENS = 8192
QKV = 640
MIXW = 768


def draw_lengths(key, part):
    key = jax.random.fold_in(key, 1)
    opening = jax.random.randint(key, (), MINLEN, TOK_DEV - MINLEN + 1).astype(jnp.int32)
    closing = (TOK_DEV - opening).astype(jnp.int32)
    middle = jnp.asarray(TOKENS - TOK_DEV, jnp.int32)
    return jnp.stack([opening, middle, closing]).astype(jnp.int32)


def head_speeds(key):
    ranks = jax.random.permutation(jax.random.fold_in(key, 11), H)
    return ranks < H // 2


def draw_decay_log(key, part):
    slowly = head_speeds(key)
    spread = jax.random.uniform(jax.random.fold_in(key, 12), (H,), jnp.float32)
    slow_rate = (0.2 + 0.8 * spread) / TOKENS
    fast_rate = 0.02 * jnp.exp(spread * jnp.log(3.0))
    return jnp.log(jnp.where(slowly, slow_rate, fast_rate)).astype(jnp.float32)


def draw_rates_bias(key, part):
    slowly = head_speeds(key)
    spread = jax.random.uniform(jax.random.fold_in(key, 13), (H, NH), jnp.float32)
    small_beta = (1.5 + 3.0 * spread) * DK / (16.0 * TOKENS)
    slow_bias = jnp.log(small_beta / (1.0 - small_beta))
    fast_bias = -0.5 + 1.5 * spread
    beta_bias = jnp.where(slowly[:, None], slow_bias, fast_bias)
    decay_bias = jax.random.uniform(jax.random.fold_in(key, 14), (H, 1), jnp.float32, -1.0, 1.0)
    return jnp.concatenate([beta_bias, decay_bias], axis=1).reshape(H * (NH + 1)).astype(jnp.float32)


def shard_levels(stream_key, extent, cuts, low, top_value):
    factor_of, own = 1.0, jax.random.fold_in(stream_key, 6)
    for position, parts in cuts:
        draws = jnp.exp(jax.random.uniform(jax.random.fold_in(own, position), (parts,), jnp.float32, low / len(cuts), top_value / len(cuts)))
        factor_of = factor_of * jnp.repeat(draws, extent[position] // parts).reshape([-1 if axis == position else 1 for axis in range(len(extent))])
    return factor_of


def noise(rng, dims, scale, most, shards=(), kind=jnp.bfloat16):
    values = scale * jax.random.normal(rng, dims, jnp.float32)
    if shards:
        values = values * shard_levels(rng, dims, shards, -0.22, 0.18)
    return jnp.clip(values, -most, most).astype(kind)


def setup_inputs(seed: int = 0) -> dict:
    key_list = jax.random.split(jax.random.key(seed), 16)
    return {
        "tokens": noise(key_list[0], (TOKENS, D), 1.0, 6.0, ((0, 8), (1, 4))),
        "lengths": draw_lengths(jax.random.fold_in(key_list[15], 71), 0),
        "norm1_gain": jnp.clip(1.0 + 0.15 * jax.random.normal(key_list[2], (D,), jnp.float32), 0.25, 1.75),
        "w_mixer": noise(key_list[3], (D, H * MIXW), D ** -0.5, 0.1875, ((1, 4),)),
        "w_rates": noise(key_list[4], (D, H * (NH + 1)), D ** -0.5, 0.1875, ((1, 4),)),
        "decay_log": draw_decay_log(jax.random.fold_in(key_list[15], 71), 0),
        "rates_bias": draw_rates_bias(jax.random.fold_in(key_list[15], 71), 0),
        "conv_weight": noise(key_list[7], (CONV, H * QKV), 0.5, 2.5, ((1, 4),), jnp.float32),
        "out_gain": jnp.clip(1.0 + 0.15 * jax.random.normal(key_list[8], (DV,), jnp.float32), 0.25, 1.75),
        "w_out": noise(key_list[9], (H * DV, D), (H * DV) ** -0.5, 0.1875, ((0, 4),)),
        "norm2_gain": jnp.clip(1.0 + 0.15 * jax.random.normal(key_list[10], (D,), jnp.float32), 0.25, 1.75),
        "w_ffn_gate": noise(key_list[11], (D, FF), D ** -0.5, 0.1875, ((1, 4),)),
        "w_ffn_up": noise(key_list[12], (D, FF), D ** -0.5, 0.1875, ((1, 4),)),
        "w_ffn_down": noise(key_list[13], (FF, D), FF ** -0.5, 0.109375, ((0, 4),)),
        "out_grad": noise(key_list[14], (TOKENS, D), 1.0, 6.0, ((0, 8), (1, 4))),
    }


EPS = 1e-06
HIGH = lax.Precision.HIGHEST

@jax.custom_vjp
def low(v):
    return lax.optimization_barrier(v.astype(jnp.bfloat16)).astype(jnp.float32)

@jax.custom_vjp
def low_back(v):
    return v

def low_keep(v):
    return (low(v), None)

def low_pass(kept, grad):
    return (grad,)

def back_keep(v):
    return (v, None)

def back_low(kept, grad):
    return (low(grad),)
low.defvjp(low_keep, low_pass)
low_back.defvjp(back_keep, back_low)

def matmul(leading, trailing):
    return jnp.dot(leading, trailing, precision=HIGH, preferred_element_type=jnp.float32)

def rms_norm(values, gain):
    return values * lax.rsqrt(lax.optimization_barrier(jnp.mean(values * values, axis=-1, keepdims=True)) + EPS) * gain

def unit_norm(values):
    return values * lax.rsqrt(lax.optimization_barrier(jnp.sum(values * values, axis=-1, keepdims=True)) + EPS)

def token_step(state, inputs):
    query, keys, values, betas, log_gate, keep_prev = inputs
    state = state * (keep_prev * jnp.exp(log_gate))[:, None, None]
    for step_no in range(NH):
        key_now = keys[:, step_no]
        recalled = jnp.einsum('hd,hdw->hw', key_now, state, precision=HIGH)
        state = state + (betas[:, step_no, None] * key_now)[:, :, None] * (values[:, step_no] - recalled)[:, None, :]
    return (state, jnp.einsum('hd,hdw->hw', query, state, precision=HIGH))

def reference(tokens, lengths, norm1_gain, w_mixer, w_rates, decay_log, rates_bias, conv_weight, out_gain, w_out, norm2_gain, w_ffn_gate, w_ffn_up, w_ffn_down, out_grad):
    ends = jnp.cumsum(lengths.astype(jnp.int32)).astype(jnp.int32)
    positions = jnp.arange(TOKENS, dtype=jnp.int32)
    docs = lax.optimization_barrier(jnp.sum((positions[:, None] >= ends[None, :]).astype(jnp.int32), axis=1)).astype(jnp.int32)
    prev_docs = jnp.concatenate([jnp.full((1,), -1, jnp.int32), docs[:-1]])
    keep_prev = (docs == prev_docs).astype(jnp.float32)

    def forward(inputs, gain_one, mixer_w, rates_w, decay_w, bias_w, conv_w, gain_out, out_w, gain_two, ffn_gate, ffn_up, ffn_down):
        h_one = low(rms_norm(inputs, gain_one))
        raw_mix = low_back(matmul(h_one, mixer_w)).reshape(TOKENS, H, MIXW)
        logits = (low_back(matmul(h_one, rates_w)) + bias_w).reshape(TOKENS, H, NH + 1)
        pre_conv = raw_mix[:, :, :QKV]
        gate_o = raw_mix[:, :, QKV:]
        taps = conv_w.reshape(CONV, H, QKV)
        mixed = jnp.zeros((TOKENS, H, QKV), jnp.float32)
        for offset in range(CONV):
            shifted = jnp.concatenate([jnp.zeros((offset, H, QKV), jnp.float32), pre_conv[:TOKENS - offset]], axis=0)
            doc_back = jnp.concatenate([jnp.full((offset,), -1, jnp.int32), docs[:TOKENS - offset]])
            mixed = mixed + jnp.where((doc_back == docs)[:, None, None], shifted, 0.0) * taps[CONV - 1 - offset]
        active = jax.nn.silu(mixed)
        query = unit_norm(active[:, :, :DK])
        keys = unit_norm(active[:, :, DK:DK + NH * DK].reshape(TOKENS, H, NH, DK))
        values = active[:, :, DK + NH * DK:].reshape(TOKENS, H, NH, DV)
        betas = jax.nn.sigmoid(logits[:, :, :NH])
        log_gate = -jnp.exp(decay_w) * jax.nn.softplus(logits[:, :, NH])
        block_len = GROUP // NH
        steps_in = (query, keys, values, betas, log_gate, keep_prev)
        blocked = jax.tree.map(lambda array: array.reshape((TOKENS // block_len, block_len) + array.shape[1:]), steps_in)
        run_block = jax.checkpoint(lambda state, block: lax.scan(token_step, state, block))
        _, outs = lax.scan(run_block, jnp.zeros((H, DK, DV), jnp.float32), blocked)
        attn = outs.reshape(TOKENS, H, DV)
        normed = (rms_norm(attn, gain_out) * jax.nn.silu(gate_o)).reshape(TOKENS, H * DV)
        branch = low_back(matmul(low(normed), out_w))
        resid = inputs + branch
        h_two = low(rms_norm(resid, gain_two))
        gate = low_back(matmul(h_two, ffn_gate))
        up_val = low_back(matmul(h_two, ffn_up))
        act_two = low(jax.nn.silu(gate) * up_val)
        return resid + matmul(act_two, ffn_down)
    params = (tokens.astype(jnp.float32), norm1_gain, w_mixer.astype(jnp.float32), w_rates.astype(jnp.float32), decay_log, rates_bias, conv_weight, out_gain, w_out.astype(jnp.float32), norm2_gain, w_ffn_gate.astype(jnp.float32), w_ffn_up.astype(jnp.float32), w_ffn_down.astype(jnp.float32))
    final, pull = jax.vjp(forward, *params)
    grads = pull(out_grad.astype(jnp.float32))
    return (final.astype(jnp.bfloat16), grads[0].astype(jnp.bfloat16), grads[1], grads[2], grads[3], grads[4], grads[5], grads[6], grads[7], grads[8], grads[9], grads[10], grads[11], grads[12])
```

```python
import functools

import jax
import jax.numpy as jnp
from jax import lax
from jax.experimental import pallas as pl
from jax.experimental.pallas import tpu as pltpu
from jax.sharding import PartitionSpec as P

DK = 128
DV = 128
NH = 2
CONV = 4
QKV = 640
MIXW = 768
EPS = 1e-06

CHUNK = 64
SPAN = 128
ROWS = 256
LEVELS = 6
HALO = 16

F32 = jnp.float32
BF16 = jnp.bfloat16

NN = (((1,), (0,)), ((), ()))
NT = (((1,), (1,)), ((), ()))
TN = (((0,), (0,)), ((), ()))

P_INV = 3
P_FWD = 3
P_STATE = 3
P_BWD = 3


def halves(value):
    high = value.astype(BF16)
    return high, (value - high.astype(F32)).astype(BF16)


def mm(left, right, dims=NN, passes=1):
    if passes == 1:
        return lax.dot_general(
            left.astype(BF16), right.astype(BF16), dims, preferred_element_type=F32
        )
    if passes == 6:
        return lax.dot_general(
            left, right, dims, precision=lax.Precision.HIGHEST, preferred_element_type=F32
        )
    left_h, left_l = halves(left)
    right_h, right_l = halves(right)
    dot = functools.partial(lax.dot_general, dimension_numbers=dims, preferred_element_type=F32)
    return dot(left_h, right_h) + (dot(left_h, right_l) + dot(left_l, right_h))


def iota(shape, axis):
    return lax.broadcasted_iota(jnp.int32, shape, axis)


def doc_of(place, marks, ends):
    count = jnp.zeros_like(place)
    for j in range(ends):
        count = count + jnp.where(place >= marks[1 + j], 1, 0)
    return jnp.where(place < 0, -1, count)


def doc_scalar(place, marks, ends):
    count = jnp.int32(0)
    for j in range(ends):
        count = count + (place >= marks[1 + j]).astype(jnp.int32)
    return jnp.where(place < 0, -1, count)


def conv_masks(start, marks, ends, rows, direction):
    place = start + iota((rows, DK), 0)
    here = doc_of(place, marks, ends)
    return [None] + [
        doc_of(place + direction * s, marks, ends) == here for s in range(1, CONV)
    ]


def softplus(v):
    return jnp.maximum(v, 0.0) + jnp.log1p(jnp.exp(-jnp.abs(v)))


def chunk_sum_matrix(upper):
    row, col = iota((SPAN, SPAN), 0), iota((SPAN, SPAN), 1)
    keep = (col >= row) if upper else (col <= row)
    keep = keep & ((row // CHUNK) == (col // CHUNK))
    return jnp.where(keep, 1.0, 0.0).astype(F32)


def part_columns(h, part):
    begin = h * QKV + part * DK
    return slice(begin, begin + DK)


def convolved(ext, conv, masks, h, part):
    cols = part_columns(h, part)
    total = ext[8 : 8 + SPAN, cols] * conv[CONV - 1 : CONV, cols]
    for s in range(1, CONV):
        moved = jnp.where(masks[s], ext[8 - s : 8 - s + SPAN, cols], 0.0)
        total = total + moved * conv[CONV - 1 - s : CONV - s, cols]
    return total


def two(array, c):
    piece = array[c * CHUNK : (c + 1) * CHUNK]
    return jnp.concatenate([piece, piece], axis=0)


def pair(first, second, c):
    at = slice(c * CHUNK, (c + 1) * CHUNK)
    return jnp.concatenate([first[at], second[at]], axis=0)


def unit_rows(v):
    scale = lax.rsqrt(jnp.sum(v * v, axis=-1, keepdims=True) + EPS)
    return v * scale, scale


def token_masks():
    row, col = iota((SPAN, SPAN), 0), iota((SPAN, SPAN), 1)
    tok_r, tok_c = row % CHUNK, col % CHUNK
    strict = (tok_c < tok_r) | ((tok_c == tok_r) & (row >= CHUNK) & (col < CHUNK))
    return tok_r ^ tok_c, strict


def gate_tiles(logits, alpha):
    gates = alpha * softplus(logits)
    sums = mm(chunk_sum_matrix(False), gates, NN, 6)
    flat = jnp.transpose(sums)[:8]
    turned = pltpu.roll(flat, CHUNK, 1)
    lane = iota(flat.shape, 1)
    first = jnp.where(lane < CHUNK, flat, turned)
    second = jnp.where(lane < CHUNK, turned, flat)
    return gates, sums, (first, second)


def spread_column(tile, col):
    return jnp.broadcast_to(tile[:, col : col + 1], (SPAN, DK))


def chunk_gates(span_start, marks, ends, sums, rows, h, c):
    start = span_start + c * CHUNK
    col_place = start + iota((CHUNK, SPAN), 0)
    row_place = start + iota((CHUNK, SPAN), 1) % CHUNK
    col_doc = doc_of(col_place, marks, ends)
    row_doc = doc_of(row_place, marks, ends)
    total = spread_column(sums, 3 * h + 2)[c * CHUNK : (c + 1) * CHUNK]
    across = rows[c][3 * h + 2 : 3 * h + 3]
    kept = (col_doc == row_doc) & (row_place <= col_place)
    decay = jnp.exp(jnp.where(kept, total - across, -1e30))
    doc_before = doc_scalar(start - 1, marks, ends)
    doc_last = doc_scalar(start + CHUNK - 1, marks, ends)
    last = total[CHUNK - 1 : CHUNK]
    opening = jnp.where(col_doc == doc_before, jnp.exp(total), 0.0)
    closing = jnp.where(col_doc == doc_last, jnp.exp(last - total), 0.0)
    whole = jnp.where(doc_before == doc_last, jnp.exp(last), 0.0)
    return decay, opening, closing, whole


def inverses(lowers, apart):
    eye = jnp.where(iota((SPAN, SPAN), 0) == iota((SPAN, SPAN), 1), 1.0, 0.0)
    result = [eye - jnp.where(apart == 0, lower, 0.0) for lower in lowers]
    for level in range(LEVELS):
        here = (apart >> level) == 1
        steps = [
            mm(inverse, jnp.where(here, lower, 0.0), NN, P_INV)
            for inverse, lower in zip(result, lowers)
        ]
        result = [
            inverse - mm(step, inverse, NN, P_INV) for inverse, step in zip(result, steps)
        ]
    return result


def rms_scale(values):
    return lax.rsqrt(jnp.mean(values * values, axis=-1, keepdims=True) + EPS)


def mixer_kernel(
    heads, ends, marks, x, x_halo, gain, w_mixer, w_rates, bias, alpha, conv,
    h_out, raw_out, rim_out, gate_out, logit_out, inv_out, map_out, state_out,
    read_out, own_out, far_out, end_out, ext, state,
):
    step = pl.program_id(0)
    span_start = marks[0] + step * SPAN

    def rounded_norm(rows):
        values = rows.astype(F32)
        return (values * rms_scale(values) * gain[...]).astype(BF16)

    @pl.when(step == 0)
    def _():
        halo = jnp.dot(rounded_norm(x_halo[...]), w_mixer[...], preferred_element_type=F32)
        for h in range(heads):
            ext[0:8, h * QKV : (h + 1) * QKV] = halo[HALO - 8 :, h * MIXW : h * MIXW + QKV]
        rim_out[...] = ext[0:8]
        for h in range(heads):
            state[h, :, :DV] = jnp.zeros((DK, DV), F32)
            state[h, :, DV:] = jnp.where(
                iota((DK, DK), 0) == iota((DK, DK), 1), 1.0, 0.0
            ).astype(F32)

    @pl.when(step > 0)
    def _():
        ext[0:8] = ext[SPAN : SPAN + 8]

    h_one = rounded_norm(x[...])
    h_out[...] = h_one
    raw = jnp.dot(h_one, w_mixer[...], preferred_element_type=F32)
    for h in range(heads):
        ext[8 : 8 + SPAN, h * QKV : (h + 1) * QKV] = raw[:, h * MIXW : h * MIXW + QKV]
        gate_out[:, h * DV : (h + 1) * DV] = raw[:, h * MIXW + QKV : (h + 1) * MIXW]
    raw_out[...] = ext[8 : 8 + SPAN]
    logits = jnp.dot(h_one, w_rates[...], preferred_element_type=F32) + bias[...]
    logit_out[...] = logits
    masks = conv_masks(span_start, marks, ends, SPAN, -1)
    apart, strict = token_masks()
    betas = jax.nn.sigmoid(logits)
    _, sums, rows = gate_tiles(logits, alpha[...])

    units = [(h, c) for h in range(heads) for c in range(SPAN // CHUNK)]
    parts = {}
    for h in range(heads):
        active = []
        for part in range(5):
            mixed = convolved(ext, conv, masks, h, part)
            active.append(mixed * jax.nn.sigmoid(mixed))
        unit = [unit_rows(active[part])[0] for part in range(3)]
        beta = [spread_column(betas, 3 * h + i) for i in range(NH)]
        parts[h] = (unit, active[3:], beta)

    lowers, reads, sides, lasts, wholes, queries = [], [], [], [], [], []
    for h, c in units:
        (query, key_a, key_b), (value_a, value_b), (beta_a, beta_b) = parts[h]
        keys, values, beta = (
            pair(key_a, key_b, c),
            pair(value_a, value_b, c),
            pair(beta_a, beta_b, c),
        )
        query_c = query[c * CHUNK : (c + 1) * CHUNK]
        decay, opening, closing, whole = chunk_gates(
            span_start, marks, ends, sums, rows, h, c
        )
        decay_two = jnp.concatenate([decay, decay], axis=0)
        opening_two = jnp.concatenate([opening, opening], axis=0)
        closing_two = jnp.concatenate([closing, closing], axis=0)
        lowers.append(
            jnp.where(strict, beta * decay_two * mm(keys, keys, NT, P_FWD), 0.0)
        )
        reads.append(decay * mm(query_c, keys, NT, P_FWD))
        sides.append(
            jnp.concatenate([beta * values, beta * opening_two * keys], axis=1)
        )
        lasts.append(closing_two * keys)
        wholes.append(whole)
        queries.append(opening * query_c)
    solved = inverses(lowers, apart)
    pieces = [mm(inverse, side, NN, P_FWD) for inverse, side in zip(solved, sides)]
    maps = [mm(last, piece, TN, P_FWD) for last, piece in zip(lasts, pieces)]
    seen = [mm(read, piece, NN, P_FWD) for read, piece in zip(reads, pieces)]
    diagonal = iota((DK, DK), 0) == iota((DK, DK), 1)
    for index, (h, c) in enumerate(units):
        inv_out[c, h] = solved[index]
        transfer = jnp.where(diagonal, wholes[index], 0.0) - maps[index][:, DV:]
        map_out[c, h] = transfer
        reader = queries[index] - seen[index][:, DV:]
        at, col = slice(c * CHUNK, (c + 1) * CHUNK), slice(h * DK, (h + 1) * DK)
        read_out[at, col] = reader
        before = state[h]
        state_out[c, h] = before
        both = mm(reader, before, NN, P_STATE)
        own_out[at, col] = seen[index][:, :DV] + both[:, :DV]
        far_out[at, col] = both[:, DV:]
        after = mm(transfer, before, NN, P_STATE)
        state[h, :, :DV] = after[:, :DV] + maps[index][:, :DV]
        state[h, :, DV:] = after[:, DV:]
    end_out[...] = state[...]


def block(shape, index):
    return pl.BlockSpec(shape, index)


def fixed(shape):
    return pl.BlockSpec(shape, lambda i: (0,) * len(shape))


SCALARS = pl.BlockSpec(memory_space=pltpu.SMEM)


def shape(dims, kind=F32):
    return jax.ShapeDtypeStruct(dims, kind)


def params(megabytes):
    return pltpu.CompilerParams(
        dimension_semantics=("arbitrary",), vmem_limit_bytes=megabytes << 20
    )


def mixer_forward(heads, ends, marks, x_all, rows, gain, w_mixer, w_rates, bias, alpha, conv):
    model = x_all.shape[1]
    steps, chunks, per = rows // SPAN, rows // CHUNK, SPAN // CHUNK
    wide = heads * QKV
    row = lambda width: block((SPAN, width), lambda i: (i, 0))
    cube = lambda last: block((per, heads, SPAN, last), lambda i: (i, 0, 0, 0))
    return pl.pallas_call(
        functools.partial(mixer_kernel, heads, ends),
        grid=(steps,),
        in_specs=[
            SCALARS,
            row(model),
            block((HALO, model), lambda i: (rows // HALO, 0)),
            fixed((1, model)),
            fixed(w_mixer.shape),
            fixed(w_rates.shape),
            fixed(bias.shape),
            fixed(alpha.shape),
            fixed(conv.shape),
        ],
        out_specs=[
            row(model),
            row(wide),
            fixed((8, wide)),
            row(heads * DV),
            row(DK),
            cube(SPAN),
            cube(DK),
            cube(DK + DV),
            row(heads * DK),
            row(heads * DV),
            row(heads * DK),
            fixed((heads, DK, DK + DV)),
        ],
        out_shape=[
            shape((rows, model), BF16),
            shape((rows, wide)),
            shape((8, wide)),
            shape((rows, heads * DV)),
            shape((rows, DK)),
            shape((chunks, heads, SPAN, SPAN)),
            shape((chunks, heads, DK, DK)),
            shape((chunks, heads, DK, DK + DV)),
            shape((rows, heads * DK)),
            shape((rows, heads * DV)),
            shape((rows, heads * DK)),
            shape((heads, DK, DK + DV)),
        ],
        scratch_shapes=[
            pltpu.VMEM((8 + SPAN, wide), F32),
            pltpu.VMEM((heads, DK, DK + DV), F32),
        ],
        compiler_params=params(40),
        name="mixer_forward",
    )(marks, x_all, x_all, gain, w_mixer, w_rates, bias, alpha, conv)


def branch_kernel(heads, place, maps, own, far, gate, gain, w_out, attn_out, normed_out, branch_out, start_out, start):
    @pl.when(pl.program_id(0) == 0)
    def _():
        start[...] = jnp.zeros_like(start)

        def join(j, carry):
            for h in range(heads):
                start[h] = (
                    mm(maps[j, h, :, DV:].astype(F32), start[h], NN, P_STATE)
                    + maps[j, h, :, :DV].astype(F32)
                )
            return carry

        lax.fori_loop(0, place[0], join, 0)
        start_out[...] = start[...]

    for h in range(heads):
        col = slice(h * DV, (h + 1) * DV)
        attn = own[:, col] + mm(far[:, col], start[h], NN, P_STATE)
        attn_out[:, col] = attn
        gates = gate[:, col]
        normed = attn * rms_scale(attn) * gain[...] * (gates * jax.nn.sigmoid(gates))
        normed_out[:, col] = normed.astype(BF16)
    branch_out[...] = jnp.dot(
        normed_out[...], w_out[...], preferred_element_type=F32
    ).astype(BF16)


def branch_forward(heads, place, maps, own, far, gate, gain, w_out):
    rows, model = own.shape[0], w_out.shape[1]
    wide = heads * DV
    row = lambda width: block((ROWS, width), lambda i: (i, 0))
    return pl.pallas_call(
        functools.partial(branch_kernel, heads),
        grid=(rows // ROWS,),
        in_specs=[
            SCALARS, fixed(maps.shape), row(wide), row(wide), row(wide), fixed(gain.shape), fixed(w_out.shape),
        ],
        out_specs=[row(wide), row(wide), row(model), fixed((heads, DK, DV))],
        out_shape=[
            shape((rows, wide)),
            shape((rows, wide), BF16),
            shape((rows, model), BF16),
            shape((heads, DK, DV)),
        ],
        scratch_shapes=[pltpu.VMEM((heads, DK, DV), F32)],
        compiler_params=params(32),
        name="branch_forward",
    )(place, maps, own, far, gate, gain, w_out)


def ffn_kernel(x, branch, grad, gain, w_gate, w_up, w_down, h_out, act_out, gg_out, gu_out, part_out, dh_out):
    resid = x[...].astype(F32) + branch[...].astype(F32)
    h_two = (resid * rms_scale(resid) * gain[...]).astype(BF16)
    h_out[...] = h_two
    gate = mm(h_two, w_gate[...])
    up = mm(h_two, w_up[...])
    sig = jax.nn.sigmoid(gate)
    silu = gate * sig
    act = (silu * up).astype(BF16)
    act_out[...] = act
    grad_act = mm(grad[...], w_down[...], NT)
    grad_gate = (grad_act * up * sig * (1.0 + gate * (1.0 - sig))).astype(BF16)
    grad_up = (grad_act * silu).astype(BF16)
    gg_out[...] = grad_gate
    gu_out[...] = grad_up
    dh_out[...] = (mm(grad_gate, w_gate[...], NT) + mm(grad_up, w_up[...], NT)).astype(BF16)
    part_out[...] = mm(act, w_down[...]).astype(BF16)


def ffn_pass(x_all, branch, grad, gain, w_gate, w_up, w_down):
    rows, model = branch.shape
    hidden = w_gate.shape[1]
    row = lambda width: block((ROWS, width), lambda i: (i, 0))
    return pl.pallas_call(
        ffn_kernel,
        grid=(rows // ROWS,),
        in_specs=[
            row(model), row(model), row(model), fixed(gain.shape), fixed(w_gate.shape), fixed(w_up.shape), fixed(w_down.shape),
        ],
        out_specs=[row(model), row(hidden), row(hidden), row(hidden), row(model), row(model)],
        out_shape=[
            shape((rows, model), BF16),
            shape((rows, hidden), BF16),
            shape((rows, hidden), BF16),
            shape((rows, hidden), BF16),
            shape((rows, model), BF16),
            shape((rows, model), BF16),
        ],
        compiler_params=params(48),
        name="ffn_pass",
    )(x_all, branch, grad, gain, w_gate, w_up, w_down)


def fold(value):
    return jnp.sum(value.reshape(value.shape[0] // 8, 8, value.shape[1]), axis=0)


def resid_kernel(
    heads, x, branch, dh, grad, gain, w_out, attn, gate, out_gain, far,
    resid_out, branch_grad_out, attn_grad_out, gate_grad_out, gain_grad_out, out_gain_grad_out, state_grad_out,
):
    @pl.when(pl.program_id(0) == 0)
    def _():
        gain_grad_out[...] = jnp.zeros_like(gain_grad_out)
        out_gain_grad_out[...] = jnp.zeros_like(out_gain_grad_out)
        state_grad_out[...] = jnp.zeros_like(state_grad_out)

    resid = x[...].astype(F32) + branch[...].astype(F32)
    scale = rms_scale(resid)
    unit = resid * scale
    grad_h = dh[...].astype(F32)
    gain_grad_out[...] += fold(grad_h * unit)
    lifted = grad_h * gain[...]
    grad_resid = grad[...].astype(F32) + scale * (
        lifted - unit * jnp.mean(lifted * unit, axis=-1, keepdims=True)
    )
    resid_out[...] = grad_resid
    grad_branch = grad_resid.astype(BF16)
    branch_grad_out[...] = grad_branch
    grad_normed = mm(grad_branch, w_out[...], NT)
    for h in range(heads):
        col = slice(h * DV, (h + 1) * DV)
        value, gates, back = attn[:, col], gate[:, col], grad_normed[:, col]
        scale_o = rms_scale(value)
        unit_o = value * scale_o
        sig = jax.nn.sigmoid(gates)
        silu = gates * sig
        gate_grad_out[:, col] = (
            back * unit_o * out_gain[...] * sig * (1.0 + gates * (1.0 - sig))
        ).astype(BF16)
        scaled = back * silu
        out_gain_grad_out[...] += fold(scaled * unit_o)
        lifted_o = scaled * out_gain[...]
        grad_attn = scale_o * (
            lifted_o - unit_o * jnp.mean(lifted_o * unit_o, axis=-1, keepdims=True)
        )
        attn_grad_out[:, col] = grad_attn
        state_grad_out[h] += mm(far[:, col], grad_attn, TN, P_STATE)


def resid_backward(heads, x_all, branch, dh, grad, gain, w_out, attn, gate, out_gain, far):
    rows, model = branch.shape
    wide = heads * DV
    row = lambda width: block((ROWS, width), lambda i: (i, 0))
    return pl.pallas_call(
        functools.partial(resid_kernel, heads),
        grid=(rows // ROWS,),
        in_specs=[
            row(model), row(model), row(model), row(model), fixed(gain.shape), fixed(w_out.shape),
            row(wide), row(wide), fixed(out_gain.shape), row(wide),
        ],
        out_specs=[
            row(model), row(model), row(wide), row(wide),
            fixed((8, model)), fixed((8, DV)), fixed((heads, DK, DV)),
        ],
        out_shape=[
            shape((rows, model)),
            shape((rows, model), BF16),
            shape((rows, wide)),
            shape((rows, wide), BF16),
            shape((8, model)),
            shape((8, DV)),
            shape((heads, DK, DV)),
        ],
        compiler_params=params(48),
        name="resid_backward",
    )(x_all, branch, dh, grad, gain, w_out, attn, gate, out_gain, far)


def mixer_back_kernel(
    heads, ends, steps, marks, place, maps, state_grads, start, raw, raw_before, rim, conv, logits, alpha,
    inv, transfers, states, end_state, reads, attn_grad, gate_grad,
    grad_raw_out, tail_out, rim_out, rates_out, sums_out, conv_out,
    ext, mixed_grad, carry, after,
):
    step = pl.program_id(0)
    at_step = steps - 1 - step
    span_start = marks[0] + at_step * SPAN
    wide = heads * QKV
    per = SPAN // CHUNK

    @pl.when(step == 0)
    def _():
        carry[...] = jnp.zeros_like(carry)
        count = maps.shape[0]

        def join(k, unused):
            j = count - 1 - k
            for h in range(heads):
                carry[h] = (
                    mm(maps[j, h, :, DV:].astype(F32), carry[h], TN, P_STATE)
                    + state_grads[j, h].astype(F32)
                )
            return unused

        lax.fori_loop(0, count - 1 - place[0], join, 0)
        for h in range(heads):
            after[h] = end_state[h, :, :DV] + mm(
                end_state[h, :, DV:], start[h], NN, P_STATE
            )
        mixed_grad[0:8] = jnp.zeros((8, wide), F32)
        mixed_grad[8 + SPAN :] = jnp.zeros((8, wide), F32)
        sums_out[...] = jnp.zeros_like(sums_out)
        conv_out[...] = jnp.zeros_like(conv_out)

    @pl.when(step > 0)
    def _():
        mixed_grad[8 + SPAN :] = mixed_grad[8:16]

    @pl.when(at_step == 0)
    def _():
        ext[0:8] = rim[...]

    @pl.when(at_step > 0)
    def _():
        ext[0:8] = raw_before[...]

    ext[8 : 8 + SPAN] = raw[...]
    masks = conv_masks(span_start, marks, ends, SPAN, -1)
    apart, strict = token_masks()
    logit = logits[...]
    betas = jax.nn.sigmoid(logit)
    gates, sums, rows = gate_tiles(logit, alpha[...])

    parts = {}
    for h in range(heads):
        mixed = [convolved(ext, conv, masks, h, part) for part in range(5)]
        active = [m * jax.nn.sigmoid(m) for m in mixed]
        unit, scale = zip(*[unit_rows(active[part]) for part in range(3)])
        beta = [spread_column(betas, 3 * h + i) for i in range(NH)]
        parts[h] = (mixed, unit, scale, active[3:], beta)

    units = [(h, c) for h in range(heads) for c in range(per)]
    befores, grads_after, befores_next = {}, {}, {}
    for h in range(heads):
        for c in reversed(range(per)):
            at, col = slice(c * CHUNK, (c + 1) * CHUNK), slice(h * DK, (h + 1) * DK)
            befores[h, c] = states[c, h, :, :DV] + mm(
                states[c, h, :, DV:], start[h], NN, P_STATE
            )
            befores_next[h, c] = after[h] if c == per - 1 else befores[h, c + 1]
        for c in reversed(range(per)):
            at, col = slice(c * CHUNK, (c + 1) * CHUNK), slice(h * DK, (h + 1) * DK)
            grads_after[h, c] = carry[h]
            carry[h] = mm(reads[at, col], attn_grad[at, col], TN, P_STATE) + mm(
                transfers[c, h], carry[h], TN, P_STATE
            )
        after[h] = befores[h, 0]

    work = {}
    for h, c in units:
        _, unit, _, values, beta = parts[h]
        keys = pair(unit[1], unit[2], c)
        value = pair(values[0], values[1], c)
        beta_c = pair(beta[0], beta[1], c)
        query = unit[0][c * CHUNK : (c + 1) * CHUNK]
        decay, opening, closing, _ = chunk_gates(span_start, marks, ends, sums, rows, h, c)
        decay_two = jnp.concatenate([decay, decay], axis=0)
        opening_two = jnp.concatenate([opening, opening], axis=0)
        closing_two = jnp.concatenate([closing, closing], axis=0)
        grown = jnp.where(strict, decay_two * mm(keys, keys, NT, P_BWD), 0.0)
        read = decay * mm(query, keys, NT, P_BWD)
        recalled = opening_two * mm(keys, befores[h, c], NN, P_BWD)
        missing = value - recalled
        deltas = mm(inv[c, h], beta_c * missing, NN, P_BWD)
        at, col = slice(c * CHUNK, (c + 1) * CHUNK), slice(h * DK, (h + 1) * DK)
        out_grad = attn_grad[at, col]
        grad_deltas = mm(read, out_grad, TN, P_BWD) + mm(
            closing_two * keys, grads_after[h, c], NN, P_BWD
        )
        work[h, c] = [
            keys, query, beta_c, decay, decay_two, opening, opening_two, closing_two,
            grown, missing, deltas, out_grad, grad_deltas,
        ]
    columns = {}
    for h, c in units:
        (
            keys, query, beta, decay, decay_two, opening, opening_two, closing_two,
            grown, missing, deltas, out_grad, grad_deltas,
        ) = work[h, c]
        grad_target = mm(inv[c, h], grad_deltas, TN, P_BWD)
        grad_lower = jnp.where(strict, -mm(grad_target, deltas, NT, P_BWD), 0.0)
        grad_beta = jnp.sum(grad_lower * grown, axis=-1, keepdims=True) + jnp.sum(
            grad_target * missing, axis=-1, keepdims=True
        )
        grad_pairs = grad_lower * beta * decay_two
        grad_value = beta * grad_target
        grad_read = decay * mm(out_grad, deltas, NT, P_BWD)
        left = mm(grad_pairs, keys, NN, P_BWD) - beta * opening_two * mm(
            grad_target, befores[h, c], NT, P_BWD
        )
        right = (
            mm(grad_pairs, keys, TN, P_BWD)
            + closing_two * mm(deltas, grads_after[h, c], NT, P_BWD)
            + mm(grad_read, query, TN, P_BWD)
        )
        grad_query = mm(grad_read, keys, NN, P_BWD) + opening * mm(
            out_grad, befores[h, c], NT, P_BWD
        )
        in_left = jnp.sum(keys * left, axis=-1, keepdims=True)
        in_right = jnp.sum(keys * right, axis=-1, keepdims=True)
        in_query = jnp.sum(query * grad_query, axis=-1, keepdims=True)
        spare = in_left - in_right
        grad_total = spare[:CHUNK] + spare[CHUNK:] + in_query
        whole = jnp.sum(grads_after[h, c] * befores_next[h, c])
        last_row = iota((CHUNK, 1), 0) == CHUNK - 1
        grad_total = grad_total + jnp.where(last_row, whole, 0.0)
        columns[h, c] = (
            grad_query - query * in_query,
            left + right - keys * (in_left + in_right),
            grad_value,
            grad_beta,
            grad_total,
        )

    lane = iota((SPAN, DK), 1)
    rates = jnp.zeros((SPAN, DK), F32)
    for h in range(heads):
        mixed, unit, scale, values, beta = parts[h]
        got = [columns[h, c] for c in range(per)]
        low, high = slice(0, CHUNK), slice(CHUNK, 2 * CHUNK)
        stack = lambda index, part: jnp.concatenate([g[index][part] for g in got], axis=0)
        act_grads = [
            scale[0] * stack(0, low),
            scale[1] * stack(1, low),
            scale[2] * stack(1, high),
            stack(2, low),
            stack(2, high),
        ]
        for i, column in enumerate((stack(3, low), stack(3, high), stack(4, low))):
            rates = rates + jnp.where(lane == 3 * h + i, column, 0.0)
        for part in range(5):
            cols = part_columns(h, part)
            sig = jax.nn.sigmoid(mixed[part])
            grad = act_grads[part] * sig * (1.0 + mixed[part] * (1.0 - sig))
            mixed_grad[8 : 8 + SPAN, cols] = grad
            conv_out[24:32, cols] += fold(grad * ext[8 : 8 + SPAN, cols])
            for s in range(1, CONV):
                moved = jnp.where(masks[s], ext[8 - s : 8 - s + SPAN, cols], 0.0)
                tap = CONV - 1 - s
                conv_out[8 * tap : 8 * tap + 8, cols] += fold(grad * moved)

    ahead = conv_masks(span_start, marks, ends, SPAN, 1)
    for h in range(heads):
        for part in range(5):
            cols = part_columns(h, part)
            grad = mixed_grad[8 : 8 + SPAN, cols] * conv[CONV - 1 : CONV, cols]
            for s in range(1, CONV):
                moved = jnp.where(ahead[s], mixed_grad[8 + s : 8 + s + SPAN, cols], 0.0)
                grad = grad + moved * conv[CONV - 1 - s : CONV - s, cols]
            begin = h * MIXW + part * DK
            grad_raw_out[:, begin : begin + DK] = grad.astype(BF16)

            @pl.when(step == 0)
            def _():
                tail_out[:, cols] = grad[SPAN - HALO :]

        grad_raw_out[:, h * MIXW + QKV : (h + 1) * MIXW] = gate_grad[:, h * DV : (h + 1) * DV]

    @pl.when(at_step == 0)
    def _():
        rim_masks = conv_masks(marks[0] - 8, marks, ends, 8, 1)
        for h in range(heads):
            for part in range(5):
                cols = part_columns(h, part)
                grad = jnp.zeros((8, DK), F32)
                for s in range(1, CONV):
                    moved = jnp.where(rim_masks[s], mixed_grad[s : s + 8, cols], 0.0)
                    grad = grad + moved * conv[CONV - 1 - s : CONV - s, cols]
                rim_out[:, cols] = grad

    back = mm(chunk_sum_matrix(True), rates, NN, 6)
    lanes = iota((1, DK), 1)
    is_gate = (lanes % (NH + 1) == NH) & (lanes < heads * (NH + 1))
    grad_logits = jnp.where(is_gate, back * alpha[...] * betas, rates * betas * (1.0 - betas))
    rates_out[...] = grad_logits.astype(BF16)
    sums_out[0:8] += fold(grad_logits)
    sums_out[8:16] += fold(back * gates)


def mixer_backward(
    heads, ends, marks, place, maps, state_grads, start, raw, rim, conv, logits, alpha,
    inv, transfers, states, end_state, reads, attn_grad, gate_grad,
):
    rows, wide = raw.shape
    steps, per = rows // SPAN, SPAN // CHUNK
    turn = lambda i: steps - 1 - i
    row = lambda width: block((SPAN, width), lambda i: (turn(i), 0))
    cube = lambda last: block((per, heads, SPAN, last), lambda i: (turn(i), 0, 0, 0))
    return pl.pallas_call(
        functools.partial(mixer_back_kernel, heads, ends, steps),
        grid=(steps,),
        in_specs=[
            SCALARS,
            SCALARS,
            fixed(maps.shape),
            fixed(state_grads.shape),
            fixed(start.shape),
            row(wide),
            block((8, wide), lambda i: (jnp.maximum(turn(i) * (SPAN // 8) - 1, 0), 0)),
            fixed(rim.shape),
            fixed(conv.shape),
            row(DK),
            fixed(alpha.shape),
            cube(SPAN),
            cube(DK),
            cube(DK + DV),
            fixed(end_state.shape),
            row(heads * DK),
            row(heads * DV),
            row(heads * DV),
        ],
        out_specs=[
            row(heads * MIXW),
            fixed((HALO, wide)),
            fixed((8, wide)),
            row(DK),
            fixed((16, DK)),
            fixed((8 * CONV, wide)),
        ],
        out_shape=[
            shape((rows, heads * MIXW), BF16),
            shape((HALO, wide)),
            shape((8, wide)),
            shape((rows, DK), BF16),
            shape((16, DK)),
            shape((8 * CONV, wide)),
        ],
        scratch_shapes=[
            pltpu.VMEM((8 + SPAN, wide), F32),
            pltpu.VMEM((8 + SPAN + 8, wide), F32),
            pltpu.VMEM((heads, DK, DV), F32),
            pltpu.VMEM((heads, DK, DV), F32),
        ],
        compiler_params=params(48),
        name="mixer_backward",
    )(
        marks, place, maps, state_grads, start, raw, raw, rim, conv, logits, alpha,
        inv, transfers, states, end_state, reads, attn_grad, gate_grad,
    )


def shifted(value, axis, steps):
    count = lax.axis_size(axis)
    first, last = (max(0, -steps), min(count, count - steps))
    return lax.ppermute(value, axis, [(source, source + steps) for source in range(first, last)])


def dot_t(leading, trailing):
    return lax.dot_general(leading, trailing, NT, preferred_element_type=F32)


def t_dot(leading, trailing):
    return lax.dot_general(leading, trailing, TN, preferred_element_type=F32)


def norm_back(grad_unit, unit, inv_scale):
    return inv_scale * (grad_unit - unit * jnp.mean(grad_unit * unit, axis=-1, keepdims=True))


def local(
    tokens, lengths, norm1_gain, w_mixer, w_rates, decay_log, rates_bias, conv_weight,
    out_gain, w_out, norm2_gain, w_ffn_gate, w_ffn_up, w_ffn_down, out_grad,
):
    rows, share = tokens.shape
    heads = decay_log.shape[0]
    ends = lengths.shape[0]
    place = lax.axis_index("seq")
    col_start = lax.axis_index("head") * share
    marks = jnp.concatenate(
        [jnp.reshape(place * rows, (1,)), jnp.cumsum(lengths)]
    ).astype(jnp.int32)
    place_arg = jnp.reshape(place, (1,)).astype(jnp.int32)

    halo = shifted(tokens[rows - HALO :], "seq", 1)
    x_all = lax.all_gather(
        jnp.concatenate([tokens, halo], axis=0), "head", axis=1, tiled=True
    )
    grad_full = lax.all_gather(out_grad, "head", axis=1, tiled=True)
    gain_one, gain_two = norm1_gain[None, :], norm2_gain[None, :]
    gain_out = out_gain[None, :]
    spare = DK - heads * (NH + 1)
    rates_w = jnp.pad(w_rates, ((0, 0), (0, spare)))
    bias = jnp.pad(rates_bias, (0, spare))[None, :]
    none = jnp.zeros((heads,), F32)
    alpha = jnp.stack([none] * NH + [-jnp.exp(decay_log)], axis=-1).reshape(-1)
    alpha = jnp.pad(alpha, (0, spare))[None, :]

    (
        h_one, raw, rim, gate_o, logits, inv, transfers, states, reads, own, far, end_state,
    ) = mixer_forward(
        heads, ends, marks, x_all, rows, gain_one, w_mixer, rates_w, bias, alpha, conv_weight
    )
    maps = lax.all_gather(end_state.astype(BF16), "seq")
    attn, normed, branch_part, start = branch_forward(
        heads, place_arg, maps, own, far, gate_o, gain_out, w_out
    )
    branch = lax.psum(branch_part, "head")
    h_two, act, grad_gate, grad_up, ffn_part, dh_part = ffn_pass(
        x_all, branch, grad_full, gain_two, w_ffn_gate, w_ffn_up, w_ffn_down
    )
    dh = lax.psum(dh_part, "head")
    ffn_share = lax.psum_scatter(ffn_part, "head", scatter_dimension=1, tiled=True)
    grad_down = t_dot(act, grad_full)
    grad_wgate = t_dot(h_two, grad_gate)
    grad_wup = t_dot(h_two, grad_up)
    own_cols = lambda value: lax.dynamic_slice_in_dim(value, col_start, share, 1)
    resid_own = own_cols(x_all[:rows]).astype(F32) + own_cols(branch).astype(F32)
    output = (resid_own + ffn_share.astype(F32)).astype(BF16)

    (
        grad_resid, grad_branch, grad_attn, grad_gate_o, gain_two_part, out_gain_part, state_grad,
    ) = resid_backward(
        heads, x_all, branch, dh, grad_full, gain_two, w_out, attn, gate_o, gain_out, far
    )
    grad_wout = t_dot(normed, grad_branch)
    state_grads = lax.all_gather(state_grad.astype(BF16), "seq")
    grad_raw, tail, rim_grad, grad_rates, sums, conv_parts = mixer_backward(
        heads, ends, marks, place_arg, maps, state_grads, start, raw, rim, conv_weight, logits, alpha,
        inv, transfers, states, end_state, reads, grad_attn, grad_gate_o,
    )
    rim_back = shifted(rim_grad, "seq", -1)
    tail = tail.at[HALO - 8 :].add(rim_back)
    for h in range(heads):
        grad_raw = lax.dynamic_update_slice(
            grad_raw, tail[:, h * QKV : (h + 1) * QKV].astype(BF16), (rows - HALO, h * MIXW)
        )
    grad_wmixer = t_dot(h_one, grad_raw)
    grad_rates = grad_rates[:, : heads * (NH + 1)]
    grad_wrates = t_dot(h_one, grad_rates)
    grad_h_part = dot_t(grad_raw, w_mixer) + dot_t(grad_rates, w_rates)
    grad_h_one = lax.psum(grad_h_part.astype(BF16), "head").astype(F32)
    x_full = x_all[:rows].astype(F32)
    scale_one = rms_scale(x_full)
    unit_one = x_full * scale_one
    grad_norm1 = jnp.sum(grad_h_one * unit_one, axis=0)
    grad_tokens = grad_resid + norm_back(grad_h_one * norm1_gain, unit_one, scale_one)
    tokens_grad = own_cols(grad_tokens).astype(BF16)

    sum_rows = jnp.sum(sums.reshape(2, 8, DK), axis=1)
    grad_bias = sum_rows[0, : heads * (NH + 1)]
    grad_decay = sum_rows[1, : heads * (NH + 1)].reshape(heads, NH + 1)[:, NH]
    grad_conv = jnp.sum(conv_parts.reshape(CONV, 8, heads * QKV), axis=1)
    grad_outgain = lax.psum(jnp.sum(out_gain_part, axis=0), "head")
    small = lax.psum(
        (grad_norm1, grad_outgain, jnp.sum(gain_two_part, axis=0), grad_decay, grad_bias, grad_conv),
        "seq",
    )
    scatter = lambda value, axis: lax.psum_scatter(
        value.astype(BF16), "seq", scatter_dimension=axis, tiled=True
    ).astype(F32)
    return (
        output, tokens_grad, small[0], scatter(grad_wmixer, 0), scatter(grad_wrates, 0),
        small[3], small[4], small[5], small[1], scatter(grad_wout, 1), small[2],
        scatter(grad_wgate, 0), scatter(grad_wup, 0), scatter(grad_down, 1),
    )


def solution(mesh):
    placed = (
        P("seq", "head"), P(), P(), P(None, "head"), P(None, "head"), P("head"), P("head"), P(None, "head"),
        P(), P("head", None), P(), P(None, "head"), P(None, "head"), P("head", None), P("seq", "head"),
    )
    return jax.shard_map(
        local,
        mesh=mesh,
        in_specs=placed,
        out_specs=(
            P("seq", "head"), P("seq", "head"), P(), P("seq", "head"), P("seq", "head"), P("head"), P("head"),
            P(None, "head"), P(), P("head", "seq"), P(), P("seq", "head"), P("seq", "head"), P("head", "seq"),
        ),
        check_vma=False,
    )
```

```python
import functools

import jax
import jax.numpy as jnp
from jax import lax
from jax.experimental import pallas as pl
from jax.experimental.pallas import tpu as pltpu
from jax.sharding import PartitionSpec as P

DK = 128
DV = 128
NH = 2
CONV = 4
QKV = 640
MIXW = 768
EPS = 1e-06

CHUNK = 64
SPAN = 128
ROWS = 256
LEVELS = 6
HALO = 16

F32 = jnp.float32
BF16 = jnp.bfloat16

NN = (((1,), (0,)), ((), ()))
NT = (((1,), (1,)), ((), ()))
TN = (((0,), (0,)), ((), ()))

P_INV = 3
P_FWD = 3
P_STATE = 3
P_BWD = 3


def halves(value):
    high = value.astype(BF16)
    return high, (value - high.astype(F32)).astype(BF16)


def mm(left, right, dims=NN, passes=1):
    if passes == 1:
        return lax.dot_general(
            left.astype(BF16), right.astype(BF16), dims, preferred_element_type=F32
        )
    if passes == 6:
        return lax.dot_general(
            left, right, dims, precision=lax.Precision.HIGHEST, preferred_element_type=F32
        )
    left_h, left_l = halves(left)
    right_h, right_l = halves(right)
    dot = functools.partial(lax.dot_general, dimension_numbers=dims, preferred_element_type=F32)
    return dot(left_h, right_h) + (dot(left_h, right_l) + dot(left_l, right_h))


def iota(shape, axis):
    return lax.broadcasted_iota(jnp.int32, shape, axis)


def doc_of(place, marks, ends):
    count = jnp.zeros_like(place)
    for j in range(ends):
        count = count + jnp.where(place >= marks[1 + j], 1, 0)
    return jnp.where(place < 0, -1, count)


def doc_scalar(place, marks, ends):
    count = jnp.int32(0)
    for j in range(ends):
        count = count + (place >= marks[1 + j]).astype(jnp.int32)
    return jnp.where(place < 0, -1, count)


def conv_masks(start, marks, ends, rows, direction):
    place = start + iota((rows, DK), 0)
    here = doc_of(place, marks, ends)
    return [None] + [
        doc_of(place + direction * s, marks, ends) == here for s in range(1, CONV)
    ]


def softplus(v):
    return jnp.maximum(v, 0.0) + jnp.log1p(jnp.exp(-jnp.abs(v)))


def chunk_sum_matrix(upper):
    row, col = iota((SPAN, SPAN), 0), iota((SPAN, SPAN), 1)
    keep = (col >= row) if upper else (col <= row)
    keep = keep & ((row // CHUNK) == (col // CHUNK))
    return jnp.where(keep, 1.0, 0.0).astype(F32)


def part_columns(h, part):
    begin = h * QKV + part * DK
    return slice(begin, begin + DK)


def convolved(ext, conv, masks, h, part):
    cols = part_columns(h, part)
    total = ext[8 : 8 + SPAN, cols] * conv[CONV - 1 : CONV, cols]
    for s in range(1, CONV):
        moved = jnp.where(masks[s], ext[8 - s : 8 - s + SPAN, cols], 0.0)
        total = total + moved * conv[CONV - 1 - s : CONV - s, cols]
    return total


def two(array, c):
    piece = array[c * CHUNK : (c + 1) * CHUNK]
    return jnp.concatenate([piece, piece], axis=0)


def pair(first, second, c):
    at = slice(c * CHUNK, (c + 1) * CHUNK)
    return jnp.concatenate([first[at], second[at]], axis=0)


def unit_rows(v):
    scale = lax.rsqrt(jnp.sum(v * v, axis=-1, keepdims=True) + EPS)
    return v * scale, scale


def token_masks():
    row, col = iota((SPAN, SPAN), 0), iota((SPAN, SPAN), 1)
    tok_r, tok_c = row % CHUNK, col % CHUNK
    strict = (tok_c < tok_r) | ((tok_c == tok_r) & (row >= CHUNK) & (col < CHUNK))
    return tok_r ^ tok_c, strict


def gate_tiles(logits, alpha):
    gates = alpha * softplus(logits)
    sums = mm(chunk_sum_matrix(False), gates, NN, 6)
    flat = jnp.transpose(sums)[:8]
    turned = pltpu.roll(flat, CHUNK, 1)
    lane = iota(flat.shape, 1)
    first = jnp.where(lane < CHUNK, flat, turned)
    second = jnp.where(lane < CHUNK, turned, flat)
    return gates, sums, (first, second)


def spread_column(tile, col):
    return jnp.broadcast_to(tile[:, col : col + 1], (SPAN, DK))


def chunk_gates(span_start, marks, ends, sums, rows, h, c):
    start = span_start + c * CHUNK
    col_place = start + iota((CHUNK, SPAN), 0)
    row_place = start + iota((CHUNK, SPAN), 1) % CHUNK
    col_doc = doc_of(col_place, marks, ends)
    row_doc = doc_of(row_place, marks, ends)
    total = spread_column(sums, 3 * h + 2)[c * CHUNK : (c + 1) * CHUNK]
    across = rows[c][3 * h + 2 : 3 * h + 3]
    kept = (col_doc == row_doc) & (row_place <= col_place)
    decay = jnp.exp(jnp.where(kept, total - across, -1e30))
    doc_before = doc_scalar(start - 1, marks, ends)
    doc_last = doc_scalar(start + CHUNK - 1, marks, ends)
    last = total[CHUNK - 1 : CHUNK]
    opening = jnp.where(col_doc == doc_before, jnp.exp(total), 0.0)
    closing = jnp.where(col_doc == doc_last, jnp.exp(last - total), 0.0)
    whole = jnp.where(doc_before == doc_last, jnp.exp(last), 0.0)
    return decay, opening, closing, whole


def inverses(lowers, apart):
    eye = jnp.where(iota((SPAN, SPAN), 0) == iota((SPAN, SPAN), 1), 1.0, 0.0)
    result = [eye - jnp.where(apart == 0, lower, 0.0) for lower in lowers]
    for level in range(LEVELS):
        here = (apart >> level) == 1
        steps = [
            mm(inverse, jnp.where(here, lower, 0.0), NN, P_INV)
            for inverse, lower in zip(result, lowers)
        ]
        result = [
            inverse - mm(step, inverse, NN, P_INV) for inverse, step in zip(result, steps)
        ]
    return result


def rms_scale(values):
    return lax.rsqrt(jnp.mean(values * values, axis=-1, keepdims=True) + EPS)


def in_order(parts, me):
    bit = 1
    while bit < len(parts):
        flip = (me // bit) % 2 == 1
        parts = [jnp.where(flip, parts[m ^ bit], parts[m]) for m in range(len(parts))]
        bit *= 2
    return parts


def mixer_kernel(heads, ends, count, marks, who, *refs):
    tokens, halos, refs = refs[:count], refs[count : 2 * count], refs[2 * count :]
    (
        gain, w_mixer, w_rates, bias, alpha, conv,
        x_out, h_out, raw_out, rim_out, gate_out, logit_out, inv_out, map_out, state_out,
        read_out, own_out, far_out, end_out, ext, state,
    ) = refs
    step = pl.program_id(0)
    joined = lambda parts: jnp.concatenate(in_order([p[...] for p in parts], who[0]), axis=1)
    span_start = marks[0] + step * SPAN

    def rounded_norm(rows):
        values = rows.astype(F32)
        return (values * rms_scale(values) * gain[...]).astype(BF16)

    @pl.when(step == 0)
    def _():
        halo = jnp.dot(rounded_norm(joined(halos)), w_mixer[...], preferred_element_type=F32)
        for h in range(heads):
            ext[0:8, h * QKV : (h + 1) * QKV] = halo[HALO - 8 :, h * MIXW : h * MIXW + QKV]
        rim_out[...] = ext[0:8]
        for h in range(heads):
            state[h, :, :DV] = jnp.zeros((DK, DV), F32)
            state[h, :, DV:] = jnp.where(
                iota((DK, DK), 0) == iota((DK, DK), 1), 1.0, 0.0
            ).astype(F32)

    @pl.when(step > 0)
    def _():
        ext[0:8] = ext[SPAN : SPAN + 8]

    x = joined(tokens)
    x_out[...] = x
    h_one = rounded_norm(x)
    h_out[...] = h_one
    raw = jnp.dot(h_one, w_mixer[...], preferred_element_type=F32)
    for h in range(heads):
        ext[8 : 8 + SPAN, h * QKV : (h + 1) * QKV] = raw[:, h * MIXW : h * MIXW + QKV]
        gate_out[:, h * DV : (h + 1) * DV] = raw[:, h * MIXW + QKV : (h + 1) * MIXW]
    raw_out[...] = ext[8 : 8 + SPAN]
    logits = jnp.dot(h_one, w_rates[...], preferred_element_type=F32) + bias[...]
    logit_out[...] = logits
    masks = conv_masks(span_start, marks, ends, SPAN, -1)
    apart, strict = token_masks()
    betas = jax.nn.sigmoid(logits)
    _, sums, rows = gate_tiles(logits, alpha[...])

    units = [(h, c) for h in range(heads) for c in range(SPAN // CHUNK)]
    parts = {}
    for h in range(heads):
        active = []
        for part in range(5):
            mixed = convolved(ext, conv, masks, h, part)
            active.append(mixed * jax.nn.sigmoid(mixed))
        unit = [unit_rows(active[part])[0] for part in range(3)]
        beta = [spread_column(betas, 3 * h + i) for i in range(NH)]
        parts[h] = (unit, active[3:], beta)

    lowers, reads, sides, lasts, wholes, queries = [], [], [], [], [], []
    for h, c in units:
        (query, key_a, key_b), (value_a, value_b), (beta_a, beta_b) = parts[h]
        keys, values, beta = (
            pair(key_a, key_b, c),
            pair(value_a, value_b, c),
            pair(beta_a, beta_b, c),
        )
        query_c = query[c * CHUNK : (c + 1) * CHUNK]
        decay, opening, closing, whole = chunk_gates(
            span_start, marks, ends, sums, rows, h, c
        )
        decay_two = jnp.concatenate([decay, decay], axis=0)
        opening_two = jnp.concatenate([opening, opening], axis=0)
        closing_two = jnp.concatenate([closing, closing], axis=0)
        lowers.append(
            jnp.where(strict, beta * decay_two * mm(keys, keys, NT, P_FWD), 0.0)
        )
        reads.append(decay * mm(query_c, keys, NT, P_FWD))
        sides.append(
            jnp.concatenate([beta * values, beta * opening_two * keys], axis=1)
        )
        lasts.append(closing_two * keys)
        wholes.append(whole)
        queries.append(opening * query_c)
    solved = inverses(lowers, apart)
    pieces = [mm(inverse, side, NN, P_FWD) for inverse, side in zip(solved, sides)]
    maps = [mm(last, piece, TN, P_FWD) for last, piece in zip(lasts, pieces)]
    seen = [mm(read, piece, NN, P_FWD) for read, piece in zip(reads, pieces)]
    diagonal = iota((DK, DK), 0) == iota((DK, DK), 1)
    for index, (h, c) in enumerate(units):
        inv_out[c, h] = solved[index]
        transfer = jnp.where(diagonal, wholes[index], 0.0) - maps[index][:, DV:]
        map_out[c, h] = transfer
        reader = queries[index] - seen[index][:, DV:]
        at, col = slice(c * CHUNK, (c + 1) * CHUNK), slice(h * DK, (h + 1) * DK)
        read_out[at, col] = reader
        before = state[h]
        state_out[c, h] = before
        both = mm(reader, before, NN, P_STATE)
        own_out[at, col] = seen[index][:, :DV] + both[:, :DV]
        far_out[at, col] = both[:, DV:]
        after = mm(transfer, before, NN, P_STATE)
        state[h, :, :DV] = after[:, :DV] + maps[index][:, :DV]
        state[h, :, DV:] = after[:, DV:]
    end_out[...] = state[...]


def block(shape, index):
    return pl.BlockSpec(shape, index)


def fixed(shape):
    return pl.BlockSpec(shape, lambda i: (0,) * len(shape))


SCALARS = pl.BlockSpec(memory_space=pltpu.SMEM)


def shape(dims, kind=F32):
    return jax.ShapeDtypeStruct(dims, kind)


def params(megabytes):
    return pltpu.CompilerParams(
        dimension_semantics=("arbitrary",), vmem_limit_bytes=megabytes << 20
    )


def mixer_forward(heads, ends, marks, who, tokens, halos, gain, w_mixer, w_rates, bias, alpha, conv):
    rows, share = tokens[0].shape
    model = gain.shape[1]
    steps, chunks, per = rows // SPAN, rows // CHUNK, SPAN // CHUNK
    wide = heads * QKV
    row = lambda width: block((SPAN, width), lambda i: (i, 0))
    cube = lambda last: block((per, heads, SPAN, last), lambda i: (i, 0, 0, 0))
    return pl.pallas_call(
        functools.partial(mixer_kernel, heads, ends, len(tokens)),
        grid=(steps,),
        in_specs=[SCALARS, SCALARS]
        + [row(share)] * len(tokens)
        + [fixed((HALO, share))] * len(halos)
        + [
            fixed((1, model)),
            fixed(w_mixer.shape),
            fixed(w_rates.shape),
            fixed(bias.shape),
            fixed(alpha.shape),
            fixed(conv.shape),
        ],
        out_specs=[
            row(model),
            row(model),
            row(wide),
            fixed((8, wide)),
            row(heads * DV),
            row(DK),
            cube(SPAN),
            cube(DK),
            cube(DK + DV),
            row(heads * DK),
            row(heads * DV),
            row(heads * DK),
            fixed((heads, DK, DK + DV)),
        ],
        out_shape=[
            shape((rows, model), BF16),
            shape((rows, model), BF16),
            shape((rows, wide)),
            shape((8, wide)),
            shape((rows, heads * DV)),
            shape((rows, DK)),
            shape((chunks, heads, SPAN, SPAN)),
            shape((chunks, heads, DK, DK)),
            shape((chunks, heads, DK, DK + DV)),
            shape((rows, heads * DK)),
            shape((rows, heads * DV)),
            shape((rows, heads * DK)),
            shape((heads, DK, DK + DV)),
        ],
        scratch_shapes=[
            pltpu.VMEM((8 + SPAN, wide), F32),
            pltpu.VMEM((heads, DK, DK + DV), F32),
        ],
        compiler_params=params(40),
        name="mixer_forward",
    )(marks, who, *tokens, *halos, gain, w_mixer, w_rates, bias, alpha, conv)


def branch_kernel(heads, pieces, place, who, maps, own, far, gate, gain, w_out, attn_out, normed_out, start_out, *refs):
    mine, other, start = refs[:pieces], refs[pieces : 2 * pieces], refs[2 * pieces]
    step = pl.program_id(0)

    @pl.when(step == 0)
    def _():
        start[...] = jnp.zeros_like(start)

        def join(j, carry):
            at = j ^ place[0]
            for h in range(heads):
                start[h] = (
                    mm(maps[at, h, :, DV:].astype(F32), start[h], NN, P_STATE)
                    + maps[at, h, :, :DV].astype(F32)
                )
            return carry

        lax.fori_loop(0, place[0], join, 0)
        start_out[...] = start[...]

    for h in range(heads):
        col = slice(h * DV, (h + 1) * DV)
        attn = own[:, col] + mm(far[:, col], start[h], NN, P_STATE)
        attn_out[:, col] = attn
        gates = gate[:, col]
        normed = attn * rms_scale(attn) * gain[...] * (gates * jax.nn.sigmoid(gates))
        normed_out[:, col] = normed.astype(BF16)
    branch = jnp.dot(normed_out[...], w_out[...], preferred_element_type=F32).astype(BF16)
    keep_half(step, who[0], branch, mine, other)


def keep_half(step, me, value, mine, other):
    for p in range(len(mine)):
        for half in range(2):

            @pl.when(step == 2 * p + half)
            def _():
                @pl.when(me % 2 == half)
                def _():
                    mine[p][...] = value

                @pl.when(me % 2 != half)
                def _():
                    other[p][...] = value


def branch_forward(heads, place, who, maps, own, far, gate, gain, w_out):
    rows, model = own.shape[0], w_out.shape[1]
    wide = heads * DV
    pieces = rows // (2 * ROWS)
    row = lambda width: block((ROWS, width), lambda i: (i, 0))
    return pl.pallas_call(
        functools.partial(branch_kernel, heads, pieces),
        grid=(rows // ROWS,),
        in_specs=[
            SCALARS, SCALARS, fixed(maps.shape), row(wide), row(wide), row(wide), fixed(gain.shape), fixed(w_out.shape),
        ],
        out_specs=[row(wide), row(wide), fixed((heads, DK, DV))]
        + [fixed((ROWS, model))] * (2 * pieces),
        out_shape=[shape((rows, wide)), shape((rows, wide), BF16), shape((heads, DK, DV))]
        + [shape((ROWS, model), BF16)] * (2 * pieces),
        scratch_shapes=[pltpu.VMEM((heads, DK, DV), F32)],
        compiler_params=params(32),
        name="branch_forward",
    )(place, who, maps, own, far, gate, gain, w_out)


def either(step, me, mine, other):
    return jnp.where(me % 2 == step, mine[...].astype(F32), other[...].astype(F32))


def ffn_kernel(count, filled, who, x, mine, other, *refs):
    grads, refs = refs[:count], refs[count:]
    gain, w_gate, w_up, w_down = refs[:4]
    refs = refs[4 + filled :]
    h_out, act_out, gg_out, gu_out, grad_out, dh_mine, dh_other = refs[:7]
    shares = refs[7:]
    step = pl.program_id(0)
    resid = x[...].astype(F32) + either(step, who[0], mine, other)
    h_two = (resid * rms_scale(resid) * gain[...]).astype(BF16)
    h_out[...] = h_two
    grad = jnp.concatenate(in_order([g[...] for g in grads], who[0]), axis=1)
    grad_out[...] = grad
    gate = mm(h_two, w_gate[...], NT)
    up = mm(h_two, w_up[...], NT)
    sig = jax.nn.sigmoid(gate)
    silu = gate * sig
    act = (silu * up).astype(BF16)
    act_out[...] = act
    grad_act = mm(grad, w_down[...], NT)
    grad_gate = (grad_act * up * sig * (1.0 + gate * (1.0 - sig))).astype(BF16)
    grad_up = (grad_act * silu).astype(BF16)
    gg_out[...] = grad_gate
    gu_out[...] = grad_up
    dh = (mm(grad_gate, w_gate[...]) + mm(grad_up, w_up[...])).astype(BF16)
    keep_half(step, who[0], dh, [dh_mine], [dh_other])
    part = mm(act, w_down[...]).astype(BF16)
    width = part.shape[1] // count
    part = in_order([part[:, m * width : (m + 1) * width] for m in range(count)], who[0])
    for m in range(count):
        shares[m][...] = part[m]


WHOLE = pl.BlockSpec(memory_space=pl.ANY)


def ffn_pass(piece, who, x_all, mine, other, grads, gain, w_gate, w_up, w_down, filled):
    rows, model = x_all.shape
    share = grads[0].shape[1]
    hidden = w_gate.shape[0]
    row = lambda width: block((ROWS, width), lambda i: (2 * piece + i, 0))
    here = lambda width: block((ROWS, width), lambda i: (i, 0))
    first = 8 + len(grads)
    return pl.pallas_call(
        functools.partial(ffn_kernel, len(grads), len(filled)),
        grid=(2,),
        in_specs=[SCALARS, row(model), fixed(mine.shape), fixed(other.shape)]
        + [row(share)] * len(grads)
        + [fixed(gain.shape), fixed(w_gate.shape), fixed(w_up.shape), fixed(w_down.shape)]
        + [WHOLE] * len(filled),
        out_specs=[row(model), row(hidden), row(hidden), row(hidden), row(model)]
        + [fixed((ROWS, model))] * 2
        + [here(share)] * len(grads),
        out_shape=[
            shape((rows, model), BF16),
            shape((rows, hidden), BF16),
            shape((rows, hidden), BF16),
            shape((rows, hidden), BF16),
            shape((rows, model), BF16),
        ]
        + [shape((ROWS, model), BF16)] * 2
        + [shape((2 * ROWS, share), BF16)] * len(grads),
        input_output_aliases={first + k: k for k in range(len(filled))},
        compiler_params=params(48),
        name="ffn_pass",
    )(who, x_all, mine, other, *grads, gain, w_gate, w_up, w_down, *filled)


def fold(value):
    return jnp.sum(value.reshape(value.shape[0] // 8, 8, value.shape[1]), axis=0)


def resid_kernel(
    heads, filled, who, x, branch_mine, branch_other, dh_mine, dh_other, grad, gain, w_out, attn, gate, out_gain, far, *refs
):
    sums_before, refs = refs[filled - 3 : filled] if filled else None, refs[filled:]
    (
        branch_grad_out, attn_grad_out, gate_grad_out, resid_out,
        gain_grad_out, out_gain_grad_out, state_grad_out, resid_all,
    ) = refs
    step = pl.program_id(0)

    @pl.when(step == 0)
    def _():
        for at, total in enumerate((gain_grad_out, out_gain_grad_out, state_grad_out)):
            total[...] = sums_before[at][...] if filled else jnp.zeros_like(total)

    resid = x[...].astype(F32) + either(step, who[0], branch_mine, branch_other)
    scale = rms_scale(resid)
    unit = resid * scale
    grad_h = either(step, who[0], dh_mine, dh_other)
    gain_grad_out[...] += fold(grad_h * unit)
    lifted = grad_h * gain[...]
    grad_resid = grad[...].astype(F32) + scale * (
        lifted - unit * jnp.mean(lifted * unit, axis=-1, keepdims=True)
    )
    resid_all[...] = grad_resid
    share = resid_out.shape[1]
    resid_out[...] = resid_all[:, pl.ds(pl.multiple_of(who[0] * share, share), share)]
    grad_branch = grad_resid.astype(BF16)
    branch_grad_out[...] = grad_branch
    grad_normed = mm(grad_branch, w_out[...], NT)
    for h in range(heads):
        col = slice(h * DV, (h + 1) * DV)
        value, gates, back = attn[:, col], gate[:, col], grad_normed[:, col]
        scale_o = rms_scale(value)
        unit_o = value * scale_o
        sig = jax.nn.sigmoid(gates)
        silu = gates * sig
        gate_grad_out[:, col] = (
            back * unit_o * out_gain[...] * sig * (1.0 + gates * (1.0 - sig))
        ).astype(BF16)
        scaled = back * silu
        out_gain_grad_out[...] += fold(scaled * unit_o)
        lifted_o = scaled * out_gain[...]
        grad_attn = scale_o * (
            lifted_o - unit_o * jnp.mean(lifted_o * unit_o, axis=-1, keepdims=True)
        )
        attn_grad_out[:, col] = grad_attn
        state_grad_out[h] += mm(far[:, col], grad_attn, TN, P_STATE)


def resid_backward(
    heads, piece, who, share, x_all, branch, dh, grad, gain, w_out, attn, gate, out_gain, far, filled
):
    rows, model = x_all.shape
    wide = heads * DV
    row = lambda width: block((ROWS, width), lambda i: (2 * piece + i, 0))
    half = fixed((ROWS, model))
    first = 13
    sums = [fixed((8, model)), fixed((8, DV)), fixed((heads, DK, DV))]
    return pl.pallas_call(
        functools.partial(resid_kernel, heads, len(filled)),
        grid=(2,),
        in_specs=[
            SCALARS, row(model), half, half, half, half, row(model), fixed(gain.shape), fixed(w_out.shape),
            row(wide), row(wide), fixed(out_gain.shape), row(wide),
        ]
        + ([WHOLE] * 4 + sums if filled else []),
        out_specs=[row(model), row(wide), row(wide), row(share)] + sums,
        out_shape=[
            shape((rows, model), BF16),
            shape((rows, wide)),
            shape((rows, wide), BF16),
            shape((rows, share)),
            shape((8, model)),
            shape((8, DV)),
            shape((heads, DK, DV)),
        ],
        scratch_shapes=[pltpu.VMEM((ROWS, model), F32)],
        input_output_aliases={first + k: k for k in range(4)} if filled else {},
        compiler_params=params(48),
        name="resid_backward",
    )(who, x_all, *branch, *dh, grad, gain, w_out, attn, gate, out_gain, far, *filled)


def mixer_back_kernel(
    heads, ends, steps, marks, place, maps, state_grads, start, raw, raw_before, rim, conv, logits, alpha,
    inv, transfers, states, end_state, reads, attn_grad, gate_grad,
    grad_raw_out, tail_out, rim_out, rates_out, sums_out, conv_out,
    ext, mixed_grad, carry, after,
):
    step = pl.program_id(0)
    at_step = steps - 1 - step
    span_start = marks[0] + at_step * SPAN
    wide = heads * QKV
    per = SPAN // CHUNK

    @pl.when(step == 0)
    def _():
        carry[...] = jnp.zeros_like(carry)
        count = maps.shape[0]

        def join(k, unused):
            at = (count - 1 - k) ^ place[0]
            for h in range(heads):
                carry[h] = (
                    mm(maps[at, h, :, DV:].astype(F32), carry[h], TN, P_STATE)
                    + state_grads[at, h].astype(F32)
                )
            return unused

        lax.fori_loop(0, count - 1 - place[0], join, 0)
        for h in range(heads):
            after[h] = end_state[h, :, :DV] + mm(
                end_state[h, :, DV:], start[h], NN, P_STATE
            )
        mixed_grad[0:8] = jnp.zeros((8, wide), F32)
        mixed_grad[8 + SPAN :] = jnp.zeros((8, wide), F32)
        sums_out[...] = jnp.zeros_like(sums_out)
        conv_out[...] = jnp.zeros_like(conv_out)

    @pl.when(step > 0)
    def _():
        mixed_grad[8 + SPAN :] = mixed_grad[8:16]

    @pl.when(at_step == 0)
    def _():
        ext[0:8] = rim[...]

    @pl.when(at_step > 0)
    def _():
        ext[0:8] = raw_before[...]

    ext[8 : 8 + SPAN] = raw[...]
    masks = conv_masks(span_start, marks, ends, SPAN, -1)
    apart, strict = token_masks()
    logit = logits[...]
    betas = jax.nn.sigmoid(logit)
    gates, sums, rows = gate_tiles(logit, alpha[...])

    parts = {}
    for h in range(heads):
        mixed = [convolved(ext, conv, masks, h, part) for part in range(5)]
        active = [m * jax.nn.sigmoid(m) for m in mixed]
        unit, scale = zip(*[unit_rows(active[part]) for part in range(3)])
        beta = [spread_column(betas, 3 * h + i) for i in range(NH)]
        parts[h] = (mixed, unit, scale, active[3:], beta)

    units = [(h, c) for h in range(heads) for c in range(per)]
    befores, grads_after, befores_next = {}, {}, {}
    for h in range(heads):
        for c in reversed(range(per)):
            at, col = slice(c * CHUNK, (c + 1) * CHUNK), slice(h * DK, (h + 1) * DK)
            befores[h, c] = states[c, h, :, :DV] + mm(
                states[c, h, :, DV:], start[h], NN, P_STATE
            )
            befores_next[h, c] = after[h] if c == per - 1 else befores[h, c + 1]
        for c in reversed(range(per)):
            at, col = slice(c * CHUNK, (c + 1) * CHUNK), slice(h * DK, (h + 1) * DK)
            grads_after[h, c] = carry[h]
            carry[h] = mm(reads[at, col], attn_grad[at, col], TN, P_STATE) + mm(
                transfers[c, h], carry[h], TN, P_STATE
            )
        after[h] = befores[h, 0]

    work = {}
    for h, c in units:
        _, unit, _, values, beta = parts[h]
        keys = pair(unit[1], unit[2], c)
        value = pair(values[0], values[1], c)
        beta_c = pair(beta[0], beta[1], c)
        query = unit[0][c * CHUNK : (c + 1) * CHUNK]
        decay, opening, closing, _ = chunk_gates(span_start, marks, ends, sums, rows, h, c)
        decay_two = jnp.concatenate([decay, decay], axis=0)
        opening_two = jnp.concatenate([opening, opening], axis=0)
        closing_two = jnp.concatenate([closing, closing], axis=0)
        grown = jnp.where(strict, decay_two * mm(keys, keys, NT, P_BWD), 0.0)
        read = decay * mm(query, keys, NT, P_BWD)
        recalled = opening_two * mm(keys, befores[h, c], NN, P_BWD)
        missing = value - recalled
        deltas = mm(inv[c, h], beta_c * missing, NN, P_BWD)
        at, col = slice(c * CHUNK, (c + 1) * CHUNK), slice(h * DK, (h + 1) * DK)
        out_grad = attn_grad[at, col]
        grad_deltas = mm(read, out_grad, TN, P_BWD) + mm(
            closing_two * keys, grads_after[h, c], NN, P_BWD
        )
        work[h, c] = [
            keys, query, beta_c, decay, decay_two, opening, opening_two, closing_two,
            grown, missing, deltas, out_grad, grad_deltas,
        ]
    columns = {}
    for h, c in units:
        (
            keys, query, beta, decay, decay_two, opening, opening_two, closing_two,
            grown, missing, deltas, out_grad, grad_deltas,
        ) = work[h, c]
        grad_target = mm(inv[c, h], grad_deltas, TN, P_BWD)
        grad_lower = jnp.where(strict, -mm(grad_target, deltas, NT, P_BWD), 0.0)
        grad_beta = jnp.sum(grad_lower * grown, axis=-1, keepdims=True) + jnp.sum(
            grad_target * missing, axis=-1, keepdims=True
        )
        grad_pairs = grad_lower * beta * decay_two
        grad_value = beta * grad_target
        grad_read = decay * mm(out_grad, deltas, NT, P_BWD)
        left = mm(grad_pairs, keys, NN, P_BWD) - beta * opening_two * mm(
            grad_target, befores[h, c], NT, P_BWD
        )
        right = (
            mm(grad_pairs, keys, TN, P_BWD)
            + closing_two * mm(deltas, grads_after[h, c], NT, P_BWD)
            + mm(grad_read, query, TN, P_BWD)
        )
        grad_query = mm(grad_read, keys, NN, P_BWD) + opening * mm(
            out_grad, befores[h, c], NT, P_BWD
        )
        in_left = jnp.sum(keys * left, axis=-1, keepdims=True)
        in_right = jnp.sum(keys * right, axis=-1, keepdims=True)
        in_query = jnp.sum(query * grad_query, axis=-1, keepdims=True)
        spare = in_left - in_right
        grad_total = spare[:CHUNK] + spare[CHUNK:] + in_query
        whole = jnp.sum(grads_after[h, c] * befores_next[h, c])
        last_row = iota((CHUNK, 1), 0) == CHUNK - 1
        grad_total = grad_total + jnp.where(last_row, whole, 0.0)
        columns[h, c] = (
            grad_query - query * in_query,
            left + right - keys * (in_left + in_right),
            grad_value,
            grad_beta,
            grad_total,
        )

    lane = iota((SPAN, DK), 1)
    rates = jnp.zeros((SPAN, DK), F32)
    for h in range(heads):
        mixed, unit, scale, values, beta = parts[h]
        got = [columns[h, c] for c in range(per)]
        low, high = slice(0, CHUNK), slice(CHUNK, 2 * CHUNK)
        stack = lambda index, part: jnp.concatenate([g[index][part] for g in got], axis=0)
        act_grads = [
            scale[0] * stack(0, low),
            scale[1] * stack(1, low),
            scale[2] * stack(1, high),
            stack(2, low),
            stack(2, high),
        ]
        for i, column in enumerate((stack(3, low), stack(3, high), stack(4, low))):
            rates = rates + jnp.where(lane == 3 * h + i, column, 0.0)
        for part in range(5):
            cols = part_columns(h, part)
            sig = jax.nn.sigmoid(mixed[part])
            grad = act_grads[part] * sig * (1.0 + mixed[part] * (1.0 - sig))
            mixed_grad[8 : 8 + SPAN, cols] = grad
            conv_out[24:32, cols] += fold(grad * ext[8 : 8 + SPAN, cols])
            for s in range(1, CONV):
                moved = jnp.where(masks[s], ext[8 - s : 8 - s + SPAN, cols], 0.0)
                tap = CONV - 1 - s
                conv_out[8 * tap : 8 * tap + 8, cols] += fold(grad * moved)

    ahead = conv_masks(span_start, marks, ends, SPAN, 1)
    for h in range(heads):
        for part in range(5):
            cols = part_columns(h, part)
            grad = mixed_grad[8 : 8 + SPAN, cols] * conv[CONV - 1 : CONV, cols]
            for s in range(1, CONV):
                moved = jnp.where(ahead[s], mixed_grad[8 + s : 8 + s + SPAN, cols], 0.0)
                grad = grad + moved * conv[CONV - 1 - s : CONV - s, cols]
            begin = h * MIXW + part * DK
            grad_raw_out[:, begin : begin + DK] = grad.astype(BF16)

            @pl.when(step == 0)
            def _():
                tail_out[:, cols] = grad[SPAN - HALO :]

        grad_raw_out[:, h * MIXW + QKV : (h + 1) * MIXW] = gate_grad[:, h * DV : (h + 1) * DV]

    @pl.when(at_step == 0)
    def _():
        rim_masks = conv_masks(marks[0] - 8, marks, ends, 8, 1)
        for h in range(heads):
            for part in range(5):
                cols = part_columns(h, part)
                grad = jnp.zeros((8, DK), F32)
                for s in range(1, CONV):
                    moved = jnp.where(rim_masks[s], mixed_grad[s : s + 8, cols], 0.0)
                    grad = grad + moved * conv[CONV - 1 - s : CONV - s, cols]
                rim_out[:, cols] = grad

    back = mm(chunk_sum_matrix(True), rates, NN, 6)
    lanes = iota((1, DK), 1)
    is_gate = (lanes % (NH + 1) == NH) & (lanes < heads * (NH + 1))
    grad_logits = jnp.where(is_gate, back * alpha[...] * betas, rates * betas * (1.0 - betas))
    rates_out[...] = grad_logits.astype(BF16)
    sums_out[0:8] += fold(grad_logits)
    sums_out[8:16] += fold(back * gates)


def mixer_backward(
    heads, ends, marks, place, maps, state_grads, start, raw, rim, conv, logits, alpha,
    inv, transfers, states, end_state, reads, attn_grad, gate_grad,
):
    rows, wide = raw.shape
    steps, per = rows // SPAN, SPAN // CHUNK
    turn = lambda i: steps - 1 - i
    row = lambda width: block((SPAN, width), lambda i: (turn(i), 0))
    cube = lambda last: block((per, heads, SPAN, last), lambda i: (turn(i), 0, 0, 0))
    return pl.pallas_call(
        functools.partial(mixer_back_kernel, heads, ends, steps),
        grid=(steps,),
        in_specs=[
            SCALARS,
            SCALARS,
            fixed(maps.shape),
            fixed(state_grads.shape),
            fixed(start.shape),
            row(wide),
            block((8, wide), lambda i: (jnp.maximum(turn(i) * (SPAN // 8) - 1, 0), 0)),
            fixed(rim.shape),
            fixed(conv.shape),
            row(DK),
            fixed(alpha.shape),
            cube(SPAN),
            cube(DK),
            cube(DK + DV),
            fixed(end_state.shape),
            row(heads * DK),
            row(heads * DV),
            row(heads * DV),
        ],
        out_specs=[
            row(heads * MIXW),
            fixed((HALO, wide)),
            fixed((8, wide)),
            row(DK),
            fixed((16, DK)),
            fixed((8 * CONV, wide)),
        ],
        out_shape=[
            shape((rows, heads * MIXW), BF16),
            shape((HALO, wide)),
            shape((8, wide)),
            shape((rows, DK), BF16),
            shape((16, DK)),
            shape((8 * CONV, wide)),
        ],
        scratch_shapes=[
            pltpu.VMEM((8 + SPAN, wide), F32),
            pltpu.VMEM((8 + SPAN + 8, wide), F32),
            pltpu.VMEM((heads, DK, DV), F32),
            pltpu.VMEM((heads, DK, DV), F32),
        ],
        compiler_params=params(48),
        name="mixer_backward",
    )(
        marks, place, maps, state_grads, start, raw, raw, rim, conv, logits, alpha,
        inv, transfers, states, end_state, reads, attn_grad, gate_grad,
    )


def input_kernel(count, who, x, gain, grad_raw, grad_rates, w_mixer, w_rates, gain_grad_out, dots_out, *shares):
    @pl.when(pl.program_id(0) == 0)
    def _():
        gain_grad_out[...] = jnp.zeros_like(gain_grad_out)

    back = mm(grad_raw[...], w_mixer[...], NT) + mm(grad_rates[...], w_rates[...], NT)
    values = x[...].astype(F32)
    unit = values * rms_scale(values)
    seen = back * unit
    gain_grad_out[...] += fold(seen)
    dots = jnp.sum(seen * gain[...], axis=-1, keepdims=True)
    dots_out[...] = jnp.transpose(jnp.broadcast_to(dots, (dots.shape[0], DK)))[:8]
    width = back.shape[1] // count
    back = back.astype(BF16)
    parts = in_order([back[:, m * width : (m + 1) * width] for m in range(count)], who[0])
    for m in range(count):
        shares[m][...] = parts[m]


def input_backward(count, who, x_all, gain, grad_raw, grad_rates, w_mixer, w_rates):
    rows, model = x_all.shape
    share = model // count
    row = lambda width: block((ROWS, width), lambda i: (i, 0))
    return pl.pallas_call(
        functools.partial(input_kernel, count),
        grid=(rows // ROWS,),
        in_specs=[
            SCALARS, row(model), fixed(gain.shape), row(grad_raw.shape[1]), row(DK), fixed(w_mixer.shape), fixed(w_rates.shape),
        ],
        out_specs=[fixed((8, model)), block((8, ROWS), lambda i: (0, i))] + [row(share)] * count,
        out_shape=[shape((8, model)), shape((8, rows))] + [shape((rows, share), BF16)] * count,
        compiler_params=params(40),
        name="input_backward",
    )(who, x_all, gain, grad_raw, grad_rates, w_mixer, w_rates)


def tokens_kernel(model, who, x, gain, resid_grad, dots, own, came, out):
    share = out.shape[1]
    cols = pl.ds(pl.multiple_of(who[0] * share, share), share)
    scale = rms_scale(x[...].astype(F32))
    unit = x[:, cols].astype(F32) * scale
    mean = jnp.transpose(dots[...])[:, :1] / model
    back = (own[...].astype(F32) + came[...].astype(F32)) * gain[:, cols]
    out[...] = (resid_grad[...] + scale * (back - unit * mean)).astype(BF16)


def tokens_backward(who, x_all, gain, resid_grad, dots, own, came):
    rows, model = x_all.shape
    share = own.shape[1]
    row = lambda width: block((ROWS, width), lambda i: (i, 0))
    return pl.pallas_call(
        functools.partial(tokens_kernel, model),
        grid=(rows // ROWS,),
        in_specs=[
            SCALARS, row(model), fixed(gain.shape), row(share), block((8, ROWS), lambda i: (0, i)), row(share), row(share),
        ],
        out_specs=row(share),
        out_shape=shape((rows, share), BF16),
        compiler_params=params(32),
        name="tokens_backward",
    )(who, x_all, gain, resid_grad, dots, own, came)


def shifted(value, axis, steps):
    count = lax.axis_size(axis)
    first, last = (max(0, -steps), min(count, count - steps))
    return lax.ppermute(value, axis, [(source, source + steps) for source in range(first, last)])


def swap(value, axis, mask):
    return lax.ppermute(value, axis, [(i, i ^ mask) for i in range(lax.axis_size(axis))])


def bits(axis):
    count, bit = lax.axis_size(axis), 1
    while bit < count:
        yield bit
        bit *= 2


def spread(value, axis, order):
    found = {0: value}
    for bit in order:
        found.update({m | bit: swap(v, axis, bit) for m, v in list(found.items())})
    return [found[m] for m in range(len(found))]


def spread_seq(value):
    found = {0: value}
    count = lax.axis_size("seq")
    for m in range(2, count, 2):
        found[m] = swap(value, "seq", m)
    for m in range(0, count, 2):
        found[m + 1] = swap(found[m], "seq", 1)
    return jnp.stack([found[m] for m in range(count)])


def summed_halves(mine, other):
    total = mine + swap(other, "head", 1)
    for bit in bits("head"):
        if bit > 1:
            total = total + swap(total, "head", bit)
    return total, swap(total, "head", 1)


def summed_shares(shares):
    live = dict(enumerate(shares))
    came = None
    for bit in bits("head"):
        if came is not None:
            live[0] = live[0] + came
        came = swap(live.pop(bit), "head", bit)
        for m in [m for m in live if m & bit]:
            live[m ^ bit] = live[m ^ bit] + swap(live.pop(m), "head", bit)
    return live[0], came


def summed(value, axis):
    for bit in bits(axis):
        value = value + swap(value, axis, bit)
    return value


def scattered(value, order):
    count, place = lax.axis_size("seq"), lax.axis_index("seq")
    rest = value.shape[1:]
    dims = len([1 for _ in bits("seq")])
    value = value.reshape((2,) * dims + rest)
    for bit in order:
        axis = dims - bit.bit_length()
        mine = (place // bit) % 2
        keep = lax.dynamic_slice_in_dim(value, mine, 1, axis)
        send = lax.dynamic_slice_in_dim(value, 1 - mine, 1, axis)
        value = keep + swap(send, "seq", bit)
    return value.reshape(rest)


def dot_t(leading, trailing):
    return lax.dot_general(leading, trailing, NT, preferred_element_type=F32)


def t_dot(leading, trailing):
    return lax.dot_general(leading, trailing, TN, preferred_element_type=F32)


def local(
    tokens, lengths, norm1_gain, w_mixer, w_rates, decay_log, rates_bias, conv_weight,
    out_gain, w_out, norm2_gain, w_ffn_gate, w_ffn_up, w_ffn_down, out_grad,
):
    rows, share = tokens.shape
    heads = decay_log.shape[0]
    ends = lengths.shape[0]
    model = norm1_gain.shape[0]
    group, ranges = lax.axis_size("head"), lax.axis_size("seq")
    place, member = lax.axis_index("seq"), lax.axis_index("head")
    marks = jnp.concatenate(
        [jnp.reshape(place * rows, (1,)), jnp.cumsum(lengths)]
    ).astype(jnp.int32)
    place_arg = jnp.reshape(place, (1,)).astype(jnp.int32)
    who = jnp.reshape(member, (1,)).astype(jnp.int32)
    up_bits, down_bits = list(bits("head")), list(bits("head"))[::-1]
    seq_bits = list(bits("seq"))

    token_parts = spread(tokens, "head", down_bits)
    halo_parts = spread(shifted(tokens[rows - HALO :], "seq", 1), "head", down_bits)
    gain_one, gain_two = norm1_gain[None, :], norm2_gain[None, :]
    gain_out = out_gain[None, :]
    spare = DK - heads * (NH + 1)
    rates_w = jnp.pad(w_rates, ((0, 0), (0, spare)))
    bias = jnp.pad(rates_bias, (0, spare))[None, :]
    none = jnp.zeros((heads,), F32)
    alpha = jnp.stack([none] * NH + [-jnp.exp(decay_log)], axis=-1).reshape(-1)
    alpha = jnp.pad(alpha, (0, spare))[None, :]

    (
        x_all, h_one, raw, rim, gate_o, logits, inv, transfers, states, reads, own, far, end_state,
    ) = mixer_forward(
        heads, ends, marks, who, token_parts, halo_parts, gain_one, w_mixer, rates_w, bias, alpha, conv_weight
    )
    grad_parts = spread(out_grad, "head", down_bits)
    maps = spread_seq(end_state.astype(BF16))
    attn, normed, start, *branch_parts = branch_forward(
        heads, place_arg, who, maps, own, far, gate_o, gain_out, w_out
    )
    pieces = len(branch_parts) // 2
    branch = [
        summed_halves(branch_parts[p], branch_parts[pieces + p]) for p in range(pieces)
    ]
    gate_t, up_t = w_ffn_gate.T, w_ffn_up.T
    filled, dh, ffn_shares = [], [], []
    for p in range(pieces):
        got = ffn_pass(
            p, who, x_all, *branch[p], grad_parts, gain_two, gate_t, up_t, w_ffn_down, filled
        )
        filled = got[:5]
        dh.append(summed_halves(got[5], got[6]))
        ffn_shares.append(got[7:])
    h_two, act, grad_gate, grad_up, grad_full = filled
    filled = []
    for p in range(pieces):
        filled = resid_backward(
            heads, p, who, share, x_all, branch[p], dh[p], grad_full, gain_two, w_out, attn, gate_o, gain_out, far, filled
        )
    grad_branch, grad_attn, grad_gate_o, resid_own, gain_two_part, out_gain_part, state_grad = filled

    by_owner = lambda value: jnp.swapaxes(
        value.reshape(value.shape[0], ranges, model // ranges), 0, 1
    ).astype(BF16)
    ffn_grads = jnp.concatenate(
        [by_owner(t_dot(act, grad_full)), by_owner(t_dot(grad_gate, h_two)), by_owner(t_dot(grad_up, h_two))],
        axis=1,
    )
    ffn_grads = lax.psum_scatter(ffn_grads, "seq", scatter_dimension=0, tiled=False)
    hidden = act.shape[1]
    grad_down, grad_wgate, grad_wup = (
        ffn_grads[k * hidden : (k + 1) * hidden].astype(F32) for k in range(3)
    )

    state_grads = spread_seq(state_grad.astype(BF16))
    grad_raw, tail, rim_grad, grad_rates, sums, conv_parts = mixer_backward(
        heads, ends, marks, place_arg, maps, state_grads, start, raw, rim, conv_weight, logits, alpha,
        inv, transfers, states, end_state, reads, grad_attn, grad_gate_o,
    )
    grad_wout = scattered(by_owner(t_dot(normed, grad_branch)), seq_bits).astype(F32)
    out_shares = [
        jnp.concatenate([s[m] for s in ffn_shares], axis=0) for m in range(group)
    ]
    first, second = summed_shares(out_shares)
    own_cols = lambda value: lax.dynamic_slice_in_dim(value, member * share, share, 1)
    branch_own = []
    for mine, other in branch:
        even = member % 2 == 0
        mine, other = own_cols(mine), own_cols(other)
        branch_own += [jnp.where(even, mine, other), jnp.where(even, other, mine)]
    output = (
        tokens.astype(F32)
        + jnp.concatenate(branch_own, axis=0).astype(F32)
        + (first.astype(F32) + second.astype(F32))
    ).astype(BF16)

    rim_back = shifted(rim_grad, "seq", -1)
    tail = tail.at[HALO - 8 :].add(rim_back)
    for h in range(heads):
        grad_raw = lax.dynamic_update_slice(
            grad_raw, tail[:, h * QKV : (h + 1) * QKV].astype(BF16), (rows - HALO, h * MIXW)
        )
    gain_one_part, dots, *back_shares = input_backward(
        group, who, x_all, gain_one, grad_raw, grad_rates, w_mixer, rates_w
    )
    back_own, back_came = summed_shares(back_shares)
    dots = summed(dots, "head")
    tokens_grad = tokens_backward(who, x_all, gain_one, resid_own, dots, back_own, back_came)

    grad_wmixer = t_dot(h_one, grad_raw).astype(BF16).reshape(ranges, model // ranges, heads * MIXW)
    cuts = 4
    width = heads * MIXW // cuts
    orders = [seq_bits] * (cuts - 1) + [seq_bits[1:] + seq_bits[:1]]
    grad_wmixer = jnp.concatenate(
        [
            scattered(grad_wmixer[:, :, k * width : (k + 1) * width], orders[k])
            for k in reversed(range(cuts))
        ][::-1],
        axis=1,
    ).astype(F32)
    grad_wrates = scattered(
        t_dot(grad_rates[:, : heads * (NH + 1)], h_one)
        .reshape(heads * (NH + 1), ranges, model // ranges)
        .swapaxes(0, 1),
        seq_bits,
    ).T

    sum_rows = jnp.sum(sums.reshape(2, 8, DK), axis=1)
    over_head = summed(
        jnp.concatenate([jnp.sum(gain_one_part, axis=0), jnp.sum(out_gain_part, axis=0)]), "head"
    )
    small = jnp.concatenate(
        [
            over_head,
            jnp.sum(gain_two_part, axis=0),
            sum_rows[0],
            sum_rows[1],
            jnp.sum(conv_parts.reshape(CONV, 8, heads * QKV), axis=1).reshape(-1),
        ]
    )
    small = summed(small.reshape(-1, DK), "seq").reshape(-1)
    cut = [model, DV, model, DK, DK]
    pieces_of, at = [], 0
    for size in cut:
        pieces_of.append(small[at : at + size])
        at += size
    grad_norm1, grad_outgain, grad_norm2, bias_row, decay_row = pieces_of
    grad_conv = small[at:].reshape(CONV, heads * QKV)
    grad_bias = bias_row[: heads * (NH + 1)]
    grad_decay = decay_row[: heads * (NH + 1)].reshape(heads, NH + 1)[:, NH]
    return (
        output, tokens_grad, grad_norm1, grad_wmixer, grad_wrates, grad_decay, grad_bias, grad_conv,
        grad_outgain, grad_wout, grad_norm2, grad_wgate.T, grad_wup.T, grad_down,
    )


def solution(mesh):
    placed = (
        P("seq", "head"), P(), P(), P(None, "head"), P(None, "head"), P("head"), P("head"), P(None, "head"),
        P(), P("head", None), P(), P(None, "head"), P(None, "head"), P("head", None), P("seq", "head"),
    )
    return jax.shard_map(
        local,
        mesh=mesh,
        in_specs=placed,
        out_specs=(
            P("seq", "head"), P("seq", "head"), P(), P("seq", "head"), P("seq", "head"), P("head"), P("head"),
            P(None, "head"), P(), P("head", "seq"), P(), P("seq", "head"), P("seq", "head"), P("head", "seq"),
        ),
        check_vma=False,
    )
```

```python
import functools

import jax
import jax.numpy as jnp
from jax import lax
from jax.experimental import pallas as pl
from jax.experimental.pallas import tpu as pltpu
from jax.sharding import PartitionSpec as P

DK = 128
DV = 128
NH = 2
CONV = 4
QKV = 640
MIXW = 768
EPS = 1e-06

CHUNK = 64
SPAN = 128
ROWS = 256
LEVELS = 6
HALO = 16

F32 = jnp.float32
BF16 = jnp.bfloat16

NN = (((1,), (0,)), ((), ()))
NT = (((1,), (1,)), ((), ()))
TN = (((0,), (0,)), ((), ()))

P_INV = 1
P_FWD = 3
P_STATE = 3
P_BWD = 1
P_SOLVE = 3
P_PAIR = 3


def halves(value):
    high = value.astype(BF16)
    return high, (value - high.astype(F32)).astype(BF16)


def mm(left, right, dims=NN, passes=1):
    if passes == 1:
        return lax.dot_general(
            left.astype(BF16), right.astype(BF16), dims, preferred_element_type=F32
        )
    if passes == 6:
        return lax.dot_general(
            left, right, dims, precision=lax.Precision.HIGHEST, preferred_element_type=F32
        )
    left_h, left_l = halves(left)
    right_h, right_l = halves(right)
    dot = functools.partial(lax.dot_general, dimension_numbers=dims, preferred_element_type=F32)
    return dot(left_h, right_h) + (dot(left_h, right_l) + dot(left_l, right_h))


def iota(shape, axis):
    return lax.broadcasted_iota(jnp.int32, shape, axis)


def doc_of(place, marks, ends):
    count = jnp.zeros_like(place)
    for j in range(ends):
        count = count + jnp.where(place >= marks[1 + j], 1, 0)
    return jnp.where(place < 0, -1, count)


def doc_scalar(place, marks, ends):
    count = jnp.int32(0)
    for j in range(ends):
        count = count + (place >= marks[1 + j]).astype(jnp.int32)
    return jnp.where(place < 0, -1, count)


def conv_masks(start, marks, ends, rows, direction):
    place = start + iota((rows, DK), 0)
    here = doc_of(place, marks, ends)
    return [None] + [
        doc_of(place + direction * s, marks, ends) == here for s in range(1, CONV)
    ]


def softplus(v):
    return jnp.maximum(v, 0.0) + jnp.log1p(jnp.exp(-jnp.abs(v)))


def chunk_sum_matrix(upper):
    row, col = iota((SPAN, SPAN), 0), iota((SPAN, SPAN), 1)
    keep = (col >= row) if upper else (col <= row)
    keep = keep & ((row // CHUNK) == (col // CHUNK))
    return jnp.where(keep, 1.0, 0.0).astype(F32)


def part_columns(h, part):
    begin = h * QKV + part * DK
    return slice(begin, begin + DK)


def convolved(ext, conv, masks, h, part):
    cols = part_columns(h, part)
    total = ext[8 : 8 + SPAN, cols] * conv[CONV - 1 : CONV, cols]
    for s in range(1, CONV):
        moved = jnp.where(masks[s], ext[8 - s : 8 - s + SPAN, cols], 0.0)
        total = total + moved * conv[CONV - 1 - s : CONV - s, cols]
    return total


def two(array, c):
    piece = array[c * CHUNK : (c + 1) * CHUNK]
    return jnp.concatenate([piece, piece], axis=0)


def pair(first, second, c):
    at = slice(c * CHUNK, (c + 1) * CHUNK)
    return jnp.concatenate([first[at], second[at]], axis=0)


def unit_rows(v):
    scale = lax.rsqrt(jnp.sum(v * v, axis=-1, keepdims=True) + EPS)
    return v * scale, scale


def token_masks():
    row, col = iota((SPAN, SPAN), 0), iota((SPAN, SPAN), 1)
    tok_r, tok_c = row % CHUNK, col % CHUNK
    strict = (tok_c < tok_r) | ((tok_c == tok_r) & (row >= CHUNK) & (col < CHUNK))
    return tok_r ^ tok_c, strict


def gate_tiles(logits, alpha):
    gates = alpha * softplus(logits)
    sums = mm(chunk_sum_matrix(False), gates, NN, 6)
    flat = jnp.transpose(sums)[:8]
    turned = pltpu.roll(flat, CHUNK, 1)
    lane = iota(flat.shape, 1)
    first = jnp.where(lane < CHUNK, flat, turned)
    second = jnp.where(lane < CHUNK, turned, flat)
    return gates, sums, (first, second)


def spread_column(tile, col):
    return jnp.broadcast_to(tile[:, col : col + 1], (SPAN, DK))


def chunk_gates(span_start, marks, ends, sums, rows, h, c):
    start = span_start + c * CHUNK
    col_place = start + iota((CHUNK, SPAN), 0)
    row_place = start + iota((CHUNK, SPAN), 1) % CHUNK
    col_doc = doc_of(col_place, marks, ends)
    row_doc = doc_of(row_place, marks, ends)
    total = spread_column(sums, 3 * h + 2)[c * CHUNK : (c + 1) * CHUNK]
    across = rows[c][3 * h + 2 : 3 * h + 3]
    kept = (col_doc == row_doc) & (row_place <= col_place)
    decay = jnp.exp(jnp.where(kept, total - across, -1e30))
    doc_before = doc_scalar(start - 1, marks, ends)
    doc_last = doc_scalar(start + CHUNK - 1, marks, ends)
    last = total[CHUNK - 1 : CHUNK]
    opening = jnp.where(col_doc == doc_before, jnp.exp(total), 0.0)
    closing = jnp.where(col_doc == doc_last, jnp.exp(last - total), 0.0)
    whole = jnp.where(doc_before == doc_last, jnp.exp(last), 0.0)
    return decay, opening, closing, whole


def inverses(lowers, apart):
    eye = jnp.where(iota((SPAN, SPAN), 0) == iota((SPAN, SPAN), 1), 1.0, 0.0)
    result = [eye - jnp.where(apart == 0, lower, 0.0) for lower in lowers]
    for level in range(LEVELS):
        here = (apart >> level) == 1
        steps = [
            mm(inverse, jnp.where(here, lower, 0.0), NN, P_INV)
            for inverse, lower in zip(result, lowers)
        ]
        result = [
            inverse - mm(step, inverse, NN, P_INV) for inverse, step in zip(result, steps)
        ]
    return result


def rms_scale(values):
    return lax.rsqrt(jnp.mean(values * values, axis=-1, keepdims=True) + EPS)


def in_order(parts, me):
    bit = 1
    while bit < len(parts):
        flip = (me // bit) % 2 == 1
        parts = [jnp.where(flip, parts[m ^ bit], parts[m]) for m in range(len(parts))]
        bit *= 2
    return parts


def mixer_kernel(heads, ends, count, marks, who, *refs):
    tokens, halos, refs = refs[:count], refs[count : 2 * count], refs[2 * count :]
    (
        gain, w_mixer, w_rates, bias, alpha, conv,
        x_out, h_out, halo_out, raw_out, rim_out, gate_out, logit_out, inv_out, map_out, state_out,
        read_out, own_out, far_out, end_out, ext, state,
    ) = refs
    step = pl.program_id(0)
    joined = lambda parts: jnp.concatenate(in_order([p[...] for p in parts], who[0]), axis=1)
    span_start = marks[0] + step * SPAN

    def rounded_norm(rows):
        values = rows.astype(F32)
        return (values * rms_scale(values) * gain[...]).astype(BF16)

    @pl.when(step == 0)
    def _():
        halo_out[...] = rounded_norm(joined(halos))
        halo = jnp.dot(halo_out[...], w_mixer[...], preferred_element_type=F32)
        for h in range(heads):
            ext[0:8, h * QKV : (h + 1) * QKV] = halo[HALO - 8 :, h * MIXW : h * MIXW + QKV]
        rim_out[...] = ext[0:8]
        for h in range(heads):
            state[h, :, :DV] = jnp.zeros((DK, DV), F32)
            state[h, :, DV:] = jnp.where(
                iota((DK, DK), 0) == iota((DK, DK), 1), 1.0, 0.0
            ).astype(F32)

    @pl.when(step > 0)
    def _():
        ext[0:8] = ext[SPAN : SPAN + 8]

    x = joined(tokens)
    x_out[...] = x
    h_one = rounded_norm(x)
    h_out[...] = h_one
    raw = jnp.dot(h_one, w_mixer[...], preferred_element_type=F32)
    for h in range(heads):
        ext[8 : 8 + SPAN, h * QKV : (h + 1) * QKV] = raw[:, h * MIXW : h * MIXW + QKV]
        gate_out[:, h * DV : (h + 1) * DV] = raw[:, h * MIXW + QKV : (h + 1) * MIXW]
    raw_out[...] = ext[8 : 8 + SPAN]
    logits = jnp.dot(h_one, w_rates[...], preferred_element_type=F32) + bias[...]
    logit_out[...] = logits
    masks = conv_masks(span_start, marks, ends, SPAN, -1)
    apart, strict = token_masks()
    betas = jax.nn.sigmoid(logits)
    _, sums, rows = gate_tiles(logits, alpha[...])

    units = [(h, c) for h in range(heads) for c in range(SPAN // CHUNK)]
    parts = {}
    for h in range(heads):
        active = []
        for part in range(5):
            mixed = convolved(ext, conv, masks, h, part)
            active.append(mixed * jax.nn.sigmoid(mixed))
        unit = [unit_rows(active[part])[0] for part in range(3)]
        beta = [spread_column(betas, 3 * h + i) for i in range(NH)]
        parts[h] = (unit, active[3:], beta)

    lowers, reads, sides, lasts, wholes, queries = [], [], [], [], [], []
    for h, c in units:
        (query, key_a, key_b), (value_a, value_b), (beta_a, beta_b) = parts[h]
        keys, values, beta = (
            pair(key_a, key_b, c),
            pair(value_a, value_b, c),
            pair(beta_a, beta_b, c),
        )
        query_c = query[c * CHUNK : (c + 1) * CHUNK]
        decay, opening, closing, whole = chunk_gates(
            span_start, marks, ends, sums, rows, h, c
        )
        decay_two = jnp.concatenate([decay, decay], axis=0)
        opening_two = jnp.concatenate([opening, opening], axis=0)
        closing_two = jnp.concatenate([closing, closing], axis=0)
        lowers.append(
            jnp.where(strict, beta * decay_two * mm(keys, keys, NT, P_FWD), 0.0)
        )
        reads.append(decay * mm(query_c, keys, NT, P_FWD))
        sides.append(
            jnp.concatenate([beta * values, beta * opening_two * keys], axis=1)
        )
        lasts.append(closing_two * keys)
        wholes.append(whole)
        queries.append(opening * query_c)
    solved = inverses(lowers, apart)
    pieces = [mm(inverse, side, NN, P_FWD) for inverse, side in zip(solved, sides)]
    maps = [mm(last, piece, TN, P_FWD) for last, piece in zip(lasts, pieces)]
    seen = [mm(read, piece, NN, P_FWD) for read, piece in zip(reads, pieces)]
    diagonal = iota((DK, DK), 0) == iota((DK, DK), 1)
    for index, (h, c) in enumerate(units):
        inv_out[c, h] = solved[index]
        transfer = jnp.where(diagonal, wholes[index], 0.0) - maps[index][:, DV:]
        map_out[c, h] = transfer
        reader = queries[index] - seen[index][:, DV:]
        at, col = slice(c * CHUNK, (c + 1) * CHUNK), slice(h * DK, (h + 1) * DK)
        read_out[at, col] = reader
        before = state[h]
        state_out[c, h] = before
        both = mm(reader, before, NN, P_STATE)
        own_out[at, col] = seen[index][:, :DV] + both[:, :DV]
        far_out[at, col] = both[:, DV:]
        after = mm(transfer, before, NN, P_STATE)
        state[h, :, :DV] = after[:, :DV] + maps[index][:, :DV]
        state[h, :, DV:] = after[:, DV:]
    end_out[...] = state[...].astype(BF16)


def block(shape, index):
    return pl.BlockSpec(shape, index)


def fixed(shape):
    return pl.BlockSpec(shape, lambda i: (0,) * len(shape))


def once(shape):
    return pl.BlockSpec(
        shape, lambda i: (0,) * len(shape), pipeline_mode=pl.Buffered(buffer_count=1)
    )


SCALARS = pl.BlockSpec(memory_space=pltpu.SMEM)


def shape(dims, kind=F32):
    return jax.ShapeDtypeStruct(dims, kind)


def params(megabytes):
    return pltpu.CompilerParams(
        dimension_semantics=("arbitrary",), vmem_limit_bytes=megabytes << 20
    )


def cost(microseconds):
    return pl.CostEstimate(
        flops=int(microseconds * 1.1e8), bytes_accessed=int(microseconds * 1e5), transcendentals=0
    )


WHOLE = pl.BlockSpec(memory_space=pl.ANY)


def mixer_forward(heads, ends, marks, who, tokens, gain, w_mixer, w_rates, bias, alpha, conv):
    rows, share = tokens[0].shape
    rows = rows - HALO
    model = gain.shape[1]
    steps, chunks, per = rows // SPAN, rows // CHUNK, SPAN // CHUNK
    wide = heads * QKV
    row = lambda width: block((SPAN, width), lambda i: (i, 0))
    cube = lambda last: block((per, heads, SPAN, last), lambda i: (i, 0, 0, 0))
    return pl.pallas_call(
        functools.partial(mixer_kernel, heads, ends, len(tokens)),
        grid=(steps,),
        in_specs=[SCALARS, SCALARS]
        + [row(share)] * len(tokens)
        + [block((HALO, share), lambda i: (rows // HALO, 0))] * len(tokens)
        + [
            fixed((1, model)),
            once(w_mixer.shape),
            once(w_rates.shape),
            fixed(bias.shape),
            fixed(alpha.shape),
            fixed(conv.shape),
        ],
        out_specs=[
            row(model),
            row(model),
            fixed((HALO, model)),
            row(wide),
            fixed((8, wide)),
            row(heads * DV),
            row(DK),
            cube(SPAN),
            cube(DK),
            cube(DK + DV),
            row(heads * DK),
            row(heads * DV),
            row(heads * DK),
            fixed((heads, DK, DK + DV)),
        ],
        out_shape=[
            shape((rows, model), BF16),
            shape((rows, model), BF16),
            shape((HALO, model), BF16),
            shape((rows, wide)),
            shape((8, wide)),
            shape((rows, heads * DV)),
            shape((rows, DK)),
            shape((chunks, heads, SPAN, SPAN)),
            shape((chunks, heads, DK, DK)),
            shape((chunks, heads, DK, DK + DV)),
            shape((rows, heads * DK)),
            shape((rows, heads * DV)),
            shape((rows, heads * DK)),
            shape((heads, DK, DK + DV), BF16),
        ],
        scratch_shapes=[
            pltpu.VMEM((8 + SPAN, wide), F32),
            pltpu.VMEM((heads, DK, DK + DV), F32),
        ],
        compiler_params=params(60),
        cost_estimate=cost(36),
        name="mixer_forward",
    )(marks, who, *tokens, *tokens, gain, w_mixer, w_rates, bias, alpha, conv)


def branch_kernel(heads, place, who, maps, own, far, gate, gain, w_out, *refs):
    attn_out, normed_out, start_out, mine, other, start = refs[-6:]
    step = pl.program_id(0)

    @pl.when(step == 0)
    def _():
        start[...] = jnp.zeros_like(start)

        def join(j, carry):
            at = j ^ place[0]
            for h in range(heads):
                start[h] = (
                    mm(maps[at, h, :, DV:].astype(F32), start[h], NN, P_STATE)
                    + maps[at, h, :, :DV].astype(F32)
                )
            return carry

        lax.fori_loop(0, place[0], join, 0)
        start_out[...] = start[...]

    for h in range(heads):
        col = slice(h * DV, (h + 1) * DV)
        attn = own[:, col] + mm(far[:, col], start[h], NN, P_STATE)
        attn_out[:, col] = attn
        gates = gate[:, col]
        normed = attn * rms_scale(attn) * gain[...] * (gates * jax.nn.sigmoid(gates))
        normed_out[:, col] = normed.astype(BF16)
    branch = jnp.dot(normed_out[...], w_out[...], preferred_element_type=F32).astype(BF16)
    keep_half(step, who[0], branch, mine, other)


def keep_half(step, me, value, mine, other):
    half = pl.num_programs(0) // 2
    at = pl.ds(pl.multiple_of(lax.rem(step, half) * ROWS, ROWS), ROWS)
    kept = (step >= half) == (lax.rem(me, 2) == 1)

    @pl.when(kept)
    def _():
        mine[at] = value

    @pl.when(jnp.logical_not(kept))
    def _():
        other[at] = value


def branch_forward(heads, place, who, maps, own, far, gate, gain, w_out, waits):
    rows, model = own.shape[0], w_out.shape[1]
    wide = heads * DV
    row = lambda width: block((ROWS, width), lambda i: (i, 0))
    return pl.pallas_call(
        functools.partial(branch_kernel, heads),
        grid=(rows // ROWS,),
        in_specs=[
            SCALARS, SCALARS, once(maps.shape), row(wide), row(wide), row(wide), fixed(gain.shape), once(w_out.shape),
        ]
        + [WHOLE] * len(waits),
        out_specs=[row(wide), row(wide), fixed((heads, DK, DV))]
        + [fixed((rows // 2, model))] * 2,
        out_shape=[shape((rows, wide)), shape((rows, wide), BF16), shape((heads, DK, DV))]
        + [shape((rows // 2, model), BF16)] * 2,
        scratch_shapes=[pltpu.VMEM((heads, DK, DV), F32)],
        compiler_params=params(14),
        cost_estimate=cost(3),
        name="branch_forward",
    )(place, who, maps, own, far, gate, gain, w_out, *waits)


def halves_spec(rows, width):
    half = rows // (2 * ROWS)
    return block((ROWS, width), lambda i: (lax.rem(i, half), 0))


def either(me, mine, other):
    step, half = pl.program_id(0), pl.num_programs(0) // 2
    kept = (step >= half) == (lax.rem(me, 2) == 1)
    return jnp.where(kept, mine[...].astype(F32), other[...].astype(F32))


def share_places(count):
    order, bit = [0], count // 2
    for bit in [1 << k for k in range(count.bit_length() - 1)][::-1]:
        order = order + [m | bit for m in order]
    return order


def keep_shares(step, value, me, kept, sent):
    count = 2 * kept.shape[0]
    width = value.shape[1] // count
    parts = in_order([value[:, m * width : (m + 1) * width] for m in range(count)], me)
    rows = pl.ds(pl.multiple_of(step * ROWS, ROWS), ROWS)
    for position, m in enumerate(share_places(count)):
        if position < count // 2:
            kept[position, rows] = parts[m]
        else:
            sent[position - count // 2, rows] = parts[m]


def ffn_kernel(count, who, x, mine, other, *refs):
    grads, refs = refs[:count], refs[count:]
    (
        gain, w_gate, w_up, w_down,
        h_out, act_out, gg_out, gu_out, grad_out, dh_mine, dh_other, kept, sent,
    ) = refs
    step = pl.program_id(0)
    resid = x[...].astype(F32) + either(who[0], mine, other)
    h_two = (resid * rms_scale(resid) * gain[...]).astype(BF16)
    h_out[...] = h_two
    grad = jnp.concatenate(in_order([g[...] for g in grads], who[0]), axis=1)
    grad_out[...] = grad
    gate = mm(h_two, w_gate[...], NT)
    up = mm(h_two, w_up[...], NT)
    sig = jax.nn.sigmoid(gate)
    silu = gate * sig
    act = (silu * up).astype(BF16)
    act_out[...] = act
    grad_act = mm(grad, w_down[...], NT)
    grad_gate = (grad_act * up * sig * (1.0 + gate * (1.0 - sig))).astype(BF16)
    grad_up = (grad_act * silu).astype(BF16)
    gg_out[...] = grad_gate
    gu_out[...] = grad_up
    dh = (mm(grad_gate, w_gate[...]) + mm(grad_up, w_up[...])).astype(BF16)
    keep_half(step, who[0], dh, dh_mine, dh_other)
    keep_shares(step, mm(act, w_down[...]).astype(BF16), who[0], kept, sent)


def ffn_pass(who, x_all, mine, other, grads, gain, w_gate, w_up, w_down):
    rows, model = x_all.shape
    share, count = grads[0].shape[1], len(grads)
    hidden = w_gate.shape[0]
    row = lambda width: block((ROWS, width), lambda i: (i, 0))
    half = halves_spec(rows, model)
    return pl.pallas_call(
        functools.partial(ffn_kernel, count),
        grid=(rows // ROWS,),
        in_specs=[SCALARS, row(model), half, half]
        + [row(share)] * count
        + [fixed(gain.shape), once(w_gate.shape), once(w_up.shape), once(w_down.shape)],
        out_specs=[row(model), row(hidden), row(hidden), row(hidden), row(model)]
        + [fixed((rows // 2, model))] * 2
        + [fixed((count // 2, rows, share))] * 2,
        out_shape=[
            shape((rows, model), BF16),
            shape((rows, hidden), BF16),
            shape((rows, hidden), BF16),
            shape((rows, hidden), BF16),
            shape((rows, model), BF16),
        ]
        + [shape((rows // 2, model), BF16)] * 2
        + [shape((count // 2, rows, share), BF16)] * 2,
        compiler_params=params(32),
        cost_estimate=cost(16),
        name="ffn_pass",
    )(who, x_all, mine, other, *grads, gain, w_gate, w_up, w_down)


def fold(value):
    return jnp.sum(value.reshape(value.shape[0] // 8, 8, value.shape[1]), axis=0)


def resid_kernel(
    heads, who, x, branch_mine, branch_other, dh_mine, dh_other, grad, gain, w_out, normed, attn, gate, out_gain, far,
    weight_out, attn_grad_out, gate_grad_out, resid_out,
    gain_grad_out, out_gain_grad_out, state_grad_out, resid_all, weight_sum,
):
    @pl.when(pl.program_id(0) == 0)
    def _():
        for total in (gain_grad_out, out_gain_grad_out, state_grad_out, weight_sum):
            total[...] = jnp.zeros_like(total)

    resid = x[...].astype(F32) + either(who[0], branch_mine, branch_other)
    scale = rms_scale(resid)
    unit = resid * scale
    grad_h = either(who[0], dh_mine, dh_other)
    gain_grad_out[...] += fold(grad_h * unit)
    lifted = grad_h * gain[...]
    grad_resid = grad[...].astype(F32) + scale * (
        lifted - unit * jnp.mean(lifted * unit, axis=-1, keepdims=True)
    )
    resid_all[...] = grad_resid
    share = resid_out.shape[1]
    resid_out[...] = resid_all[:, pl.ds(pl.multiple_of(who[0] * share, share), share)]
    grad_branch = grad_resid.astype(BF16)
    weight_sum[...] += mm(normed[...], grad_branch, TN)

    @pl.when(pl.program_id(0) == pl.num_programs(0) - 1)
    def _():
        weight_out[...] = weight_sum[...].astype(BF16)

    grad_normed = mm(grad_branch, w_out[...], NT)
    for h in range(heads):
        col = slice(h * DV, (h + 1) * DV)
        value, gates, back = attn[:, col], gate[:, col], grad_normed[:, col]
        scale_o = rms_scale(value)
        unit_o = value * scale_o
        sig = jax.nn.sigmoid(gates)
        silu = gates * sig
        gate_grad_out[:, col] = (
            back * unit_o * out_gain[...] * sig * (1.0 + gates * (1.0 - sig))
        ).astype(BF16)
        scaled = back * silu
        out_gain_grad_out[...] += fold(scaled * unit_o)
        lifted_o = scaled * out_gain[...]
        grad_attn = scale_o * (
            lifted_o - unit_o * jnp.mean(lifted_o * unit_o, axis=-1, keepdims=True)
        )
        attn_grad_out[:, col] = grad_attn
        state_grad_out[h] += mm(far[:, col], grad_attn, TN, P_STATE)


def resid_backward(heads, who, share, x_all, branch, dh, grad, gain, w_out, normed, attn, gate, out_gain, far):
    rows, model = x_all.shape
    wide = heads * DV
    row = lambda width: block((ROWS, width), lambda i: (i, 0))
    half = halves_spec(rows, model)
    return pl.pallas_call(
        functools.partial(resid_kernel, heads),
        grid=(rows // ROWS,),
        in_specs=[
            SCALARS, row(model), half, half, half, half, row(model), fixed(gain.shape), once(w_out.shape),
            row(wide), row(wide), row(wide), fixed(out_gain.shape), row(wide),
        ],
        out_specs=[fixed(w_out.shape), row(wide), row(wide), row(share)]
        + [fixed((8, model)), fixed((8, DV)), fixed((heads, DK, DV))],
        out_shape=[
            shape(w_out.shape, BF16),
            shape((rows, wide)),
            shape((rows, wide), BF16),
            shape((rows, share)),
            shape((8, model)),
            shape((8, DV)),
            shape((heads, DK, DV)),
        ],
        scratch_shapes=[pltpu.VMEM((ROWS, model), F32), pltpu.VMEM(w_out.shape, F32)],
        compiler_params=params(22),
        cost_estimate=cost(9),
        name="resid_backward",
    )(who, x_all, *branch, *dh, grad, gain, w_out, normed, attn, gate, out_gain, far)


def mixer_back_kernel(
    heads, ends, steps, marks, place, maps, state_grads, start, raw, raw_before, rim, conv, logits, alpha,
    inv, transfers, states, reads, attn_grad, gate_grad,
    grad_raw_out, tail_out, rim_out, sums_out, conv_out,
    ext, mixed_grad, carry,
):
    step = pl.program_id(0)
    at_step = steps - 1 - step
    span_start = marks[0] + at_step * SPAN
    wide = heads * QKV
    per = SPAN // CHUNK

    @pl.when(step == 0)
    def _():
        carry[...] = jnp.zeros_like(carry)
        count = maps.shape[0]

        def join(k, unused):
            at = (count - 1 - k) ^ place[0]
            for h in range(heads):
                carry[h] = (
                    mm(maps[at, h, :, DV:].astype(F32), carry[h], TN, P_STATE)
                    + state_grads[at, h].astype(F32)
                )
            return unused

        lax.fori_loop(0, count - 1 - place[0], join, 0)
        mixed_grad[0:8] = jnp.zeros((8, wide), F32)
        mixed_grad[8 + SPAN :] = jnp.zeros((8, wide), F32)
        sums_out[...] = jnp.zeros_like(sums_out)
        conv_out[...] = jnp.zeros_like(conv_out)

    @pl.when(step > 0)
    def _():
        mixed_grad[8 + SPAN :] = mixed_grad[8:16]

    @pl.when(at_step == 0)
    def _():
        ext[0:8] = rim[...]

    @pl.when(at_step > 0)
    def _():
        ext[0:8] = raw_before[...]

    ext[8 : 8 + SPAN] = raw[...]
    masks = conv_masks(span_start, marks, ends, SPAN, -1)
    apart, strict = token_masks()
    logit = logits[...]
    betas = jax.nn.sigmoid(logit)
    gates, sums, rows = gate_tiles(logit, alpha[...])

    parts = {}
    for h in range(heads):
        mixed = [convolved(ext, conv, masks, h, part) for part in range(5)]
        active = [m * jax.nn.sigmoid(m) for m in mixed]
        unit, scale = zip(*[unit_rows(active[part]) for part in range(3)])
        beta = [spread_column(betas, 3 * h + i) for i in range(NH)]
        parts[h] = (mixed, unit, scale, active[3:], beta)

    units = [(h, c) for h in range(heads) for c in range(per)]
    befores, grads_after = {}, {}
    for h in range(heads):
        for c in reversed(range(per)):
            at, col = slice(c * CHUNK, (c + 1) * CHUNK), slice(h * DK, (h + 1) * DK)
            befores[h, c] = states[c, h, :, :DV] + mm(
                states[c, h, :, DV:], start[h], NN, P_STATE
            )
        for c in reversed(range(per)):
            at, col = slice(c * CHUNK, (c + 1) * CHUNK), slice(h * DK, (h + 1) * DK)
            grads_after[h, c] = carry[h]
            carry[h] = mm(reads[at, col], attn_grad[at, col], TN, P_STATE) + mm(
                transfers[c, h], carry[h], TN, P_STATE
            )

    work = {}
    for h, c in units:
        _, unit, _, values, beta = parts[h]
        keys = pair(unit[1], unit[2], c)
        value = pair(values[0], values[1], c)
        beta_c = pair(beta[0], beta[1], c)
        query = unit[0][c * CHUNK : (c + 1) * CHUNK]
        decay, opening, closing, chunk_whole = chunk_gates(
            span_start, marks, ends, sums, rows, h, c
        )
        decay_two = jnp.concatenate([decay, decay], axis=0)
        opening_two = jnp.concatenate([opening, opening], axis=0)
        closing_two = jnp.concatenate([closing, closing], axis=0)
        grown = jnp.where(strict, decay_two * mm(keys, keys, NT, P_BWD), 0.0)
        read = decay * mm(query, keys, NT, P_BWD)
        recalled = opening_two * mm(keys, befores[h, c], NN, P_SOLVE)
        missing = value - recalled
        deltas = mm(inv[c, h], beta_c * missing, NN, P_SOLVE)
        at, col = slice(c * CHUNK, (c + 1) * CHUNK), slice(h * DK, (h + 1) * DK)
        out_grad = attn_grad[at, col]
        grad_deltas = mm(read, out_grad, TN, P_SOLVE) + mm(
            closing_two * keys, grads_after[h, c], NN, P_SOLVE
        )
        work[h, c] = [
            keys, query, beta_c, decay, decay_two, opening, opening_two, closing_two,
            grown, missing, deltas, out_grad, grad_deltas, chunk_whole,
        ]
    columns = {}
    for h, c in units:
        (
            keys, query, beta, decay, decay_two, opening, opening_two, closing_two,
            grown, missing, deltas, out_grad, grad_deltas, chunk_whole,
        ) = work[h, c]
        grad_target = mm(inv[c, h], grad_deltas, TN, P_SOLVE)
        grad_lower = jnp.where(strict, -mm(grad_target, deltas, NT, P_PAIR), 0.0)
        grad_beta = jnp.sum(grad_lower * grown, axis=-1, keepdims=True) + jnp.sum(
            grad_target * missing, axis=-1, keepdims=True
        )
        grad_pairs = grad_lower * beta * decay_two
        grad_value = beta * grad_target
        grad_read = decay * mm(out_grad, deltas, NT, P_PAIR)
        left = mm(grad_pairs, keys, NN, P_BWD) - beta * opening_two * mm(
            grad_target, befores[h, c], NT, P_BWD
        )
        closed = closing_two * mm(deltas, grads_after[h, c], NT, P_BWD)
        right = mm(grad_pairs, keys, TN, P_BWD) + closed + mm(grad_read, query, TN, P_BWD)
        grad_query = mm(grad_read, keys, NN, P_BWD) + opening * mm(
            out_grad, befores[h, c], NT, P_BWD
        )
        in_left = jnp.sum(keys * left, axis=-1, keepdims=True)
        in_right = jnp.sum(keys * right, axis=-1, keepdims=True)
        in_query = jnp.sum(query * grad_query, axis=-1, keepdims=True)
        spare = in_left - in_right
        grad_total = spare[:CHUNK] + spare[CHUNK:] + in_query
        whole = jnp.sum(keys * closed) + jnp.sum(
            chunk_whole * jnp.sum(grads_after[h, c] * befores[h, c], axis=0, keepdims=True)
        )
        last_row = iota((CHUNK, 1), 0) == CHUNK - 1
        grad_total = grad_total + jnp.where(last_row, whole, 0.0)
        columns[h, c] = (
            grad_query - query * in_query,
            left + right - keys * (in_left + in_right),
            grad_value,
            grad_beta,
            grad_total,
        )

    lane = iota((SPAN, DK), 1)
    rates = jnp.zeros((SPAN, DK), F32)
    for h in range(heads):
        mixed, unit, scale, values, beta = parts[h]
        got = [columns[h, c] for c in range(per)]
        low, high = slice(0, CHUNK), slice(CHUNK, 2 * CHUNK)
        stack = lambda index, part: jnp.concatenate([g[index][part] for g in got], axis=0)
        act_grads = [
            scale[0] * stack(0, low),
            scale[1] * stack(1, low),
            scale[2] * stack(1, high),
            stack(2, low),
            stack(2, high),
        ]
        for i, column in enumerate((stack(3, low), stack(3, high), stack(4, low))):
            rates = rates + jnp.where(lane == 3 * h + i, column, 0.0)
        for part in range(5):
            cols = part_columns(h, part)
            sig = jax.nn.sigmoid(mixed[part])
            grad = act_grads[part] * sig * (1.0 + mixed[part] * (1.0 - sig))
            mixed_grad[8 : 8 + SPAN, cols] = grad
            conv_out[24:32, cols] += fold(grad * ext[8 : 8 + SPAN, cols])
            for s in range(1, CONV):
                moved = jnp.where(masks[s], ext[8 - s : 8 - s + SPAN, cols], 0.0)
                tap = CONV - 1 - s
                conv_out[8 * tap : 8 * tap + 8, cols] += fold(grad * moved)

    ahead = conv_masks(span_start, marks, ends, SPAN, 1)
    for h in range(heads):
        for part in range(5):
            cols = part_columns(h, part)
            grad = mixed_grad[8 : 8 + SPAN, cols] * conv[CONV - 1 : CONV, cols]
            for s in range(1, CONV):
                moved = jnp.where(ahead[s], mixed_grad[8 + s : 8 + s + SPAN, cols], 0.0)
                grad = grad + moved * conv[CONV - 1 - s : CONV - s, cols]
            begin = h * MIXW + part * DK
            grad_raw_out[:, begin : begin + DK] = grad.astype(BF16)

            @pl.when(step == 0)
            def _():
                tail_out[:, cols] = grad[SPAN - HALO :]

        grad_raw_out[:, h * MIXW + QKV : (h + 1) * MIXW] = gate_grad[:, h * DV : (h + 1) * DV]

    @pl.when(at_step == 0)
    def _():
        rim_masks = conv_masks(marks[0] - 8, marks, ends, 8, 1)
        for h in range(heads):
            for part in range(5):
                cols = part_columns(h, part)
                grad = jnp.zeros((8, DK), F32)
                for s in range(1, CONV):
                    moved = jnp.where(rim_masks[s], mixed_grad[s : s + 8, cols], 0.0)
                    grad = grad + moved * conv[CONV - 1 - s : CONV - s, cols]
                rim_out[:, cols] = grad

    back = mm(chunk_sum_matrix(True), rates, NN, 6)
    lanes = iota((1, DK), 1)
    is_gate = (lanes % (NH + 1) == NH) & (lanes < heads * (NH + 1))
    grad_logits = jnp.where(is_gate, back * alpha[...] * betas, rates * betas * (1.0 - betas))
    grad_raw_out[:, heads * MIXW :] = grad_logits.astype(BF16)
    sums_out[0:8] += fold(grad_logits)
    sums_out[8:16] += fold(back * gates)


def mixer_backward(
    heads, ends, marks, place, maps, state_grads, start, raw, rim, conv, logits, alpha,
    inv, transfers, states, reads, attn_grad, gate_grad,
):
    rows, wide = raw.shape
    steps, per = rows // SPAN, SPAN // CHUNK
    turn = lambda i: steps - 1 - i
    row = lambda width: block((SPAN, width), lambda i: (turn(i), 0))
    cube = lambda last: block((per, heads, SPAN, last), lambda i: (turn(i), 0, 0, 0))
    return pl.pallas_call(
        functools.partial(mixer_back_kernel, heads, ends, steps),
        grid=(steps,),
        in_specs=[
            SCALARS,
            SCALARS,
            once(maps.shape),
            once(state_grads.shape),
            fixed(start.shape),
            row(wide),
            block((8, wide), lambda i: (jnp.maximum(turn(i) * (SPAN // 8) - 1, 0), 0)),
            fixed(rim.shape),
            fixed(conv.shape),
            row(DK),
            fixed(alpha.shape),
            cube(SPAN),
            cube(DK),
            cube(DK + DV),
            row(heads * DK),
            row(heads * DV),
            row(heads * DV),
        ],
        out_specs=[
            row(heads * MIXW + DK),
            fixed((HALO, wide)),
            fixed((8, wide)),
            fixed((16, DK)),
            fixed((8 * CONV, wide)),
        ],
        out_shape=[
            shape((rows, heads * MIXW + DK), BF16),
            shape((HALO, wide)),
            shape((8, wide)),
            shape((16, DK)),
            shape((8 * CONV, wide)),
        ],
        scratch_shapes=[
            pltpu.VMEM((8 + SPAN, wide), F32),
            pltpu.VMEM((8 + SPAN + 8, wide), F32),
            pltpu.VMEM((heads, DK, DV), F32),
        ],
        compiler_params=params(60),
        cost_estimate=cost(50),
        name="mixer_backward",
    )(
        marks, place, maps, state_grads, start, raw, raw, rim, conv, logits, alpha,
        inv, transfers, states, reads, attn_grad, gate_grad,
    )


def weights_kernel(widths, orders, place, h_one, halo, grad, rim, out_weights, *outs):
    step, count = pl.program_id(0), pl.num_programs(0)
    total = mm(h_one[...], grad[...], TN) + mm(halo[...], rim[...], TN)
    total = jnp.concatenate([total, jnp.transpose(out_weights[...].astype(F32))], axis=1)
    at = 0
    for k, (width, order) in enumerate(zip(widths, orders)):
        value = total[:, at : at + width].astype(BF16)
        at += width
        position = weight_places(step, order)

        @pl.when(position < count // 2)
        def _():
            outs[2 * k][position] = value

        @pl.when(position >= count // 2)
        def _():
            outs[2 * k + 1][position - count // 2] = value


def weight_places(i, bits_in_order):
    position = 0
    for bit in bits_in_order:
        position = 2 * position + lax.rem(i // bit, 2)
    return position


def mixer_weights(place, ranges, h_one, halo, grad, rim, out_weights, widths, orders):
    rows, model = h_one.shape
    deep = model // ranges
    if deep % DK:
        whole = (t_dot(h_one, grad) + t_dot(halo, rim)).astype(BF16)
        whole = jnp.concatenate([whole, out_weights.T], axis=1).reshape(ranges, deep, -1)
        cuts, at = [], 0
        for width, order in zip(widths, orders):
            whole_cut = ordered(whole[:, :, at : at + width], order)
            cuts.append((whole_cut[: ranges // 2], whole_cut[ranges // 2 :]))
            at += width
        return cuts
    outs = pl.pallas_call(
        functools.partial(weights_kernel, widths, orders),
        grid_spec=pltpu.PrefetchScalarGridSpec(
            num_scalar_prefetch=1,
            grid=(ranges,),
            in_specs=[
                block((rows, deep), lambda i, place: (0, i ^ place[0])),
                block((HALO, deep), lambda i, place: (0, i ^ place[0])),
                block(grad.shape, lambda i, place: (0, 0)),
                block(rim.shape, lambda i, place: (0, 0)),
                block((out_weights.shape[0], deep), lambda i, place: (0, i ^ place[0])),
            ],
            out_specs=[
                block((ranges // 2, deep, width), lambda i, place: (0, 0, 0))
                for width in widths
                for _ in range(2)
            ],
        ),
        out_shape=[
            shape((ranges // 2, deep, width), BF16) for width in widths for _ in range(2)
        ],
        compiler_params=params(60),
        cost_estimate=cost(5),
        name="mixer_weights",
    )(place, h_one, halo, grad, rim, out_weights)
    return list(zip(outs[::2], outs[1::2]))


def input_kernel(heads, who, x, gain, grad, w_mixer, w_rates, gain_grad_out, kept, sent):
    step = pl.program_id(0)

    @pl.when(step == 0)
    def _():
        gain_grad_out[...] = jnp.zeros_like(gain_grad_out)
        rows = kept.shape[1] - HALO
        for out in (kept, sent):
            out[:, rows:] = jnp.zeros((out.shape[0], HALO, out.shape[2]), BF16)

    back = mm(grad[:, : heads * MIXW], w_mixer[...], NT) + mm(
        grad[:, heads * MIXW :], w_rates[...], NT
    )
    values = x[...].astype(F32)
    unit = values * rms_scale(values)
    seen = back * unit
    gain_grad_out[...] += fold(seen)
    keep_shares(step, back.astype(BF16), who[0], kept, sent)
    dots = jnp.sum(seen * gain[...], axis=-1, keepdims=True)
    dots = jnp.transpose(jnp.broadcast_to(dots, (ROWS, DK)))[:HALO]
    rows, share = kept.shape[1] - HALO, kept.shape[2]
    per = ROWS // share
    at = iota((HALO, share), 0)
    for k in range(per):
        line = jnp.where(at == step * per + k, dots[:, k * share : (k + 1) * share], 0.0)
        for out in (kept, sent):
            for j in range(out.shape[0]):
                out[j, rows:] = (out[j, rows:].astype(F32) + line).astype(BF16)


def input_backward(heads, count, who, x_all, gain, grad, w_mixer, w_rates):
    rows, model = x_all.shape
    share = model // count
    row = lambda width: block((ROWS, width), lambda i: (i, 0))
    return pl.pallas_call(
        functools.partial(input_kernel, heads),
        grid=(rows // ROWS,),
        in_specs=[
            SCALARS, row(model), fixed(gain.shape), row(grad.shape[1]), once(w_mixer.shape), once(w_rates.shape),
        ],
        out_specs=[fixed((8, model))] + [fixed((count // 2, rows + HALO, share))] * 2,
        out_shape=[shape((8, model))] + [shape((count // 2, rows + HALO, share), BF16)] * 2,
        compiler_params=params(60),
        cost_estimate=cost(6),
        name="input_backward",
    )(who, x_all, gain, grad, w_mixer, w_rates)


def tokens_kernel(model, who, x, gain, resid_grad, own_dots, came_dots, own, came, out):
    share = out.shape[1]
    cols = pl.ds(pl.multiple_of(who[0] * share, share), share)
    scale = rms_scale(x[...].astype(F32))
    unit = x[:, cols].astype(F32) * scale
    dots = own_dots[...].astype(F32) + came_dots[...].astype(F32)
    per = ROWS // share
    at = iota((HALO, share), 0)
    line = jnp.concatenate(
        [
            jnp.sum(jnp.where(at == pl.program_id(0) * per + k, dots, 0.0), axis=0, keepdims=True)
            for k in range(per)
        ],
        axis=1,
    )
    mean = jnp.transpose(jnp.broadcast_to(line, (8, ROWS)))[:, :1] / model
    back = (own[...].astype(F32) + came[...].astype(F32)) * gain[:, cols]
    out[...] = (resid_grad[...] + scale * (back - unit * mean)).astype(BF16)


def tokens_backward(who, x_all, gain, resid_grad, own, came):
    rows, model = x_all.shape
    share = own.shape[1]
    row = lambda width: block((ROWS, width), lambda i: (i, 0))
    extra = block((HALO, share), lambda i: (rows // HALO, 0))
    return pl.pallas_call(
        functools.partial(tokens_kernel, model),
        grid=(rows // ROWS,),
        in_specs=[
            SCALARS, row(model), fixed(gain.shape), row(share), extra, extra, row(share), row(share),
        ],
        out_specs=row(share),
        out_shape=shape((rows, share), BF16),
        compiler_params=params(10),
        cost_estimate=cost(2),
        name="tokens_backward",
    )(who, x_all, gain, resid_grad, own, came, own, came)


def shifted(value, axis, steps):
    count = lax.axis_size(axis)
    first, last = (max(0, -steps), min(count, count - steps))
    return lax.ppermute(value, axis, [(source, source + steps) for source in range(first, last)])


def swap(value, axis, mask):
    return lax.ppermute(value, axis, [(i, i ^ mask) for i in range(lax.axis_size(axis))])


def bits(axis):
    count, bit = lax.axis_size(axis), 1
    while bit < count:
        yield bit
        bit *= 2


def spread(value, axis, order):
    found = {0: value}
    for bit in order:
        found.update({m | bit: swap(v, axis, bit) for m, v in list(found.items())})
    return [found[m] for m in range(len(found))]


def spread_seq(value):
    found = {0: value}
    count = lax.axis_size("seq")
    for m in range(2, count, 2):
        found[m] = swap(value, "seq", m)
    for m in range(0, count, 2):
        found[m + 1] = swap(found[m], "seq", 1)
    return jnp.stack([found[m] for m in range(count)])


def tie(*values):
    return lax.optimization_barrier(values)


def summed_halves(mine, other, beside):
    total = mine + swap(other, "head", 1)
    for bit in bits("head"):
        if bit > 1:
            came, *beside = tie(swap(total, "head", bit), *beside)
            for value in beside:
                came = came + 0 * value.reshape(-1)[0]
            beside = ()
            total = total + came
    return total, swap(total, "head", 1)


def summed_shares(kept, sent):
    for bit in bits("head"):
        came = swap(sent, "head", bit)
        half = kept.shape[0] // 2
        if half:
            sent = kept[half:] + came[half:]
            kept = kept[:half] + came[:half]
    return kept[0], came[0]


def summed(value, axis):
    for bit in bits(axis):
        value = value + swap(value, axis, bit)
    return value


def spread_small(value):
    found = [value] + [swap(value, "seq", m) for m in range(2, lax.axis_size("seq"), 2)]
    here = jnp.stack(found)
    there = swap(here, "seq", 1)
    return jnp.stack([here, there], axis=1).reshape((-1,) + value.shape)


def ordered(value, order):
    place = lax.axis_index("seq")
    positions = [0]
    for bit in order[::-1]:
        positions = positions + [m | bit for m in positions]
    return jnp.take(value, jnp.array(positions) ^ place, axis=0)


def first_exchange(cuts, orders):
    came = []
    for (_, sent), order in zip(cuts, orders):
        if came and order[0] == orders[0][0]:
            came[-1], sent = tie(came[-1], sent)
        came.append(swap(sent, "seq", order[0]))
    return came


def scattered(cuts, came, orders):
    kept = [k for k, _ in cuts]
    for stage in range(len(orders[0])):
        if stage:
            came = [swap(value, "seq", order[stage]) for value, order in zip(sent, orders)]
        half = kept[0].shape[0] // 2
        sent = [k[half:] + c[half:] for k, c in zip(kept, came)]
        kept = [k[: max(half, 1)] + c[: max(half, 1)] for k, c in zip(kept, came)]
    return [k[0] for k in kept]


def t_dot(leading, trailing):
    return lax.dot_general(leading, trailing, TN, preferred_element_type=F32)


def local(
    tokens, lengths, norm1_gain, w_mixer, w_rates, decay_log, rates_bias, conv_weight,
    out_gain, w_out, norm2_gain, w_ffn_gate, w_ffn_up, w_ffn_down, out_grad,
):
    rows, share = tokens.shape
    heads = decay_log.shape[0]
    ends = lengths.shape[0]
    model = norm1_gain.shape[0]
    group, ranges = lax.axis_size("head"), lax.axis_size("seq")
    place, member = lax.axis_index("seq"), lax.axis_index("head")
    marks = jnp.concatenate(
        [jnp.reshape(place * rows, (1,)), jnp.cumsum(lengths)]
    ).astype(jnp.int32)
    place_arg = jnp.reshape(place, (1,)).astype(jnp.int32)
    who = jnp.reshape(member, (1,)).astype(jnp.int32)
    down_bits = list(bits("head"))[::-1]
    seq_bits = list(bits("seq"))

    halo = shifted(tokens[rows - HALO :], "seq", 1)
    token_parts = spread(jnp.concatenate([tokens, halo], axis=0), "head", down_bits)
    gain_one, gain_two = norm1_gain[None, :], norm2_gain[None, :]
    gain_out = out_gain[None, :]
    spare = DK - heads * (NH + 1)
    rates_w = jnp.pad(w_rates, ((0, 0), (0, spare)))
    bias = jnp.pad(rates_bias, (0, spare))[None, :]
    none = jnp.zeros((heads,), F32)
    alpha = jnp.stack([none] * NH + [-jnp.exp(decay_log)], axis=-1).reshape(-1)
    alpha = jnp.pad(alpha, (0, spare))[None, :]

    (
        x_all, h_one, h_halo, raw, rim, gate_o, logits, inv, transfers, states, reads, own, far, end_state,
    ) = mixer_forward(
        heads, ends, marks, who, token_parts, gain_one, w_mixer, rates_w, bias, alpha, conv_weight
    )
    out_grad, end_state = tie(out_grad, end_state)
    grad_parts = spread(out_grad, "head", down_bits)
    maps = spread_seq(end_state)
    attn, normed, start, *branch = branch_forward(
        heads, place_arg, who, maps, own, far, gate_o, gain_out, w_out, grad_parts
    )
    branch = summed_halves(*branch, [])
    h_two, act, grad_gate, grad_up, grad_full, dh_mine, dh_other, kept, sent = ffn_pass(
        who, x_all, *branch, grad_parts, gain_two, w_ffn_gate.T, w_ffn_up.T, w_ffn_down
    )
    by_owner = lambda value: jnp.swapaxes(
        value.reshape(value.shape[0], ranges, model // ranges), 0, 1
    ).astype(BF16)
    ffn_grads = [
        by_owner(t_dot(act, grad_full)), by_owner(t_dot(grad_gate, h_two)), by_owner(t_dot(grad_up, h_two)),
    ]
    ffn_grads = jnp.concatenate(ffn_grads, axis=1)
    dh = summed_halves(dh_mine, dh_other, [ffn_grads])
    hidden = act.shape[1]
    ffn_grads = lax.psum_scatter(ffn_grads, "seq", scatter_dimension=0, tiled=False)
    (
        out_weights, grad_attn, grad_gate_o, resid_own, gain_two_part, out_gain_part, state_grad,
    ) = resid_backward(
        heads, who, share, x_all, branch, dh, grad_full, gain_two, w_out, normed, attn, gate_o, gain_out, far
    )

    sent, state_grad = tie(sent, state_grad)
    state_grads = spread_small(state_grad.astype(BF16))
    first, second = summed_shares(kept, sent)
    own_cols = lambda value: lax.dynamic_slice_in_dim(value, member * share, share, 1)
    even = member % 2 == 0
    mine, other = own_cols(branch[0]), own_cols(branch[1])
    branch_own = [jnp.where(even, mine, other), jnp.where(even, other, mine)]
    output = (
        tokens.astype(F32)
        + jnp.concatenate(branch_own, axis=0).astype(F32)
        + (first.astype(F32) + second.astype(F32))
    ).astype(BF16)
    grad_raw, tail, rim_grad, sums, conv_parts = mixer_backward(
        heads, ends, marks, place_arg, maps, state_grads, start, raw, rim, conv_weight, logits, alpha,
        inv, transfers, states, reads, grad_attn, grad_gate_o,
    )
    rim_wide = jnp.pad(rim_grad, ((HALO - 8, 0), (0, 0))).astype(BF16)
    none = jnp.zeros((HALO, MIXW - QKV), BF16)
    rim_wide = jnp.concatenate(
        [b for h in range(heads) for b in (rim_wide[:, h * QKV : (h + 1) * QKV], none)]
        + [jnp.zeros((HALO, DK), BF16)],
        axis=1,
    )
    cut_widths = [MIXW] * (heads - 1) + [512, 256, DK + heads * DV]
    orders = [seq_bits] * (heads + 1) + [seq_bits[1:] + seq_bits[:1]]
    cuts = mixer_weights(
        place_arg, ranges, h_one, h_halo, grad_raw, rim_wide, out_weights, cut_widths, orders
    )
    cuts, ffn_grads = tie(cuts, ffn_grads)
    grad_down, grad_wgate, grad_wup = (
        ffn_grads[k * hidden : (k + 1) * hidden].astype(F32) for k in range(3)
    )
    came = first_exchange(cuts, orders)
    came[-1], grad_raw = tie(came[-1], grad_raw)
    tail = tail.at[HALO - 8 :].add(shifted(rim_grad, "seq", -1))
    for h in range(heads):
        grad_raw = lax.dynamic_update_slice(
            grad_raw, tail[:, h * QKV : (h + 1) * QKV].astype(BF16), (rows - HALO, h * MIXW)
        )
    gain_one_part, back_kept, back_sent = input_backward(
        heads, group, who, x_all, gain_one, grad_raw, w_mixer, rates_w
    )
    back_own, back_came = summed_shares(back_kept, back_sent)
    sum_rows = jnp.sum(sums.reshape(2, 8, DK), axis=1)
    small = jnp.concatenate(
        [
            jnp.sum(gain_one_part, axis=0),
            jnp.sum(out_gain_part, axis=0),
            jnp.sum(gain_two_part, axis=0),
            sum_rows[0],
            sum_rows[1],
            jnp.sum(conv_parts.reshape(CONV, 8, heads * QKV), axis=1).reshape(-1),
        ]
    )
    small = small.reshape(-1, DK)
    came[-2], small, back_own = tie(came[-2], small, back_own)
    cuts = scattered(cuts, came, orders)
    tokens_grad = tokens_backward(who, x_all, gain_one, resid_own, back_own, back_came)
    grad_wmixer = jnp.concatenate(cuts[:-1], axis=1).astype(F32)
    grad_wrates = cuts[-1][:, : heads * (NH + 1)].astype(F32)
    grad_wout = cuts[-1][:, DK:].T.astype(F32)

    small = summed(small, "seq").reshape(-1)
    cut = [model, DV, model, DK, DK]
    pieces_of, at = [], 0
    for size in cut:
        pieces_of.append(small[at : at + size])
        at += size
    over_head = summed(small[: model + DV], "head")
    grad_norm1, grad_outgain = over_head[:model], over_head[model:]
    _, _, grad_norm2, bias_row, decay_row = pieces_of
    grad_conv = small[at:].reshape(CONV, heads * QKV)
    grad_bias = bias_row[: heads * (NH + 1)]
    grad_decay = decay_row[: heads * (NH + 1)].reshape(heads, NH + 1)[:, NH]
    return (
        output, tokens_grad, grad_norm1, grad_wmixer, grad_wrates, grad_decay, grad_bias, grad_conv,
        grad_outgain, grad_wout, grad_norm2, grad_wgate.T, grad_wup.T, grad_down,
    )


def solution(mesh):
    placed = (
        P("seq", "head"), P(), P(), P(None, "head"), P(None, "head"), P("head"), P("head"), P(None, "head"),
        P(), P("head", None), P(), P(None, "head"), P(None, "head"), P("head", None), P("seq", "head"),
    )
    return jax.shard_map(
        local,
        mesh=mesh,
        in_specs=placed,
        out_specs=(
            P("seq", "head"), P("seq", "head"), P(), P("seq", "head"), P("seq", "head"), P("head"), P("head"),
            P(None, "head"), P(), P("head", "seq"), P(), P("seq", "head"), P("seq", "head"), P("head", "seq"),
        ),
        check_vma=False,
    )
```

```python
import functools

import jax
import jax.numpy as jnp
from jax import lax
from jax.experimental import pallas as pl
from jax.experimental.pallas import tpu as pltpu
from jax.sharding import PartitionSpec as P

DK = 128
DV = 128
NH = 2
CONV = 4
QKV = 640
MIXW = 768
EPS = 1e-06

CHUNK = 64
SPAN = 128
ROWS = 256
LEVELS = 6
HALO = 16

F32 = jnp.float32
BF16 = jnp.bfloat16

NN = (((1,), (0,)), ((), ()))
NT = (((1,), (1,)), ((), ()))
TN = (((0,), (0,)), ((), ()))

P_INV = 1
P_FWD = 3
P_STATE = 3
P_BWD = 1
P_SOLVE = 3
P_PAIR = 3


def halves(value):
    high = value.astype(BF16)
    return high, (value - high.astype(F32)).astype(BF16)


def mm(left, right, dims=NN, passes=1):
    if passes == 1:
        return lax.dot_general(
            left.astype(BF16), right.astype(BF16), dims, preferred_element_type=F32
        )
    if passes == 6:
        return lax.dot_general(
            left, right, dims, precision=lax.Precision.HIGHEST, preferred_element_type=F32
        )
    left_h, left_l = halves(left)
    right_h, right_l = halves(right)
    dot = functools.partial(lax.dot_general, dimension_numbers=dims, preferred_element_type=F32)
    return dot(left_h, right_h) + (dot(left_h, right_l) + dot(left_l, right_h))


def iota(shape, axis):
    return lax.broadcasted_iota(jnp.int32, shape, axis)


def doc_of(place, marks, ends):
    count = jnp.zeros_like(place)
    for j in range(ends):
        count = count + jnp.where(place >= marks[1 + j], 1, 0)
    return jnp.where(place < 0, -1, count)


def doc_scalar(place, marks, ends):
    count = jnp.int32(0)
    for j in range(ends):
        count = count + (place >= marks[1 + j]).astype(jnp.int32)
    return jnp.where(place < 0, -1, count)


def conv_masks(start, marks, ends, rows, direction):
    place = start + iota((rows, DK), 0)
    here = doc_of(place, marks, ends)
    return [None] + [
        doc_of(place + direction * s, marks, ends) == here for s in range(1, CONV)
    ]


def softplus(v):
    return jnp.maximum(v, 0.0) + jnp.log1p(jnp.exp(-jnp.abs(v)))


def chunk_sum_matrix(upper):
    row, col = iota((SPAN, SPAN), 0), iota((SPAN, SPAN), 1)
    keep = (col >= row) if upper else (col <= row)
    keep = keep & ((row // CHUNK) == (col // CHUNK))
    return jnp.where(keep, 1.0, 0.0).astype(F32)


def part_columns(h, part):
    begin = h * QKV + part * DK
    return slice(begin, begin + DK)


def convolved(ext, conv, masks, h, part):
    cols = part_columns(h, part)
    total = ext[8 : 8 + SPAN, cols] * conv[CONV - 1 : CONV, cols]
    for s in range(1, CONV):
        moved = jnp.where(masks[s], ext[8 - s : 8 - s + SPAN, cols], 0.0)
        total = total + moved * conv[CONV - 1 - s : CONV - s, cols]
    return total


def two(array, c):
    piece = array[c * CHUNK : (c + 1) * CHUNK]
    return jnp.concatenate([piece, piece], axis=0)


def pair(first, second, c):
    at = slice(c * CHUNK, (c + 1) * CHUNK)
    return jnp.concatenate([first[at], second[at]], axis=0)


def unit_rows(v):
    scale = lax.rsqrt(jnp.sum(v * v, axis=-1, keepdims=True) + EPS)
    return v * scale, scale


def token_masks():
    row, col = iota((SPAN, SPAN), 0), iota((SPAN, SPAN), 1)
    tok_r, tok_c = row % CHUNK, col % CHUNK
    strict = (tok_c < tok_r) | ((tok_c == tok_r) & (row >= CHUNK) & (col < CHUNK))
    return tok_r ^ tok_c, strict


def gate_tiles(logits, alpha):
    gates = alpha * softplus(logits)
    sums = mm(chunk_sum_matrix(False), gates, NN, 6)
    flat = jnp.transpose(sums)[:8]
    turned = pltpu.roll(flat, CHUNK, 1)
    lane = iota(flat.shape, 1)
    first = jnp.where(lane < CHUNK, flat, turned)
    second = jnp.where(lane < CHUNK, turned, flat)
    return gates, sums, (first, second)


def spread_column(tile, col):
    return jnp.broadcast_to(tile[:, col : col + 1], (SPAN, DK))


def chunk_gates(span_start, marks, ends, sums, rows, h, c):
    start = span_start + c * CHUNK
    col_place = start + iota((CHUNK, SPAN), 0)
    row_place = start + iota((CHUNK, SPAN), 1) % CHUNK
    col_doc = doc_of(col_place, marks, ends)
    row_doc = doc_of(row_place, marks, ends)
    total = spread_column(sums, 3 * h + 2)[c * CHUNK : (c + 1) * CHUNK]
    across = rows[c][3 * h + 2 : 3 * h + 3]
    kept = (col_doc == row_doc) & (row_place <= col_place)
    decay = jnp.exp(jnp.where(kept, total - across, -1e30))
    doc_before = doc_scalar(start - 1, marks, ends)
    doc_last = doc_scalar(start + CHUNK - 1, marks, ends)
    last = total[CHUNK - 1 : CHUNK]
    opening = jnp.where(col_doc == doc_before, jnp.exp(total), 0.0)
    closing = jnp.where(col_doc == doc_last, jnp.exp(last - total), 0.0)
    whole = jnp.where(doc_before == doc_last, jnp.exp(last), 0.0)
    return decay, opening, closing, whole


def inverses(lowers, apart):
    eye = jnp.where(iota((SPAN, SPAN), 0) == iota((SPAN, SPAN), 1), 1.0, 0.0)
    result = [eye - jnp.where(apart == 0, lower, 0.0) for lower in lowers]
    for level in range(LEVELS):
        here = (apart >> level) == 1
        steps = [
            mm(inverse, jnp.where(here, lower, 0.0), NN, P_INV)
            for inverse, lower in zip(result, lowers)
        ]
        result = [
            inverse - mm(step, inverse, NN, P_INV) for inverse, step in zip(result, steps)
        ]
    return result


def rms_scale(values):
    return lax.rsqrt(jnp.mean(values * values, axis=-1, keepdims=True) + EPS)


def in_order(parts, me):
    bit = 1
    while bit < len(parts):
        flip = (me // bit) % 2 == 1
        parts = [jnp.where(flip, parts[m ^ bit], parts[m]) for m in range(len(parts))]
        bit *= 2
    return parts


def mixer_kernel(heads, ends, count, marks, who, *refs):
    tokens, halos, refs = refs[:count], refs[count : 2 * count], refs[2 * count :]
    (
        gain, w_mixer, w_rates, bias, alpha, conv,
        x_out, h_out, halo_out, raw_out, rim_out, gate_out, logit_out, inv_out, map_out, state_out,
        read_out, own_out, far_out, end_out, ext, state,
    ) = refs
    step = pl.program_id(0)
    joined = lambda parts: jnp.concatenate(in_order([p[...] for p in parts], who[0]), axis=1)
    span_start = marks[0] + step * SPAN

    def rounded_norm(rows):
        values = rows.astype(F32)
        return (values * rms_scale(values) * gain[...]).astype(BF16)

    @pl.when(step == 0)
    def _():
        halo_out[...] = rounded_norm(joined(halos))
        halo = jnp.dot(halo_out[...], w_mixer[...], preferred_element_type=F32)
        for h in range(heads):
            ext[0:8, h * QKV : (h + 1) * QKV] = halo[HALO - 8 :, h * MIXW : h * MIXW + QKV]
        rim_out[...] = ext[0:8]
        for h in range(heads):
            state[h, :, :DV] = jnp.zeros((DK, DV), F32)
            state[h, :, DV:] = jnp.where(
                iota((DK, DK), 0) == iota((DK, DK), 1), 1.0, 0.0
            ).astype(F32)

    @pl.when(step > 0)
    def _():
        ext[0:8] = ext[SPAN : SPAN + 8]

    x = joined(tokens)
    x_out[...] = x
    h_one = rounded_norm(x)
    h_out[...] = h_one
    raw = jnp.dot(h_one, w_mixer[...], preferred_element_type=F32)
    for h in range(heads):
        ext[8 : 8 + SPAN, h * QKV : (h + 1) * QKV] = raw[:, h * MIXW : h * MIXW + QKV]
        gate_out[:, h * DV : (h + 1) * DV] = raw[:, h * MIXW + QKV : (h + 1) * MIXW]
    raw_out[...] = ext[8 : 8 + SPAN]
    logits = jnp.dot(h_one, w_rates[...], preferred_element_type=F32) + bias[...]
    logit_out[...] = logits
    masks = conv_masks(span_start, marks, ends, SPAN, -1)
    apart, strict = token_masks()
    betas = jax.nn.sigmoid(logits)
    _, sums, rows = gate_tiles(logits, alpha[...])

    units = [(h, c) for h in range(heads) for c in range(SPAN // CHUNK)]
    parts = {}
    for h in range(heads):
        active = []
        for part in range(5):
            mixed = convolved(ext, conv, masks, h, part)
            active.append(mixed * jax.nn.sigmoid(mixed))
        unit = [unit_rows(active[part])[0] for part in range(3)]
        beta = [spread_column(betas, 3 * h + i) for i in range(NH)]
        parts[h] = (unit, active[3:], beta)

    lowers, reads, sides, lasts, wholes, queries = [], [], [], [], [], []
    for h, c in units:
        (query, key_a, key_b), (value_a, value_b), (beta_a, beta_b) = parts[h]
        keys, values, beta = (
            pair(key_a, key_b, c),
            pair(value_a, value_b, c),
            pair(beta_a, beta_b, c),
        )
        query_c = query[c * CHUNK : (c + 1) * CHUNK]
        decay, opening, closing, whole = chunk_gates(
            span_start, marks, ends, sums, rows, h, c
        )
        decay_two = jnp.concatenate([decay, decay], axis=0)
        opening_two = jnp.concatenate([opening, opening], axis=0)
        closing_two = jnp.concatenate([closing, closing], axis=0)
        lowers.append(
            jnp.where(strict, beta * decay_two * mm(keys, keys, NT, P_FWD), 0.0)
        )
        reads.append(decay * mm(query_c, keys, NT, P_FWD))
        sides.append(
            jnp.concatenate([beta * values, beta * opening_two * keys], axis=1)
        )
        lasts.append(closing_two * keys)
        wholes.append(whole)
        queries.append(opening * query_c)
    solved = inverses(lowers, apart)
    pieces = [mm(inverse, side, NN, P_FWD) for inverse, side in zip(solved, sides)]
    maps = [mm(last, piece, TN, P_FWD) for last, piece in zip(lasts, pieces)]
    seen = [mm(read, piece, NN, P_FWD) for read, piece in zip(reads, pieces)]
    diagonal = iota((DK, DK), 0) == iota((DK, DK), 1)
    for index, (h, c) in enumerate(units):
        inv_out[c, h] = solved[index]
        transfer = jnp.where(diagonal, wholes[index], 0.0) - maps[index][:, DV:]
        map_out[c, h] = transfer
        reader = queries[index] - seen[index][:, DV:]
        at, col = slice(c * CHUNK, (c + 1) * CHUNK), slice(h * DK, (h + 1) * DK)
        read_out[at, col] = reader
        before = state[h]
        state_out[c, h] = before
        both = mm(reader, before, NN, P_STATE)
        own_out[at, col] = seen[index][:, :DV] + both[:, :DV]
        far_out[at, col] = both[:, DV:]
        after = mm(transfer, before, NN, P_STATE)
        state[h, :, :DV] = after[:, :DV] + maps[index][:, :DV]
        state[h, :, DV:] = after[:, DV:]
    end_out[...] = state[...].astype(BF16)


def block(shape, index):
    return pl.BlockSpec(shape, index)


def fixed(shape):
    return pl.BlockSpec(shape, lambda i: (0,) * len(shape))


def once(shape):
    return pl.BlockSpec(
        shape, lambda i: (0,) * len(shape), pipeline_mode=pl.Buffered(buffer_count=1)
    )


SCALARS = pl.BlockSpec(memory_space=pltpu.SMEM)


def shape(dims, kind=F32):
    return jax.ShapeDtypeStruct(dims, kind)


def params(megabytes):
    return pltpu.CompilerParams(
        dimension_semantics=("arbitrary",), vmem_limit_bytes=megabytes << 20
    )


def cost(microseconds):
    return pl.CostEstimate(
        flops=int(microseconds * 1.1e8), bytes_accessed=int(microseconds * 1e5), transcendentals=0
    )


WHOLE = pl.BlockSpec(memory_space=pl.ANY)


def mixer_forward(heads, ends, marks, who, tokens, gain, w_mixer, w_rates, bias, alpha, conv):
    rows, share = tokens[0].shape
    rows = rows - HALO
    model = gain.shape[1]
    steps, chunks, per = rows // SPAN, rows // CHUNK, SPAN // CHUNK
    wide = heads * QKV
    row = lambda width: block((SPAN, width), lambda i: (i, 0))
    cube = lambda last: block((per, heads, SPAN, last), lambda i: (i, 0, 0, 0))
    return pl.pallas_call(
        functools.partial(mixer_kernel, heads, ends, len(tokens)),
        grid=(steps,),
        in_specs=[SCALARS, SCALARS]
        + [row(share)] * len(tokens)
        + [block((HALO, share), lambda i: (rows // HALO, 0))] * len(tokens)
        + [
            fixed((1, model)),
            once(w_mixer.shape),
            once(w_rates.shape),
            fixed(bias.shape),
            fixed(alpha.shape),
            fixed(conv.shape),
        ],
        out_specs=[
            row(model),
            row(model),
            fixed((HALO, model)),
            row(wide),
            fixed((8, wide)),
            row(heads * DV),
            row(DK),
            cube(SPAN),
            cube(DK),
            cube(DK + DV),
            row(heads * DK),
            row(heads * DV),
            row(heads * DK),
            fixed((heads, DK, DK + DV)),
        ],
        out_shape=[
            shape((rows, model), BF16),
            shape((rows, model), BF16),
            shape((HALO, model), BF16),
            shape((rows, wide)),
            shape((8, wide)),
            shape((rows, heads * DV)),
            shape((rows, DK)),
            shape((chunks, heads, SPAN, SPAN)),
            shape((chunks, heads, DK, DK)),
            shape((chunks, heads, DK, DK + DV)),
            shape((rows, heads * DK)),
            shape((rows, heads * DV)),
            shape((rows, heads * DK)),
            shape((heads, DK, DK + DV), BF16),
        ],
        scratch_shapes=[
            pltpu.VMEM((8 + SPAN, wide), F32),
            pltpu.VMEM((heads, DK, DK + DV), F32),
        ],
        compiler_params=params(60),
        cost_estimate=cost(36),
        name="mixer_forward",
    )(marks, who, *tokens, *tokens, gain, w_mixer, w_rates, bias, alpha, conv)


def branch_kernel(heads, pieces, place, who, maps, own, far, gate, gain, w_out, *refs):
    attn_out, normed_out, start_out, *refs, start = refs[-4 - 2 * pieces :]
    mine, other = refs[:pieces], refs[pieces:]
    step = pl.program_id(0)

    @pl.when(step == 0)
    def _():
        start[...] = jnp.zeros_like(start)

        def join(j, carry):
            at = j ^ place[0]
            for h in range(heads):
                start[h] = (
                    mm(maps[at, h, :, DV:].astype(F32), start[h], NN, P_STATE)
                    + maps[at, h, :, :DV].astype(F32)
                )
            return carry

        lax.fori_loop(0, place[0], join, 0)
        start_out[...] = start[...]

    for h in range(heads):
        col = slice(h * DV, (h + 1) * DV)
        attn = own[:, col] + mm(far[:, col], start[h], NN, P_STATE)
        attn_out[:, col] = attn
        gates = gate[:, col]
        normed = attn * rms_scale(attn) * gain[...] * (gates * jax.nn.sigmoid(gates))
        normed_out[:, col] = normed.astype(BF16)
    branch = jnp.dot(normed_out[...], w_out[...], preferred_element_type=F32).astype(BF16)
    keep_half(step, who[0], branch, mine, other)


def keep_half(step, me, value, mine, other):
    for p in range(len(mine)):
        for half in range(2):

            @pl.when(step == 2 * p + half)
            def _():
                @pl.when(lax.rem(me, 2) == half)
                def _():
                    mine[p][...] = value

                @pl.when(lax.rem(me, 2) != half)
                def _():
                    other[p][...] = value


def pick_half(step, me, mine, other, out):
    for p in range(len(mine)):
        for half in range(2):

            @pl.when(step == 2 * p + half)
            def _():
                @pl.when(lax.rem(me, 2) == half)
                def _():
                    out[...] = mine[p][...].astype(F32)

                @pl.when(lax.rem(me, 2) != half)
                def _():
                    out[...] = other[p][...].astype(F32)


def branch_forward(heads, place, who, maps, own, far, gate, gain, w_out, waits):
    rows, model = own.shape[0], w_out.shape[1]
    wide = heads * DV
    pieces = rows // (2 * ROWS)
    row = lambda width: block((ROWS, width), lambda i: (i, 0))
    return pl.pallas_call(
        functools.partial(branch_kernel, heads, pieces),
        grid=(rows // ROWS,),
        in_specs=[
            SCALARS, SCALARS, once(maps.shape), row(wide), row(wide), row(wide), fixed(gain.shape), once(w_out.shape),
        ]
        + [WHOLE] * len(waits),
        out_specs=[row(wide), row(wide), fixed((heads, DK, DV))]
        + [fixed((ROWS, model))] * (2 * pieces),
        out_shape=[shape((rows, wide)), shape((rows, wide), BF16), shape((heads, DK, DV))]
        + [shape((ROWS, model), BF16)] * (2 * pieces),
        scratch_shapes=[pltpu.VMEM((heads, DK, DV), F32)],
        compiler_params=params(14),
        cost_estimate=cost(3),
        name="branch_forward",
    )(place, who, maps, own, far, gate, gain, w_out, *waits)


def share_places(count):
    order, bit = [0], count // 2
    for bit in [1 << k for k in range(count.bit_length() - 1)][::-1]:
        order = order + [m | bit for m in order]
    return order


def keep_shares(step, value, me, kept, sent):
    count = 2 * kept.shape[0]
    width = value.shape[1] // count
    parts = in_order([value[:, m * width : (m + 1) * width] for m in range(count)], me)
    rows = pl.ds(pl.multiple_of(step * ROWS, ROWS), ROWS)
    for position, m in enumerate(share_places(count)):
        if position < count // 2:
            kept[position, rows] = parts[m]
        else:
            sent[position - count // 2, rows] = parts[m]


def ffn_kernel(count, filled, who, x, mine, other, *refs):
    grads, refs = refs[:count], refs[count:]
    gain, w_gate, w_up, w_down = refs[:4]
    (
        h_out, act_out, gg_out, gu_out, grad_out, kept, sent, dh_mine, dh_other, picked,
    ) = refs[4 + filled :]
    step = pl.program_id(0)
    pick_half(step, who[0], [mine], [other], picked)
    resid = x[...].astype(F32) + picked[...]
    h_two = (resid * rms_scale(resid) * gain[...]).astype(BF16)
    h_out[...] = h_two
    grad = jnp.concatenate(in_order([g[...] for g in grads], who[0]), axis=1)
    grad_out[...] = grad
    gate = mm(h_two, w_gate[...], NT)
    up = mm(h_two, w_up[...], NT)
    sig = jax.nn.sigmoid(gate)
    silu = gate * sig
    act = (silu * up).astype(BF16)
    act_out[...] = act
    grad_act = mm(grad, w_down[...], NT)
    grad_gate = (grad_act * up * sig * (1.0 + gate * (1.0 - sig))).astype(BF16)
    grad_up = (grad_act * silu).astype(BF16)
    gg_out[...] = grad_gate
    gu_out[...] = grad_up
    dh = (mm(grad_gate, w_gate[...]) + mm(grad_up, w_up[...])).astype(BF16)
    keep_half(step, who[0], dh, [dh_mine], [dh_other])
    keep_shares(step, mm(act, w_down[...]).astype(BF16), who[0], kept, sent)


def ffn_pass(piece, who, x_all, mine, other, grads, gain, w_gate, w_up, w_down, filled):
    rows, model = x_all.shape
    share, count = grads[0].shape[1], len(grads)
    hidden = w_gate.shape[0]
    row = lambda width: block((ROWS, width), lambda i: (2 * piece + i, 0))
    half = fixed((ROWS, model))
    shares = block((count // 2, 2 * ROWS, share), lambda i: (0, piece, 0))
    first = 8 + count
    return pl.pallas_call(
        functools.partial(ffn_kernel, count, len(filled)),
        grid=(2,),
        in_specs=[SCALARS, row(model), half, half]
        + [row(share)] * count
        + [fixed(gain.shape), once(w_gate.shape), once(w_up.shape), once(w_down.shape)]
        + [WHOLE] * len(filled),
        out_specs=[row(model), row(hidden), row(hidden), row(hidden), row(model)]
        + [shares] * 2
        + [half] * 2,
        out_shape=[
            shape((rows, model), BF16),
            shape((rows, hidden), BF16),
            shape((rows, hidden), BF16),
            shape((rows, hidden), BF16),
            shape((rows, model), BF16),
        ]
        + [shape((count // 2, rows, share), BF16)] * 2
        + [shape((ROWS, model), BF16)] * 2,
        scratch_shapes=[pltpu.VMEM((ROWS, model), F32)],
        input_output_aliases={first + k: k for k in range(len(filled))},
        compiler_params=params(32),
        cost_estimate=cost(10),
        name="ffn_pass",
    )(who, x_all, mine, other, *grads, gain, w_gate, w_up, w_down, *filled)


def fold(value):
    return jnp.sum(value.reshape(value.shape[0] // 8, 8, value.shape[1]), axis=0)


def resid_kernel(
    heads, pieces, who, x, *refs
):
    take = lambda k: refs[k * pieces : (k + 1) * pieces]
    branch_mine, branch_other, dh_mine, dh_other = take(0), take(1), take(2), take(3)
    (
        grad, gain, w_out, normed, attn, gate, out_gain, far,
        weight_out, attn_grad_out, gate_grad_out, resid_out,
        gain_grad_out, out_gain_grad_out, state_grad_out, resid_all, weight_sum, dh,
    ) = refs[4 * pieces :]
    step = pl.program_id(0)
    pick_half(step, who[0], branch_mine, branch_other, resid_all)
    pick_half(step, who[0], dh_mine, dh_other, dh)

    @pl.when(pl.program_id(0) == 0)
    def _():
        for total in (gain_grad_out, out_gain_grad_out, state_grad_out, weight_sum):
            total[...] = jnp.zeros_like(total)

    resid = x[...].astype(F32) + resid_all[...]
    scale = rms_scale(resid)
    unit = resid * scale
    grad_h = dh[...]
    gain_grad_out[...] += fold(grad_h * unit)
    lifted = grad_h * gain[...]
    grad_resid = grad[...].astype(F32) + scale * (
        lifted - unit * jnp.mean(lifted * unit, axis=-1, keepdims=True)
    )
    resid_all[...] = grad_resid
    share = resid_out.shape[1]
    resid_out[...] = resid_all[:, pl.ds(pl.multiple_of(who[0] * share, share), share)]
    grad_branch = grad_resid.astype(BF16)
    weight_sum[...] += mm(normed[...], grad_branch, TN)

    @pl.when(pl.program_id(0) == pl.num_programs(0) - 1)
    def _():
        weight_out[...] = weight_sum[...].astype(BF16)

    grad_normed = mm(grad_branch, w_out[...], NT)
    for h in range(heads):
        col = slice(h * DV, (h + 1) * DV)
        value, gates, back = attn[:, col], gate[:, col], grad_normed[:, col]
        scale_o = rms_scale(value)
        unit_o = value * scale_o
        sig = jax.nn.sigmoid(gates)
        silu = gates * sig
        gate_grad_out[:, col] = (
            back * unit_o * out_gain[...] * sig * (1.0 + gates * (1.0 - sig))
        ).astype(BF16)
        scaled = back * silu
        out_gain_grad_out[...] += fold(scaled * unit_o)
        lifted_o = scaled * out_gain[...]
        grad_attn = scale_o * (
            lifted_o - unit_o * jnp.mean(lifted_o * unit_o, axis=-1, keepdims=True)
        )
        attn_grad_out[:, col] = grad_attn
        state_grad_out[h] += mm(far[:, col], grad_attn, TN, P_STATE)


def resid_backward(heads, who, share, x_all, branch, dh, grad, gain, w_out, normed, attn, gate, out_gain, far):
    rows, model = x_all.shape
    wide = heads * DV
    row = lambda width: block((ROWS, width), lambda i: (i, 0))
    pieces = rows // (2 * ROWS)
    halves = [fixed((ROWS, model))] * (4 * pieces)
    return pl.pallas_call(
        functools.partial(resid_kernel, heads, pieces),
        grid=(rows // ROWS,),
        in_specs=[
            SCALARS, row(model), *halves, row(model), fixed(gain.shape), once(w_out.shape),
            row(wide), row(wide), row(wide), fixed(out_gain.shape), row(wide),
        ],
        out_specs=[fixed(w_out.shape), row(wide), row(wide), row(share)]
        + [fixed((8, model)), fixed((8, DV)), fixed((heads, DK, DV))],
        out_shape=[
            shape(w_out.shape, BF16),
            shape((rows, wide)),
            shape((rows, wide), BF16),
            shape((rows, share)),
            shape((8, model)),
            shape((8, DV)),
            shape((heads, DK, DV)),
        ],
        scratch_shapes=[
            pltpu.VMEM((ROWS, model), F32),
            pltpu.VMEM(w_out.shape, F32),
            pltpu.VMEM((ROWS, model), F32),
        ],
        compiler_params=params(60),
        cost_estimate=cost(9),
        name="resid_backward",
    )(
        who, x_all, *[b[0] for b in branch], *[b[1] for b in branch], *[d[0] for d in dh], *[d[1] for d in dh],
        grad, gain, w_out, normed, attn, gate, out_gain, far,
    )


def mixer_back_kernel(
    heads, ends, steps, marks, place, maps, state_grads, start, raw, raw_before, rim, conv, logits, alpha,
    inv, transfers, states, reads, attn_grad, gate_grad,
    grad_raw_out, tail_out, rim_out, sums_out, conv_out,
    ext, mixed_grad, carry,
):
    step = pl.program_id(0)
    at_step = steps - 1 - step
    span_start = marks[0] + at_step * SPAN
    wide = heads * QKV
    per = SPAN // CHUNK

    @pl.when(step == 0)
    def _():
        carry[...] = jnp.zeros_like(carry)
        count = maps.shape[0]

        def join(k, unused):
            at = (count - 1 - k) ^ place[0]
            for h in range(heads):
                carry[h] = (
                    mm(maps[at, h, :, DV:].astype(F32), carry[h], TN, P_STATE)
                    + state_grads[at, h].astype(F32)
                )
            return unused

        lax.fori_loop(0, count - 1 - place[0], join, 0)
        mixed_grad[0:8] = jnp.zeros((8, wide), F32)
        mixed_grad[8 + SPAN :] = jnp.zeros((8, wide), F32)
        sums_out[...] = jnp.zeros_like(sums_out)
        conv_out[...] = jnp.zeros_like(conv_out)

    @pl.when(step > 0)
    def _():
        mixed_grad[8 + SPAN :] = mixed_grad[8:16]

    @pl.when(at_step == 0)
    def _():
        ext[0:8] = rim[...]

    @pl.when(at_step > 0)
    def _():
        ext[0:8] = raw_before[...]

    ext[8 : 8 + SPAN] = raw[...]
    masks = conv_masks(span_start, marks, ends, SPAN, -1)
    apart, strict = token_masks()
    logit = logits[...]
    betas = jax.nn.sigmoid(logit)
    gates, sums, rows = gate_tiles(logit, alpha[...])

    parts = {}
    for h in range(heads):
        mixed = [convolved(ext, conv, masks, h, part) for part in range(5)]
        active = [m * jax.nn.sigmoid(m) for m in mixed]
        unit, scale = zip(*[unit_rows(active[part]) for part in range(3)])
        beta = [spread_column(betas, 3 * h + i) for i in range(NH)]
        parts[h] = (mixed, unit, scale, active[3:], beta)

    units = [(h, c) for h in range(heads) for c in range(per)]
    befores, grads_after = {}, {}
    for h in range(heads):
        for c in reversed(range(per)):
            at, col = slice(c * CHUNK, (c + 1) * CHUNK), slice(h * DK, (h + 1) * DK)
            befores[h, c] = states[c, h, :, :DV] + mm(
                states[c, h, :, DV:], start[h], NN, P_STATE
            )
        for c in reversed(range(per)):
            at, col = slice(c * CHUNK, (c + 1) * CHUNK), slice(h * DK, (h + 1) * DK)
            grads_after[h, c] = carry[h]
            carry[h] = mm(reads[at, col], attn_grad[at, col], TN, P_STATE) + mm(
                transfers[c, h], carry[h], TN, P_STATE
            )

    work = {}
    for h, c in units:
        _, unit, _, values, beta = parts[h]
        keys = pair(unit[1], unit[2], c)
        value = pair(values[0], values[1], c)
        beta_c = pair(beta[0], beta[1], c)
        query = unit[0][c * CHUNK : (c + 1) * CHUNK]
        decay, opening, closing, chunk_whole = chunk_gates(
            span_start, marks, ends, sums, rows, h, c
        )
        decay_two = jnp.concatenate([decay, decay], axis=0)
        opening_two = jnp.concatenate([opening, opening], axis=0)
        closing_two = jnp.concatenate([closing, closing], axis=0)
        grown = jnp.where(strict, decay_two * mm(keys, keys, NT, P_BWD), 0.0)
        read = decay * mm(query, keys, NT, P_BWD)
        recalled = opening_two * mm(keys, befores[h, c], NN, P_SOLVE)
        missing = value - recalled
        deltas = mm(inv[c, h], beta_c * missing, NN, P_SOLVE)
        at, col = slice(c * CHUNK, (c + 1) * CHUNK), slice(h * DK, (h + 1) * DK)
        out_grad = attn_grad[at, col]
        grad_deltas = mm(read, out_grad, TN, P_SOLVE) + mm(
            closing_two * keys, grads_after[h, c], NN, P_SOLVE
        )
        work[h, c] = [
            keys, query, beta_c, decay, decay_two, opening, opening_two, closing_two,
            grown, missing, deltas, out_grad, grad_deltas, chunk_whole,
        ]
    columns = {}
    for h, c in units:
        (
            keys, query, beta, decay, decay_two, opening, opening_two, closing_two,
            grown, missing, deltas, out_grad, grad_deltas, chunk_whole,
        ) = work[h, c]
        grad_target = mm(inv[c, h], grad_deltas, TN, P_SOLVE)
        grad_lower = jnp.where(strict, -mm(grad_target, deltas, NT, P_PAIR), 0.0)
        grad_beta = jnp.sum(grad_lower * grown, axis=-1, keepdims=True) + jnp.sum(
            grad_target * missing, axis=-1, keepdims=True
        )
        grad_pairs = grad_lower * beta * decay_two
        grad_value = beta * grad_target
        grad_read = decay * mm(out_grad, deltas, NT, P_PAIR)
        left = mm(grad_pairs, keys, NN, P_BWD) - beta * opening_two * mm(
            grad_target, befores[h, c], NT, P_BWD
        )
        closed = closing_two * mm(deltas, grads_after[h, c], NT, P_BWD)
        right = mm(grad_pairs, keys, TN, P_BWD) + closed + mm(grad_read, query, TN, P_BWD)
        grad_query = mm(grad_read, keys, NN, P_BWD) + opening * mm(
            out_grad, befores[h, c], NT, P_BWD
        )
        in_left = jnp.sum(keys * left, axis=-1, keepdims=True)
        in_right = jnp.sum(keys * right, axis=-1, keepdims=True)
        in_query = jnp.sum(query * grad_query, axis=-1, keepdims=True)
        spare = in_left - in_right
        grad_total = spare[:CHUNK] + spare[CHUNK:] + in_query
        whole = jnp.sum(keys * closed) + jnp.sum(
            chunk_whole * jnp.sum(grads_after[h, c] * befores[h, c], axis=0, keepdims=True)
        )
        last_row = iota((CHUNK, 1), 0) == CHUNK - 1
        grad_total = grad_total + jnp.where(last_row, whole, 0.0)
        columns[h, c] = (
            grad_query - query * in_query,
            left + right - keys * (in_left + in_right),
            grad_value,
            grad_beta,
            grad_total,
        )

    lane = iota((SPAN, DK), 1)
    rates = jnp.zeros((SPAN, DK), F32)
    for h in range(heads):
        mixed, unit, scale, values, beta = parts[h]
        got = [columns[h, c] for c in range(per)]
        low, high = slice(0, CHUNK), slice(CHUNK, 2 * CHUNK)
        stack = lambda index, part: jnp.concatenate([g[index][part] for g in got], axis=0)
        act_grads = [
            scale[0] * stack(0, low),
            scale[1] * stack(1, low),
            scale[2] * stack(1, high),
            stack(2, low),
            stack(2, high),
        ]
        for i, column in enumerate((stack(3, low), stack(3, high), stack(4, low))):
            rates = rates + jnp.where(lane == 3 * h + i, column, 0.0)
        for part in range(5):
            cols = part_columns(h, part)
            sig = jax.nn.sigmoid(mixed[part])
            grad = act_grads[part] * sig * (1.0 + mixed[part] * (1.0 - sig))
            mixed_grad[8 : 8 + SPAN, cols] = grad
            conv_out[24:32, cols] += fold(grad * ext[8 : 8 + SPAN, cols])
            for s in range(1, CONV):
                moved = jnp.where(masks[s], ext[8 - s : 8 - s + SPAN, cols], 0.0)
                tap = CONV - 1 - s
                conv_out[8 * tap : 8 * tap + 8, cols] += fold(grad * moved)

    ahead = conv_masks(span_start, marks, ends, SPAN, 1)
    for h in range(heads):
        for part in range(5):
            cols = part_columns(h, part)
            grad = mixed_grad[8 : 8 + SPAN, cols] * conv[CONV - 1 : CONV, cols]
            for s in range(1, CONV):
                moved = jnp.where(ahead[s], mixed_grad[8 + s : 8 + s + SPAN, cols], 0.0)
                grad = grad + moved * conv[CONV - 1 - s : CONV - s, cols]
            begin = h * MIXW + part * DK
            grad_raw_out[:, begin : begin + DK] = grad.astype(BF16)

            @pl.when(step == 0)
            def _():
                tail_out[:, cols] = grad[SPAN - HALO :]

        grad_raw_out[:, h * MIXW + QKV : (h + 1) * MIXW] = gate_grad[:, h * DV : (h + 1) * DV]

    @pl.when(at_step == 0)
    def _():
        rim_masks = conv_masks(marks[0] - 8, marks, ends, 8, 1)
        for h in range(heads):
            for part in range(5):
                cols = part_columns(h, part)
                grad = jnp.zeros((8, DK), F32)
                for s in range(1, CONV):
                    moved = jnp.where(rim_masks[s], mixed_grad[s : s + 8, cols], 0.0)
                    grad = grad + moved * conv[CONV - 1 - s : CONV - s, cols]
                rim_out[:, cols] = grad

    back = mm(chunk_sum_matrix(True), rates, NN, 6)
    lanes = iota((1, DK), 1)
    is_gate = (lanes % (NH + 1) == NH) & (lanes < heads * (NH + 1))
    grad_logits = jnp.where(is_gate, back * alpha[...] * betas, rates * betas * (1.0 - betas))
    grad_raw_out[:, heads * MIXW :] = grad_logits.astype(BF16)
    sums_out[0:8] += fold(grad_logits)
    sums_out[8:16] += fold(back * gates)


def mixer_backward(
    heads, ends, marks, place, maps, state_grads, start, raw, rim, conv, logits, alpha,
    inv, transfers, states, reads, attn_grad, gate_grad,
):
    rows, wide = raw.shape
    steps, per = rows // SPAN, SPAN // CHUNK
    turn = lambda i: steps - 1 - i
    row = lambda width: block((SPAN, width), lambda i: (turn(i), 0))
    cube = lambda last: block((per, heads, SPAN, last), lambda i: (turn(i), 0, 0, 0))
    return pl.pallas_call(
        functools.partial(mixer_back_kernel, heads, ends, steps),
        grid=(steps,),
        in_specs=[
            SCALARS,
            SCALARS,
            once(maps.shape),
            once(state_grads.shape),
            fixed(start.shape),
            row(wide),
            block((8, wide), lambda i: (jnp.maximum(turn(i) * (SPAN // 8) - 1, 0), 0)),
            fixed(rim.shape),
            fixed(conv.shape),
            row(DK),
            fixed(alpha.shape),
            cube(SPAN),
            cube(DK),
            cube(DK + DV),
            row(heads * DK),
            row(heads * DV),
            row(heads * DV),
        ],
        out_specs=[
            row(heads * MIXW + DK),
            fixed((HALO, wide)),
            fixed((8, wide)),
            fixed((16, DK)),
            fixed((8 * CONV, wide)),
        ],
        out_shape=[
            shape((rows, heads * MIXW + DK), BF16),
            shape((HALO, wide)),
            shape((8, wide)),
            shape((16, DK)),
            shape((8 * CONV, wide)),
        ],
        scratch_shapes=[
            pltpu.VMEM((8 + SPAN, wide), F32),
            pltpu.VMEM((8 + SPAN + 8, wide), F32),
            pltpu.VMEM((heads, DK, DV), F32),
        ],
        compiler_params=params(60),
        cost_estimate=cost(50),
        name="mixer_backward",
    )(
        marks, place, maps, state_grads, start, raw, raw, rim, conv, logits, alpha,
        inv, transfers, states, reads, attn_grad, gate_grad,
    )


def weights_kernel(widths, orders, place, h_one, halo, grad, rim, out_weights, *outs):
    step, count = pl.program_id(0), pl.num_programs(0)
    total = mm(h_one[...], grad[...], TN) + mm(halo[...], rim[...], TN)
    total = jnp.concatenate([total, jnp.transpose(out_weights[...].astype(F32))], axis=1)
    at = 0
    for k, (width, order) in enumerate(zip(widths, orders)):
        value = total[:, at : at + width].astype(BF16)
        at += width
        position = weight_places(step, order)

        @pl.when(position < count // 2)
        def _():
            outs[2 * k][position] = value

        @pl.when(position >= count // 2)
        def _():
            outs[2 * k + 1][position - count // 2] = value


def weight_places(i, bits_in_order):
    position = 0
    for bit in bits_in_order:
        position = 2 * position + lax.rem(i // bit, 2)
    return position


def mixer_weights(place, ranges, h_one, halo, grad, rim, out_weights, widths, orders):
    rows, model = h_one.shape
    deep = model // ranges
    if deep % DK:
        whole = (t_dot(h_one, grad) + t_dot(halo, rim)).astype(BF16)
        whole = jnp.concatenate([whole, out_weights.T], axis=1).reshape(ranges, deep, -1)
        cuts, at = [], 0
        for width, order in zip(widths, orders):
            whole_cut = ordered(whole[:, :, at : at + width], order)
            cuts.append((whole_cut[: ranges // 2], whole_cut[ranges // 2 :]))
            at += width
        return cuts
    outs = pl.pallas_call(
        functools.partial(weights_kernel, widths, orders),
        grid_spec=pltpu.PrefetchScalarGridSpec(
            num_scalar_prefetch=1,
            grid=(ranges,),
            in_specs=[
                block((rows, deep), lambda i, place: (0, i ^ place[0])),
                block((HALO, deep), lambda i, place: (0, i ^ place[0])),
                block(grad.shape, lambda i, place: (0, 0)),
                block(rim.shape, lambda i, place: (0, 0)),
                block((out_weights.shape[0], deep), lambda i, place: (0, i ^ place[0])),
            ],
            out_specs=[
                block((ranges // 2, deep, width), lambda i, place: (0, 0, 0))
                for width in widths
                for _ in range(2)
            ],
        ),
        out_shape=[
            shape((ranges // 2, deep, width), BF16) for width in widths for _ in range(2)
        ],
        compiler_params=params(60),
        cost_estimate=cost(5),
        name="mixer_weights",
    )(place, h_one, halo, grad, rim, out_weights)
    return list(zip(outs[::2], outs[1::2]))


def input_kernel(heads, who, x, gain, grad, w_mixer, w_rates, gain_grad_out, kept, sent):
    step = pl.program_id(0)

    @pl.when(step == 0)
    def _():
        gain_grad_out[...] = jnp.zeros_like(gain_grad_out)
        rows = kept.shape[1] - HALO
        for out in (kept, sent):
            out[:, rows:] = jnp.zeros((out.shape[0], HALO, out.shape[2]), BF16)

    back = mm(grad[:, : heads * MIXW], w_mixer[...], NT) + mm(
        grad[:, heads * MIXW :], w_rates[...], NT
    )
    values = x[...].astype(F32)
    unit = values * rms_scale(values)
    seen = back * unit
    gain_grad_out[...] += fold(seen)
    keep_shares(step, back.astype(BF16), who[0], kept, sent)
    dots = jnp.sum(seen * gain[...], axis=-1, keepdims=True)
    dots = jnp.transpose(jnp.broadcast_to(dots, (ROWS, DK)))[:HALO]
    rows, share = kept.shape[1] - HALO, kept.shape[2]
    per = ROWS // share
    at = iota((HALO, share), 0)
    for k in range(per):
        line = jnp.where(at == step * per + k, dots[:, k * share : (k + 1) * share], 0.0)
        for out in (kept, sent):
            for j in range(out.shape[0]):
                out[j, rows:] = (out[j, rows:].astype(F32) + line).astype(BF16)


def input_backward(heads, count, who, x_all, gain, grad, w_mixer, w_rates):
    rows, model = x_all.shape
    share = model // count
    row = lambda width: block((ROWS, width), lambda i: (i, 0))
    return pl.pallas_call(
        functools.partial(input_kernel, heads),
        grid=(rows // ROWS,),
        in_specs=[
            SCALARS, row(model), fixed(gain.shape), row(grad.shape[1]), once(w_mixer.shape), once(w_rates.shape),
        ],
        out_specs=[fixed((8, model))] + [fixed((count // 2, rows + HALO, share))] * 2,
        out_shape=[shape((8, model))] + [shape((count // 2, rows + HALO, share), BF16)] * 2,
        compiler_params=params(60),
        cost_estimate=cost(6),
        name="input_backward",
    )(who, x_all, gain, grad, w_mixer, w_rates)


def tokens_kernel(model, who, x, gain, resid_grad, own_dots, came_dots, own, came, out):
    share = out.shape[1]
    cols = pl.ds(pl.multiple_of(who[0] * share, share), share)
    scale = rms_scale(x[...].astype(F32))
    unit = x[:, cols].astype(F32) * scale
    dots = own_dots[...].astype(F32) + came_dots[...].astype(F32)
    per = ROWS // share
    at = iota((HALO, share), 0)
    line = jnp.concatenate(
        [
            jnp.sum(jnp.where(at == pl.program_id(0) * per + k, dots, 0.0), axis=0, keepdims=True)
            for k in range(per)
        ],
        axis=1,
    )
    mean = jnp.transpose(jnp.broadcast_to(line, (8, ROWS)))[:, :1] / model
    back = (own[...].astype(F32) + came[...].astype(F32)) * gain[:, cols]
    out[...] = (resid_grad[...] + scale * (back - unit * mean)).astype(BF16)


def tokens_backward(who, x_all, gain, resid_grad, own, came):
    rows, model = x_all.shape
    share = own.shape[1]
    row = lambda width: block((ROWS, width), lambda i: (i, 0))
    extra = block((HALO, share), lambda i: (rows // HALO, 0))
    return pl.pallas_call(
        functools.partial(tokens_kernel, model),
        grid=(rows // ROWS,),
        in_specs=[
            SCALARS, row(model), fixed(gain.shape), row(share), extra, extra, row(share), row(share),
        ],
        out_specs=row(share),
        out_shape=shape((rows, share), BF16),
        compiler_params=params(10),
        cost_estimate=cost(2),
        name="tokens_backward",
    )(who, x_all, gain, resid_grad, own, came, own, came)


def shifted(value, axis, steps):
    count = lax.axis_size(axis)
    first, last = (max(0, -steps), min(count, count - steps))
    return lax.ppermute(value, axis, [(source, source + steps) for source in range(first, last)])


def swap(value, axis, mask):
    return lax.ppermute(value, axis, [(i, i ^ mask) for i in range(lax.axis_size(axis))])


def bits(axis):
    count, bit = lax.axis_size(axis), 1
    while bit < count:
        yield bit
        bit *= 2


def spread(value, axis, order, beside=()):
    found = {0: value}
    for at, bit in enumerate(order):
        came = {m | bit: swap(v, axis, bit) for m, v in list(found.items())}
        if at == 0 and beside:
            came[bit], *beside = tie(came[bit], *beside)
        found.update(came)
    return [found[m] for m in range(len(found))], beside


def spread_seq(value):
    found = {0: value}
    count = lax.axis_size("seq")
    for m in range(2, count, 2):
        found[m] = swap(value, "seq", m)
    for m in range(0, count, 2):
        found[m + 1] = swap(found[m], "seq", 1)
    return jnp.stack([found[m] for m in range(count)])


def tie(*values):
    return lax.optimization_barrier(values)


def core_sum(mine, other):
    return mine + swap(other, "head", 1)


def over_y(total, came):
    total = total + came
    for bit in bits("head"):
        if bit > 2:
            total = total + swap(total, "head", bit)
    return total, swap(total, "head", 1)


def summed_shares(kept, sent):
    for bit in bits("head"):
        came = swap(sent, "head", bit)
        half = kept.shape[0] // 2
        if half:
            sent = kept[half:] + came[half:]
            kept = kept[:half] + came[:half]
    return kept[0], came[0]


def summed(value, axis):
    for bit in bits(axis):
        value = value + swap(value, axis, bit)
    return value


def spread_small(value):
    found = [value] + [swap(value, "seq", m) for m in range(2, lax.axis_size("seq"), 2)]
    here = jnp.stack(found)
    there = swap(here, "seq", 1)
    return jnp.stack([here, there], axis=1).reshape((-1,) + value.shape)


def ordered(value, order):
    place = lax.axis_index("seq")
    positions = [0]
    for bit in order[::-1]:
        positions = positions + [m | bit for m in positions]
    return jnp.take(value, jnp.array(positions) ^ place, axis=0)


def first_exchange(cuts, orders):
    came = []
    for (_, sent), order in zip(cuts, orders):
        if came:
            at = -1 if order[0] == orders[0][0] else 0
            came[at], sent = tie(came[at], sent)
        came.append(swap(sent, "seq", order[0]))
    return came


def scattered(cuts, came, orders):
    kept = [k for k, _ in cuts]
    for stage in range(len(orders[0])):
        if stage:
            came = [swap(value, "seq", order[stage]) for value, order in zip(sent, orders)]
        half = kept[0].shape[0] // 2
        sent = [k[half:] + c[half:] for k, c in zip(kept, came)]
        kept = [k[: max(half, 1)] + c[: max(half, 1)] for k, c in zip(kept, came)]
    return [k[0] for k in kept]


def t_dot(leading, trailing):
    return lax.dot_general(leading, trailing, TN, preferred_element_type=F32)


def local(
    tokens, lengths, norm1_gain, w_mixer, w_rates, decay_log, rates_bias, conv_weight,
    out_gain, w_out, norm2_gain, w_ffn_gate, w_ffn_up, w_ffn_down, out_grad,
):
    rows, share = tokens.shape
    heads = decay_log.shape[0]
    ends = lengths.shape[0]
    model = norm1_gain.shape[0]
    group, ranges = lax.axis_size("head"), lax.axis_size("seq")
    place, member = lax.axis_index("seq"), lax.axis_index("head")
    marks = jnp.concatenate(
        [jnp.reshape(place * rows, (1,)), jnp.cumsum(lengths)]
    ).astype(jnp.int32)
    place_arg = jnp.reshape(place, (1,)).astype(jnp.int32)
    who = jnp.reshape(member, (1,)).astype(jnp.int32)
    down_bits = list(bits("head"))[::-1]
    seq_bits = list(bits("seq"))

    halo = shifted(tokens[rows - HALO :], "seq", 1)
    gain_one, gain_two = norm1_gain[None, :], norm2_gain[None, :]
    gain_out = out_gain[None, :]
    spare = DK - heads * (NH + 1)
    rates_w = jnp.pad(w_rates, ((0, 0), (0, spare)))
    bias = jnp.pad(rates_bias, (0, spare))[None, :]
    none = jnp.zeros((heads,), F32)
    alpha = jnp.stack([none] * NH + [-jnp.exp(decay_log)], axis=-1).reshape(-1)
    alpha = jnp.pad(alpha, (0, spare))[None, :]

    token_parts, (marks, rates_w, bias, alpha) = spread(
        jnp.concatenate([tokens, halo], axis=0), "head", down_bits, (marks, rates_w, bias, alpha)
    )
    (
        x_all, h_one, h_halo, raw, rim, gate_o, logits, inv, transfers, states, reads, own, far, end_state,
    ) = mixer_forward(
        heads, ends, marks, who, token_parts, gain_one, w_mixer, rates_w, bias, alpha, conv_weight
    )
    out_grad, end_state = tie(out_grad, end_state)
    grad_parts, _ = spread(out_grad, "head", down_bits)
    maps = spread_seq(end_state)
    attn, normed, start, *branch = branch_forward(
        heads, place_arg, who, maps, own, far, gate_o, gain_out, w_out, grad_parts
    )
    pieces = len(branch) // 2
    halves = [core_sum(branch[p], branch[pieces + p]) for p in range(pieces)]
    sent_y = [swap(halves[0], "head", 2)]
    for p in range(1, pieces):
        sent_y[-1], halves[p] = tie(sent_y[-1], halves[p])
        sent_y.append(swap(halves[p], "head", 2))
    branch, dh_halves, dh, filled = [], [], [], []
    gate_t, up_t = w_ffn_gate.T, w_ffn_up.T
    for p in range(pieces):
        if p:
            sent_y[p], *filled = tie(sent_y[p], *filled)
        branch.append(over_y(halves[p], sent_y[p]))
        *filled, dh_mine, dh_other = ffn_pass(
            p, who, x_all, *branch[p], grad_parts, gain_two, gate_t, up_t, w_ffn_down, filled
        )
        if p:
            dh_y, dh_other = tie(dh_y, dh_other)
            dh.append(over_y(dh_halves[p - 1], dh_y))
        dh_halves.append(core_sum(dh_mine, dh_other))
        dh_y = swap(dh_halves[p], "head", 2)
    h_two, act, grad_gate, grad_up, grad_full, kept, sent = filled
    dh_halves[-1], act, grad_gate, grad_up = tie(dh_halves[-1], act, grad_gate, grad_up)
    by_owner = lambda value: jnp.swapaxes(
        value.reshape(value.shape[0], ranges, model // ranges), 0, 1
    ).astype(BF16)
    ffn_grads = jnp.concatenate(
        [by_owner(t_dot(act, grad_full)), by_owner(t_dot(grad_gate, h_two)), by_owner(t_dot(grad_up, h_two))],
        axis=1,
    )
    dh_y, ffn_grads = tie(dh_y, ffn_grads)
    ffn_grads = lax.psum_scatter(ffn_grads, "seq", scatter_dimension=0, tiled=False)
    dh.append(over_y(dh_halves[-1], dh_y))
    hidden = act.shape[1]
    (
        out_weights, grad_attn, grad_gate_o, resid_own, gain_two_part, out_gain_part, state_grad,
    ) = resid_backward(
        heads, who, share, x_all, branch, dh, grad_full, gain_two, w_out, normed, attn, gate_o, gain_out, far
    )

    sent, state_grad = tie(sent, state_grad)
    state_grads = spread_small(state_grad.astype(BF16))
    grad_raw, tail, rim_grad, sums, conv_parts = mixer_backward(
        heads, ends, marks, place_arg, maps, state_grads, start, raw, rim, conv_weight, logits, alpha,
        inv, transfers, states, reads, grad_attn, grad_gate_o,
    )
    rim_wide = jnp.pad(rim_grad, ((HALO - 8, 0), (0, 0))).astype(BF16)
    none = jnp.zeros((HALO, MIXW - QKV), BF16)
    rim_wide = jnp.concatenate(
        [b for h in range(heads) for b in (rim_wide[:, h * QKV : (h + 1) * QKV], none)]
        + [jnp.zeros((HALO, DK), BF16)],
        axis=1,
    )
    cut_widths = [MIXW] * (heads - 1) + [512, 256, DK + heads * DV]
    orders = [seq_bits] * (heads + 1) + [seq_bits[1:] + seq_bits[:1]]
    cuts = mixer_weights(
        place_arg, ranges, h_one, h_halo, grad_raw, rim_wide, out_weights, cut_widths, orders
    )
    cuts, ffn_grads, conv_parts, sums, rim_grad, kept = tie(
        cuts, ffn_grads, conv_parts, sums, rim_grad, kept
    )
    grad_down, grad_wgate, grad_wup = (
        ffn_grads[k * hidden : (k + 1) * hidden].astype(F32) for k in range(3)
    )
    came = first_exchange(cuts, orders)
    came[0], grad_raw = tie(came[0], grad_raw)
    first, second = summed_shares(kept, sent)
    own_cols = lambda value: lax.dynamic_slice_in_dim(value, member * share, share, 1)
    even = member % 2 == 0
    branch_own = []
    for mine, other in branch:
        mine, other = own_cols(mine), own_cols(other)
        branch_own += [jnp.where(even, mine, other), jnp.where(even, other, mine)]
    output = (
        tokens.astype(F32)
        + jnp.concatenate(branch_own, axis=0).astype(F32)
        + (first.astype(F32) + second.astype(F32))
    ).astype(BF16)
    tail = tail.at[HALO - 8 :].add(shifted(rim_grad, "seq", -1))
    for h in range(heads):
        grad_raw = lax.dynamic_update_slice(
            grad_raw, tail[:, h * QKV : (h + 1) * QKV].astype(BF16), (rows - HALO, h * MIXW)
        )
    gain_one_part, back_kept, back_sent = input_backward(
        heads, group, who, x_all, gain_one, grad_raw, w_mixer, rates_w
    )
    back_own, back_came = summed_shares(back_kept, back_sent)
    sum_rows = jnp.sum(sums.reshape(2, 8, DK), axis=1)
    small = jnp.concatenate(
        [
            jnp.sum(gain_one_part, axis=0),
            jnp.sum(out_gain_part, axis=0),
            jnp.sum(gain_two_part, axis=0),
            sum_rows[0],
            sum_rows[1],
            jnp.sum(conv_parts.reshape(CONV, 8, heads * QKV), axis=1).reshape(-1),
        ]
    )
    small = small.reshape(-1, DK)
    came[-2], small, back_own = tie(came[-2], small, back_own)
    cuts = scattered(cuts, came, orders)
    tokens_grad = tokens_backward(who, x_all, gain_one, resid_own, back_own, back_came)
    grad_wmixer = jnp.concatenate(cuts[:-1], axis=1).astype(F32)
    grad_wrates = cuts[-1][:, : heads * (NH + 1)].astype(F32)
    grad_wout = cuts[-1][:, DK:].T.astype(F32)

    small = summed(small, "seq").reshape(-1)
    cut = [model, DV, model, DK, DK]
    pieces_of, at = [], 0
    for size in cut:
        pieces_of.append(small[at : at + size])
        at += size
    over_head = summed(small[: model + DV], "head")
    grad_norm1, grad_outgain = over_head[:model], over_head[model:]
    _, _, grad_norm2, bias_row, decay_row = pieces_of
    grad_conv = small[at:].reshape(CONV, heads * QKV)
    grad_bias = bias_row[: heads * (NH + 1)]
    grad_decay = decay_row[: heads * (NH + 1)].reshape(heads, NH + 1)[:, NH]
    return (
        output, tokens_grad, grad_norm1, grad_wmixer, grad_wrates, grad_decay, grad_bias, grad_conv,
        grad_outgain, grad_wout, grad_norm2, grad_wgate.T, grad_wup.T, grad_down,
    )


def solution(mesh):
    placed = (
        P("seq", "head"), P(), P(), P(None, "head"), P(None, "head"), P("head"), P("head"), P(None, "head"),
        P(), P("head", None), P(), P(None, "head"), P(None, "head"), P("head", None), P("seq", "head"),
    )
    return jax.shard_map(
        local,
        mesh=mesh,
        in_specs=placed,
        out_specs=(
            P("seq", "head"), P("seq", "head"), P(), P("seq", "head"), P("seq", "head"), P("head"), P("head"),
            P(None, "head"), P(), P("head", "seq"), P(), P("seq", "head"), P("seq", "head"), P("head", "seq"),
        ),
        check_vma=False,
    )
```

```python
import functools

import jax
import jax.numpy as jnp
from jax import lax
from jax.experimental import pallas as pl
from jax.experimental.pallas import tpu as pltpu
from jax.sharding import PartitionSpec as P

DK = 128
DV = 128
NH = 2
CONV = 4
QKV = 640
MIXW = 768
EPS = 1e-06

CHUNK = 64
TILE = 2 * CHUNK
FWD_SPAN = 256
BWD_SPAN = 128
ROWS = 256
LEVELS = 6
HALO = 16

F32 = jnp.float32
BF16 = jnp.bfloat16

NN = (((1,), (0,)), ((), ()))
NT = (((1,), (1,)), ((), ()))
TN = (((0,), (0,)), ((), ()))

P_INV = 1
P_FWD = 3
P_STATE = 3
P_BWD = 1
P_SOLVE = 3
P_PAIR = 3


def halves(value):
    high = value.astype(BF16)
    return high, (value - high.astype(F32)).astype(BF16)


def mm(left, right, dims=NN, passes=1):
    if passes == 1:
        return lax.dot_general(
            left.astype(BF16), right.astype(BF16), dims, preferred_element_type=F32
        )
    if passes == 6:
        return lax.dot_general(
            left, right, dims, precision=lax.Precision.HIGHEST, preferred_element_type=F32
        )
    left_h, left_l = halves(left)
    right_h, right_l = halves(right)
    dot = functools.partial(lax.dot_general, dimension_numbers=dims, preferred_element_type=F32)
    return dot(left_h, right_h) + (dot(left_h, right_l) + dot(left_l, right_h))


def iota(shape, axis):
    return lax.broadcasted_iota(jnp.int32, shape, axis)


def doc_of(place, marks, ends):
    count = jnp.zeros_like(place)
    for j in range(ends):
        count = count + jnp.where(place >= marks[1 + j], 1, 0)
    return jnp.where(place < 0, -1, count)


def doc_scalar(place, marks, ends):
    count = jnp.int32(0)
    for j in range(ends):
        count = count + (place >= marks[1 + j]).astype(jnp.int32)
    return jnp.where(place < 0, -1, count)


def conv_masks(start, marks, ends, rows, direction):
    place = start + iota((rows, DK), 0)
    here = doc_of(place, marks, ends)
    return [None] + [
        doc_of(place + direction * s, marks, ends) == here for s in range(1, CONV)
    ]


def softplus(v):
    return jnp.maximum(v, 0.0) + jnp.log1p(jnp.exp(-jnp.abs(v)))


def chunk_sum_matrix(upper):
    row, col = iota((TILE, TILE), 0), iota((TILE, TILE), 1)
    keep = (col >= row) if upper else (col <= row)
    keep = keep & ((row // CHUNK) == (col // CHUNK))
    return jnp.where(keep, 1.0, 0.0).astype(F32)


def chunk_sums(upper, value):
    matrix = chunk_sum_matrix(upper)
    return jnp.concatenate(
        [mm(matrix, value[at : at + TILE], NN, 6) for at in range(0, value.shape[0], TILE)], axis=0
    )


def part_columns(h, part):
    begin = h * QKV + part * DK
    return slice(begin, begin + DK)


def convolved(ext, conv, masks, h, part):
    cols = part_columns(h, part)
    span = masks[1].shape[0]
    total = ext[8 : 8 + span, cols] * conv[CONV - 1 : CONV, cols]
    for s in range(1, CONV):
        moved = jnp.where(masks[s], ext[8 - s : 8 - s + span, cols], 0.0)
        total = total + moved * conv[CONV - 1 - s : CONV - s, cols]
    return total


def two(array, c):
    piece = array[c * CHUNK : (c + 1) * CHUNK]
    return jnp.concatenate([piece, piece], axis=0)


def pair(first, second, c):
    at = slice(c * CHUNK, (c + 1) * CHUNK)
    return jnp.concatenate([first[at], second[at]], axis=0)


def unit_rows(v):
    scale = lax.rsqrt(jnp.sum(v * v, axis=-1, keepdims=True) + EPS)
    return v * scale, scale


def token_masks():
    row, col = iota((TILE, TILE), 0), iota((TILE, TILE), 1)
    tok_r, tok_c = row % CHUNK, col % CHUNK
    strict = (tok_c < tok_r) | ((tok_c == tok_r) & (row >= CHUNK) & (col < CHUNK))
    return tok_r ^ tok_c, strict


def gate_tiles(logits, alpha):
    gates = alpha * softplus(logits)
    sums = chunk_sums(False, gates)
    rows = []
    for at in range(0, logits.shape[0], TILE):
        flat = jnp.transpose(sums[at : at + TILE])[:8]
        turned = pltpu.roll(flat, CHUNK, 1)
        lane = iota(flat.shape, 1)
        rows.append(jnp.where(lane < CHUNK, flat, turned))
        rows.append(jnp.where(lane < CHUNK, turned, flat))
    return gates, sums, rows


def spread_column(tile, col):
    return jnp.broadcast_to(tile[:, col : col + 1], (tile.shape[0], DK))


def chunk_gates(span_start, marks, ends, sums, rows, h, c):
    start = span_start + c * CHUNK
    col_place = start + iota((CHUNK, TILE), 0)
    row_place = start + iota((CHUNK, TILE), 1) % CHUNK
    col_doc = doc_of(col_place, marks, ends)
    row_doc = doc_of(row_place, marks, ends)
    total = spread_column(sums[c * CHUNK : (c + 1) * CHUNK], 3 * h + 2)
    across = rows[c][3 * h + 2 : 3 * h + 3]
    kept = (col_doc == row_doc) & (row_place <= col_place)
    decay = jnp.exp(jnp.where(kept, total - across, -1e30))
    doc_before = doc_scalar(start - 1, marks, ends)
    doc_last = doc_scalar(start + CHUNK - 1, marks, ends)
    last = total[CHUNK - 1 : CHUNK]
    opening = jnp.where(col_doc == doc_before, jnp.exp(total), 0.0)
    closing = jnp.where(col_doc == doc_last, jnp.exp(last - total), 0.0)
    whole = jnp.where(doc_before == doc_last, jnp.exp(last), 0.0)
    return decay, opening, closing, whole


def inverses(lowers, apart):
    eye = jnp.where(iota((TILE, TILE), 0) == iota((TILE, TILE), 1), 1.0, 0.0)
    result = [eye - jnp.where(apart == 0, lower, 0.0) for lower in lowers]
    for level in range(LEVELS):
        here = (apart >> level) == 1
        steps = [
            mm(inverse, jnp.where(here, lower, 0.0), NN, P_INV)
            for inverse, lower in zip(result, lowers)
        ]
        result = [
            inverse - mm(step, inverse, NN, P_INV) for inverse, step in zip(result, steps)
        ]
    return result


def rms_scale(values):
    return lax.rsqrt(jnp.mean(values * values, axis=-1, keepdims=True) + EPS)


def in_order(parts, me):
    bit = 1
    while bit < len(parts):
        flip = (me // bit) % 2 == 1
        parts = [jnp.where(flip, parts[m ^ bit], parts[m]) for m in range(len(parts))]
        bit *= 2
    return parts


def mixer_kernel(heads, ends, count, marks, who, *refs):
    tokens, halos, refs = refs[:count], refs[count : 2 * count], refs[2 * count :]
    (
        gain, w_mixer, w_rates, bias, alpha, conv,
        x_out, h_out, halo_out, raw_out, rim_out, gate_out, logit_out, inv_out, map_out, state_out,
        read_out, own_out, far_out, end_out, ext, state,
    ) = refs
    step = pl.program_id(0)
    joined = lambda parts: jnp.concatenate(in_order([p[...] for p in parts], who[0]), axis=1)
    span_start = marks[0] + step * FWD_SPAN

    def rounded_norm(rows):
        values = rows.astype(F32)
        return (values * rms_scale(values) * gain[...]).astype(BF16)

    @pl.when(step == 0)
    def _():
        halo_out[...] = rounded_norm(joined(halos))
        halo = jnp.dot(halo_out[...], w_mixer[...], preferred_element_type=F32)
        for h in range(heads):
            ext[0:8, h * QKV : (h + 1) * QKV] = halo[HALO - 8 :, h * MIXW : h * MIXW + QKV]
        rim_out[...] = ext[0:8]
        for h in range(heads):
            state[h, :, :DV] = jnp.zeros((DK, DV), F32)
            state[h, :, DV:] = jnp.where(
                iota((DK, DK), 0) == iota((DK, DK), 1), 1.0, 0.0
            ).astype(F32)

    @pl.when(step > 0)
    def _():
        ext[0:8] = ext[FWD_SPAN : FWD_SPAN + 8]

    x = joined(tokens)
    x_out[...] = x
    h_one = rounded_norm(x)
    h_out[...] = h_one
    raw = jnp.dot(h_one, w_mixer[...], preferred_element_type=F32)
    for h in range(heads):
        ext[8 : 8 + FWD_SPAN, h * QKV : (h + 1) * QKV] = raw[:, h * MIXW : h * MIXW + QKV]
        gate_out[:, h * DV : (h + 1) * DV] = raw[:, h * MIXW + QKV : (h + 1) * MIXW]
    raw_out[...] = ext[8 : 8 + FWD_SPAN]
    logits = jnp.dot(h_one, w_rates[...], preferred_element_type=F32) + bias[...]
    logit_out[...] = logits
    masks = conv_masks(span_start, marks, ends, FWD_SPAN, -1)
    apart, strict = token_masks()
    betas = jax.nn.sigmoid(logits)
    _, sums, rows = gate_tiles(logits, alpha[...])

    units = [(h, c) for h in range(heads) for c in range(FWD_SPAN // CHUNK)]
    parts = {}
    for h in range(heads):
        active = []
        for part in range(5):
            mixed = convolved(ext, conv, masks, h, part)
            active.append(mixed * jax.nn.sigmoid(mixed))
        unit = [unit_rows(active[part])[0] for part in range(3)]
        beta = [spread_column(betas, 3 * h + i) for i in range(NH)]
        parts[h] = (unit, active[3:], beta)

    lowers, reads, sides, lasts, wholes, queries = [], [], [], [], [], []
    for h, c in units:
        (query, key_a, key_b), (value_a, value_b), (beta_a, beta_b) = parts[h]
        keys, values, beta = (
            pair(key_a, key_b, c),
            pair(value_a, value_b, c),
            pair(beta_a, beta_b, c),
        )
        query_c = query[c * CHUNK : (c + 1) * CHUNK]
        decay, opening, closing, whole = chunk_gates(
            span_start, marks, ends, sums, rows, h, c
        )
        decay_two = jnp.concatenate([decay, decay], axis=0)
        opening_two = jnp.concatenate([opening, opening], axis=0)
        closing_two = jnp.concatenate([closing, closing], axis=0)
        lowers.append(
            jnp.where(strict, beta * decay_two * mm(keys, keys, NT, P_FWD), 0.0)
        )
        reads.append(decay * mm(query_c, keys, NT, P_FWD))
        sides.append(
            jnp.concatenate([beta * values, beta * opening_two * keys], axis=1)
        )
        lasts.append(closing_two * keys)
        wholes.append(whole)
        queries.append(opening * query_c)
    solved = inverses(lowers, apart)
    pieces = [mm(inverse, side, NN, P_FWD) for inverse, side in zip(solved, sides)]
    maps = [mm(last, piece, TN, P_FWD) for last, piece in zip(lasts, pieces)]
    seen = [mm(read, piece, NN, P_FWD) for read, piece in zip(reads, pieces)]
    diagonal = iota((DK, DK), 0) == iota((DK, DK), 1)
    for index, (h, c) in enumerate(units):
        inv_out[c, h] = solved[index]
        transfer = jnp.where(diagonal, wholes[index], 0.0) - maps[index][:, DV:]
        map_out[c, h] = transfer
        reader = queries[index] - seen[index][:, DV:]
        at, col = slice(c * CHUNK, (c + 1) * CHUNK), slice(h * DK, (h + 1) * DK)
        read_out[at, col] = reader
        before = state[h]
        state_out[c, h] = before
        both = mm(reader, before, NN, P_STATE)
        own_out[at, col] = seen[index][:, :DV] + both[:, :DV]
        far_out[at, col] = both[:, DV:]
        after = mm(transfer, before, NN, P_STATE)
        state[h, :, :DV] = after[:, :DV] + maps[index][:, :DV]
        state[h, :, DV:] = after[:, DV:]
    end_out[...] = state[...].astype(BF16)


def block(shape, index):
    return pl.BlockSpec(shape, index)


def fixed(shape):
    return pl.BlockSpec(shape, lambda i: (0,) * len(shape))


def once(shape):
    return pl.BlockSpec(
        shape, lambda i: (0,) * len(shape), pipeline_mode=pl.Buffered(buffer_count=1)
    )


SCALARS = pl.BlockSpec(memory_space=pltpu.SMEM)


def shape(dims, kind=F32):
    return jax.ShapeDtypeStruct(dims, kind)


def params(megabytes):
    return pltpu.CompilerParams(
        dimension_semantics=("arbitrary",), vmem_limit_bytes=megabytes << 20
    )


def cost(microseconds):
    return pl.CostEstimate(
        flops=int(microseconds * 1.1e8), bytes_accessed=int(microseconds * 1e5), transcendentals=0
    )


WHOLE = pl.BlockSpec(memory_space=pl.ANY)


def mixer_forward(heads, ends, marks, who, tokens, gain, w_mixer, w_rates, bias, alpha, conv):
    rows, share = tokens[0].shape
    rows = rows - HALO
    model = gain.shape[1]
    steps, chunks, per = rows // FWD_SPAN, rows // CHUNK, FWD_SPAN // CHUNK
    wide = heads * QKV
    row = lambda width: block((FWD_SPAN, width), lambda i: (i, 0))
    cube = lambda last: block((per, heads, TILE, last), lambda i: (i, 0, 0, 0))
    return pl.pallas_call(
        functools.partial(mixer_kernel, heads, ends, len(tokens)),
        grid=(steps,),
        in_specs=[SCALARS, SCALARS]
        + [row(share)] * len(tokens)
        + [block((HALO, share), lambda i: (rows // HALO, 0))] * len(tokens)
        + [
            fixed((1, model)),
            once(w_mixer.shape),
            once(w_rates.shape),
            fixed(bias.shape),
            fixed(alpha.shape),
            fixed(conv.shape),
        ],
        out_specs=[
            row(model),
            row(model),
            fixed((HALO, model)),
            row(wide),
            fixed((8, wide)),
            row(heads * DV),
            row(DK),
            cube(TILE),
            cube(DK),
            cube(DK + DV),
            row(heads * DK),
            row(heads * DV),
            row(heads * DK),
            fixed((heads, DK, DK + DV)),
        ],
        out_shape=[
            shape((rows, model), BF16),
            shape((rows, model), BF16),
            shape((HALO, model), BF16),
            shape((rows, wide)),
            shape((8, wide)),
            shape((rows, heads * DV)),
            shape((rows, DK)),
            shape((chunks, heads, TILE, TILE)),
            shape((chunks, heads, DK, DK)),
            shape((chunks, heads, DK, DK + DV)),
            shape((rows, heads * DK)),
            shape((rows, heads * DV)),
            shape((rows, heads * DK)),
            shape((heads, DK, DK + DV), BF16),
        ],
        scratch_shapes=[
            pltpu.VMEM((8 + FWD_SPAN, wide), F32),
            pltpu.VMEM((heads, DK, DK + DV), F32),
        ],
        compiler_params=params(60),
        cost_estimate=cost(36),
        name="mixer_forward",
    )(marks, who, *tokens, *tokens, gain, w_mixer, w_rates, bias, alpha, conv)


def branch_kernel(heads, pieces, place, who, maps, own, far, gate, gain, w_out, *refs):
    attn_out, normed_out, start_out, *refs, start = refs[-4 - 2 * pieces :]
    mine, other = refs[:pieces], refs[pieces:]
    step = pl.program_id(0)

    @pl.when(step == 0)
    def _():
        start[...] = jnp.zeros_like(start)

        def join(j, carry):
            at = j ^ place[0]
            for h in range(heads):
                start[h] = (
                    mm(maps[at, h, :, DV:].astype(F32), start[h], NN, P_STATE)
                    + maps[at, h, :, :DV].astype(F32)
                )
            return carry

        lax.fori_loop(0, place[0], join, 0)
        start_out[...] = start[...]

    for h in range(heads):
        col = slice(h * DV, (h + 1) * DV)
        attn = own[:, col] + mm(far[:, col], start[h], NN, P_STATE)
        attn_out[:, col] = attn
        gates = gate[:, col]
        normed = attn * rms_scale(attn) * gain[...] * (gates * jax.nn.sigmoid(gates))
        normed_out[:, col] = normed.astype(BF16)
    branch = jnp.dot(normed_out[...], w_out[...], preferred_element_type=F32).astype(BF16)
    keep_half(step, who[0], branch, mine, other)


def keep_half(step, me, value, mine, other):
    for p in range(len(mine)):
        for half in range(2):

            @pl.when(step == 2 * p + half)
            def _():
                @pl.when(lax.rem(me, 2) == half)
                def _():
                    mine[p][...] = value

                @pl.when(lax.rem(me, 2) != half)
                def _():
                    other[p][...] = value


def pick_half(step, me, mine, other, out):
    for p in range(len(mine)):
        for half in range(2):

            @pl.when(step == 2 * p + half)
            def _():
                @pl.when(lax.rem(me, 2) == half)
                def _():
                    out[...] = mine[p][...].astype(F32)

                @pl.when(lax.rem(me, 2) != half)
                def _():
                    out[...] = other[p][...].astype(F32)


def branch_forward(heads, place, who, maps, own, far, gate, gain, w_out, waits):
    rows, model = own.shape[0], w_out.shape[1]
    wide = heads * DV
    pieces = rows // (2 * ROWS)
    row = lambda width: block((ROWS, width), lambda i: (i, 0))
    return pl.pallas_call(
        functools.partial(branch_kernel, heads, pieces),
        grid=(rows // ROWS,),
        in_specs=[
            SCALARS, SCALARS, once(maps.shape), row(wide), row(wide), row(wide), fixed(gain.shape), once(w_out.shape),
        ]
        + [WHOLE] * len(waits),
        out_specs=[row(wide), row(wide), fixed((heads, DK, DV))]
        + [fixed((ROWS, model))] * (2 * pieces),
        out_shape=[shape((rows, wide)), shape((rows, wide), BF16), shape((heads, DK, DV))]
        + [shape((ROWS, model), BF16)] * (2 * pieces),
        scratch_shapes=[pltpu.VMEM((heads, DK, DV), F32)],
        compiler_params=params(14),
        cost_estimate=cost(3),
        name="branch_forward",
    )(place, who, maps, own, far, gate, gain, w_out, *waits)


def share_places(count):
    order, bit = [0], count // 2
    for bit in [1 << k for k in range(count.bit_length() - 1)][::-1]:
        order = order + [m | bit for m in order]
    return order


def keep_shares(step, value, me, kept, sent):
    count = 2 * kept.shape[0]
    width = value.shape[1] // count
    parts = in_order([value[:, m * width : (m + 1) * width] for m in range(count)], me)
    rows = pl.ds(pl.multiple_of(step * ROWS, ROWS), ROWS)
    for position, m in enumerate(share_places(count)):
        if position < count // 2:
            kept[position, rows] = parts[m]
        else:
            sent[position - count // 2, rows] = parts[m]


def ffn_kernel(count, filled, who, x, mine, other, *refs):
    grads, refs = refs[:count], refs[count:]
    gain, w_gate, w_up, w_down = refs[:4]
    (
        h_out, act_out, gg_out, gu_out, grad_out, kept, sent, dh_mine, dh_other, picked,
    ) = refs[4 + filled :]
    step = pl.program_id(0)
    pick_half(step, who[0], [mine], [other], picked)
    resid = x[...].astype(F32) + picked[...]
    h_two = (resid * rms_scale(resid) * gain[...]).astype(BF16)
    h_out[...] = h_two
    grad = jnp.concatenate(in_order([g[...] for g in grads], who[0]), axis=1)
    grad_out[...] = grad
    gate = mm(h_two, w_gate[...], NT)
    up = mm(h_two, w_up[...], NT)
    sig = jax.nn.sigmoid(gate)
    silu = gate * sig
    act = (silu * up).astype(BF16)
    act_out[...] = act
    grad_act = mm(grad, w_down[...], NT)
    grad_gate = (grad_act * up * sig * (1.0 + gate * (1.0 - sig))).astype(BF16)
    grad_up = (grad_act * silu).astype(BF16)
    gg_out[...] = grad_gate
    gu_out[...] = grad_up
    dh = (mm(grad_gate, w_gate[...]) + mm(grad_up, w_up[...])).astype(BF16)
    keep_half(step, who[0], dh, [dh_mine], [dh_other])
    keep_shares(step, mm(act, w_down[...]).astype(BF16), who[0], kept, sent)


def ffn_pass(piece, who, x_all, mine, other, grads, gain, w_gate, w_up, w_down, filled):
    rows, model = x_all.shape
    share, count = grads[0].shape[1], len(grads)
    hidden = w_gate.shape[0]
    row = lambda width: block((ROWS, width), lambda i: (2 * piece + i, 0))
    half = fixed((ROWS, model))
    shares = block((count // 2, 2 * ROWS, share), lambda i: (0, piece, 0))
    first = 8 + count
    return pl.pallas_call(
        functools.partial(ffn_kernel, count, len(filled)),
        grid=(2,),
        in_specs=[SCALARS, row(model), half, half]
        + [row(share)] * count
        + [fixed(gain.shape), once(w_gate.shape), once(w_up.shape), once(w_down.shape)]
        + [WHOLE] * len(filled),
        out_specs=[row(model), row(hidden), row(hidden), row(hidden), row(model)]
        + [shares] * 2
        + [half] * 2,
        out_shape=[
            shape((rows, model), BF16),
            shape((rows, hidden), BF16),
            shape((rows, hidden), BF16),
            shape((rows, hidden), BF16),
            shape((rows, model), BF16),
        ]
        + [shape((count // 2, rows, share), BF16)] * 2
        + [shape((ROWS, model), BF16)] * 2,
        scratch_shapes=[pltpu.VMEM((ROWS, model), F32)],
        input_output_aliases={first + k: k for k in range(len(filled))},
        compiler_params=params(32),
        cost_estimate=cost(10),
        name="ffn_pass",
    )(who, x_all, mine, other, *grads, gain, w_gate, w_up, w_down, *filled)


def fold(value):
    return jnp.sum(value.reshape(value.shape[0] // 8, 8, value.shape[1]), axis=0)


def resid_kernel(
    heads, pieces, who, x, *refs
):
    take = lambda k: refs[k * pieces : (k + 1) * pieces]
    branch_mine, branch_other, dh_mine, dh_other = take(0), take(1), take(2), take(3)
    (
        grad, gain, w_out, normed, attn, gate, out_gain, far,
        weight_out, attn_grad_out, gate_grad_out, resid_out,
        gain_grad_out, out_gain_grad_out, state_grad_out, resid_all, weight_sum, dh,
    ) = refs[4 * pieces :]
    step = pl.program_id(0)
    pick_half(step, who[0], branch_mine, branch_other, resid_all)
    pick_half(step, who[0], dh_mine, dh_other, dh)

    @pl.when(pl.program_id(0) == 0)
    def _():
        for total in (gain_grad_out, out_gain_grad_out, state_grad_out, weight_sum):
            total[...] = jnp.zeros_like(total)

    resid = x[...].astype(F32) + resid_all[...]
    scale = rms_scale(resid)
    unit = resid * scale
    grad_h = dh[...]
    gain_grad_out[...] += fold(grad_h * unit)
    lifted = grad_h * gain[...]
    grad_resid = grad[...].astype(F32) + scale * (
        lifted - unit * jnp.mean(lifted * unit, axis=-1, keepdims=True)
    )
    resid_all[...] = grad_resid
    share = resid_out.shape[1]
    resid_out[...] = resid_all[:, pl.ds(pl.multiple_of(who[0] * share, share), share)]
    grad_branch = grad_resid.astype(BF16)
    weight_sum[...] += mm(normed[...], grad_branch, TN)

    @pl.when(pl.program_id(0) == pl.num_programs(0) - 1)
    def _():
        weight_out[...] = weight_sum[...].astype(BF16)

    grad_normed = mm(grad_branch, w_out[...], NT)
    for h in range(heads):
        col = slice(h * DV, (h + 1) * DV)
        value, gates, back = attn[:, col], gate[:, col], grad_normed[:, col]
        scale_o = rms_scale(value)
        unit_o = value * scale_o
        sig = jax.nn.sigmoid(gates)
        silu = gates * sig
        gate_grad_out[:, col] = (
            back * unit_o * out_gain[...] * sig * (1.0 + gates * (1.0 - sig))
        ).astype(BF16)
        scaled = back * silu
        out_gain_grad_out[...] += fold(scaled * unit_o)
        lifted_o = scaled * out_gain[...]
        grad_attn = scale_o * (
            lifted_o - unit_o * jnp.mean(lifted_o * unit_o, axis=-1, keepdims=True)
        )
        attn_grad_out[:, col] = grad_attn
        state_grad_out[h] += mm(far[:, col], grad_attn, TN, P_STATE)


def resid_backward(heads, who, share, x_all, branch, dh, grad, gain, w_out, normed, attn, gate, out_gain, far):
    rows, model = x_all.shape
    wide = heads * DV
    row = lambda width: block((ROWS, width), lambda i: (i, 0))
    pieces = rows // (2 * ROWS)
    halves = [fixed((ROWS, model))] * (4 * pieces)
    return pl.pallas_call(
        functools.partial(resid_kernel, heads, pieces),
        grid=(rows // ROWS,),
        in_specs=[
            SCALARS, row(model), *halves, row(model), fixed(gain.shape), once(w_out.shape),
            row(wide), row(wide), row(wide), fixed(out_gain.shape), row(wide),
        ],
        out_specs=[fixed(w_out.shape), row(wide), row(wide), row(share)]
        + [fixed((8, model)), fixed((8, DV)), fixed((heads, DK, DV))],
        out_shape=[
            shape(w_out.shape, BF16),
            shape((rows, wide)),
            shape((rows, wide), BF16),
            shape((rows, share)),
            shape((8, model)),
            shape((8, DV)),
            shape((heads, DK, DV)),
        ],
        scratch_shapes=[
            pltpu.VMEM((ROWS, model), F32),
            pltpu.VMEM(w_out.shape, F32),
            pltpu.VMEM((ROWS, model), F32),
        ],
        compiler_params=params(60),
        cost_estimate=cost(9),
        name="resid_backward",
    )(
        who, x_all, *[b[0] for b in branch], *[b[1] for b in branch], *[d[0] for d in dh], *[d[1] for d in dh],
        grad, gain, w_out, normed, attn, gate, out_gain, far,
    )


def mixer_back_kernel(
    heads, ends, steps, marks, place, maps, state_grads, start, raw, raw_before, rim, conv, logits, alpha,
    inv, transfers, states, reads, attn_grad, gate_grad,
    grad_raw_out, tail_out, rim_out, sums_out, conv_out,
    ext, mixed_grad, carry,
):
    step = pl.program_id(0)
    at_step = steps - 1 - step
    span_start = marks[0] + at_step * BWD_SPAN
    wide = heads * QKV
    per = BWD_SPAN // CHUNK

    @pl.when(step == 0)
    def _():
        carry[...] = jnp.zeros_like(carry)
        count = maps.shape[0]

        def join(k, unused):
            at = (count - 1 - k) ^ place[0]
            for h in range(heads):
                carry[h] = (
                    mm(maps[at, h, :, DV:].astype(F32), carry[h], TN, P_STATE)
                    + state_grads[at, h].astype(F32)
                )
            return unused

        lax.fori_loop(0, count - 1 - place[0], join, 0)
        mixed_grad[0:8] = jnp.zeros((8, wide), F32)
        mixed_grad[8 + BWD_SPAN :] = jnp.zeros((8, wide), F32)
        sums_out[...] = jnp.zeros_like(sums_out)
        conv_out[...] = jnp.zeros_like(conv_out)

    @pl.when(step > 0)
    def _():
        mixed_grad[8 + BWD_SPAN :] = mixed_grad[8:16]

    @pl.when(at_step == 0)
    def _():
        ext[0:8] = rim[...]

    @pl.when(at_step > 0)
    def _():
        ext[0:8] = raw_before[...]

    ext[8 : 8 + BWD_SPAN] = raw[...]
    masks = conv_masks(span_start, marks, ends, BWD_SPAN, -1)
    apart, strict = token_masks()
    logit = logits[...]
    betas = jax.nn.sigmoid(logit)
    gates, sums, rows = gate_tiles(logit, alpha[...])

    parts = {}
    for h in range(heads):
        mixed = [convolved(ext, conv, masks, h, part) for part in range(5)]
        active = [m * jax.nn.sigmoid(m) for m in mixed]
        unit, scale = zip(*[unit_rows(active[part]) for part in range(3)])
        beta = [spread_column(betas, 3 * h + i) for i in range(NH)]
        parts[h] = (mixed, unit, scale, active[3:], beta)

    units = [(h, c) for h in range(heads) for c in range(per)]
    befores, grads_after = {}, {}
    for h in range(heads):
        for c in reversed(range(per)):
            at, col = slice(c * CHUNK, (c + 1) * CHUNK), slice(h * DK, (h + 1) * DK)
            befores[h, c] = states[c, h, :, :DV] + mm(
                states[c, h, :, DV:], start[h], NN, P_STATE
            )
        for c in reversed(range(per)):
            at, col = slice(c * CHUNK, (c + 1) * CHUNK), slice(h * DK, (h + 1) * DK)
            grads_after[h, c] = carry[h]
            carry[h] = mm(reads[at, col], attn_grad[at, col], TN, P_STATE) + mm(
                transfers[c, h], carry[h], TN, P_STATE
            )

    work = {}
    for h, c in units:
        _, unit, _, values, beta = parts[h]
        keys = pair(unit[1], unit[2], c)
        value = pair(values[0], values[1], c)
        beta_c = pair(beta[0], beta[1], c)
        query = unit[0][c * CHUNK : (c + 1) * CHUNK]
        decay, opening, closing, chunk_whole = chunk_gates(
            span_start, marks, ends, sums, rows, h, c
        )
        decay_two = jnp.concatenate([decay, decay], axis=0)
        opening_two = jnp.concatenate([opening, opening], axis=0)
        closing_two = jnp.concatenate([closing, closing], axis=0)
        grown = jnp.where(strict, decay_two * mm(keys, keys, NT, P_BWD), 0.0)
        read = decay * mm(query, keys, NT, P_BWD)
        recalled = opening_two * mm(keys, befores[h, c], NN, P_SOLVE)
        missing = value - recalled
        deltas = mm(inv[c, h], beta_c * missing, NN, P_SOLVE)
        at, col = slice(c * CHUNK, (c + 1) * CHUNK), slice(h * DK, (h + 1) * DK)
        out_grad = attn_grad[at, col]
        grad_deltas = mm(read, out_grad, TN, P_SOLVE) + mm(
            closing_two * keys, grads_after[h, c], NN, P_SOLVE
        )
        work[h, c] = [
            keys, query, beta_c, decay, decay_two, opening, opening_two, closing_two,
            grown, missing, deltas, out_grad, grad_deltas, chunk_whole,
        ]
    columns = {}
    for h, c in units:
        (
            keys, query, beta, decay, decay_two, opening, opening_two, closing_two,
            grown, missing, deltas, out_grad, grad_deltas, chunk_whole,
        ) = work[h, c]
        grad_target = mm(inv[c, h], grad_deltas, TN, P_SOLVE)
        grad_lower = jnp.where(strict, -mm(grad_target, deltas, NT, P_PAIR), 0.0)
        grad_beta = jnp.sum(grad_lower * grown, axis=-1, keepdims=True) + jnp.sum(
            grad_target * missing, axis=-1, keepdims=True
        )
        grad_pairs = grad_lower * beta * decay_two
        grad_value = beta * grad_target
        grad_read = decay * mm(out_grad, deltas, NT, P_PAIR)
        left = mm(grad_pairs, keys, NN, P_BWD) - beta * opening_two * mm(
            grad_target, befores[h, c], NT, P_BWD
        )
        closed = closing_two * mm(deltas, grads_after[h, c], NT, P_BWD)
        right = mm(grad_pairs, keys, TN, P_BWD) + closed + mm(grad_read, query, TN, P_BWD)
        grad_query = mm(grad_read, keys, NN, P_BWD) + opening * mm(
            out_grad, befores[h, c], NT, P_BWD
        )
        in_left = jnp.sum(keys * left, axis=-1, keepdims=True)
        in_right = jnp.sum(keys * right, axis=-1, keepdims=True)
        in_query = jnp.sum(query * grad_query, axis=-1, keepdims=True)
        spare = in_left - in_right
        grad_total = spare[:CHUNK] + spare[CHUNK:] + in_query
        whole = jnp.sum(keys * closed) + jnp.sum(
            chunk_whole * jnp.sum(grads_after[h, c] * befores[h, c], axis=0, keepdims=True)
        )
        last_row = iota((CHUNK, 1), 0) == CHUNK - 1
        grad_total = grad_total + jnp.where(last_row, whole, 0.0)
        columns[h, c] = (
            grad_query - query * in_query,
            left + right - keys * (in_left + in_right),
            grad_value,
            grad_beta,
            grad_total,
        )

    lane = iota((BWD_SPAN, DK), 1)
    rates = jnp.zeros((BWD_SPAN, DK), F32)
    for h in range(heads):
        mixed, unit, scale, values, beta = parts[h]
        got = [columns[h, c] for c in range(per)]
        low, high = slice(0, CHUNK), slice(CHUNK, 2 * CHUNK)
        stack = lambda index, part: jnp.concatenate([g[index][part] for g in got], axis=0)
        act_grads = [
            scale[0] * stack(0, low),
            scale[1] * stack(1, low),
            scale[2] * stack(1, high),
            stack(2, low),
            stack(2, high),
        ]
        for i, column in enumerate((stack(3, low), stack(3, high), stack(4, low))):
            rates = rates + jnp.where(lane == 3 * h + i, column, 0.0)
        for part in range(5):
            cols = part_columns(h, part)
            sig = jax.nn.sigmoid(mixed[part])
            grad = act_grads[part] * sig * (1.0 + mixed[part] * (1.0 - sig))
            mixed_grad[8 : 8 + BWD_SPAN, cols] = grad
            conv_out[24:32, cols] += fold(grad * ext[8 : 8 + BWD_SPAN, cols])
            for s in range(1, CONV):
                moved = jnp.where(masks[s], ext[8 - s : 8 - s + BWD_SPAN, cols], 0.0)
                tap = CONV - 1 - s
                conv_out[8 * tap : 8 * tap + 8, cols] += fold(grad * moved)

    ahead = conv_masks(span_start, marks, ends, BWD_SPAN, 1)
    for h in range(heads):
        for part in range(5):
            cols = part_columns(h, part)
            grad = mixed_grad[8 : 8 + BWD_SPAN, cols] * conv[CONV - 1 : CONV, cols]
            for s in range(1, CONV):
                moved = jnp.where(ahead[s], mixed_grad[8 + s : 8 + s + BWD_SPAN, cols], 0.0)
                grad = grad + moved * conv[CONV - 1 - s : CONV - s, cols]
            begin = h * MIXW + part * DK
            grad_raw_out[:, begin : begin + DK] = grad.astype(BF16)

            @pl.when(step == 0)
            def _():
                tail_out[:, cols] = grad[BWD_SPAN - HALO :]

        grad_raw_out[:, h * MIXW + QKV : (h + 1) * MIXW] = gate_grad[:, h * DV : (h + 1) * DV]

    @pl.when(at_step == 0)
    def _():
        rim_masks = conv_masks(marks[0] - 8, marks, ends, 8, 1)
        for h in range(heads):
            for part in range(5):
                cols = part_columns(h, part)
                grad = jnp.zeros((8, DK), F32)
                for s in range(1, CONV):
                    moved = jnp.where(rim_masks[s], mixed_grad[s : s + 8, cols], 0.0)
                    grad = grad + moved * conv[CONV - 1 - s : CONV - s, cols]
                rim_out[:, cols] = grad

    back = chunk_sums(True, rates)
    lanes = iota((1, DK), 1)
    is_gate = (lanes % (NH + 1) == NH) & (lanes < heads * (NH + 1))
    grad_logits = jnp.where(is_gate, back * alpha[...] * betas, rates * betas * (1.0 - betas))
    grad_raw_out[:, heads * MIXW :] = grad_logits.astype(BF16)
    sums_out[0:8] += fold(grad_logits)
    sums_out[8:16] += fold(back * gates)


def mixer_backward(
    heads, ends, marks, place, maps, state_grads, start, raw, rim, conv, logits, alpha,
    inv, transfers, states, reads, attn_grad, gate_grad,
):
    rows, wide = raw.shape
    steps, per = rows // BWD_SPAN, BWD_SPAN // CHUNK
    turn = lambda i: steps - 1 - i
    row = lambda width: block((BWD_SPAN, width), lambda i: (turn(i), 0))
    cube = lambda last: block((per, heads, TILE, last), lambda i: (turn(i), 0, 0, 0))
    return pl.pallas_call(
        functools.partial(mixer_back_kernel, heads, ends, steps),
        grid=(steps,),
        in_specs=[
            SCALARS,
            SCALARS,
            once(maps.shape),
            once(state_grads.shape),
            fixed(start.shape),
            row(wide),
            block((8, wide), lambda i: (jnp.maximum(turn(i) * (BWD_SPAN // 8) - 1, 0), 0)),
            fixed(rim.shape),
            fixed(conv.shape),
            row(DK),
            fixed(alpha.shape),
            cube(TILE),
            cube(DK),
            cube(DK + DV),
            row(heads * DK),
            row(heads * DV),
            row(heads * DV),
        ],
        out_specs=[
            row(heads * MIXW + DK),
            fixed((HALO, wide)),
            fixed((8, wide)),
            fixed((16, DK)),
            fixed((8 * CONV, wide)),
        ],
        out_shape=[
            shape((rows, heads * MIXW + DK), BF16),
            shape((HALO, wide)),
            shape((8, wide)),
            shape((16, DK)),
            shape((8 * CONV, wide)),
        ],
        scratch_shapes=[
            pltpu.VMEM((8 + BWD_SPAN, wide), F32),
            pltpu.VMEM((8 + BWD_SPAN + 8, wide), F32),
            pltpu.VMEM((heads, DK, DV), F32),
        ],
        compiler_params=params(60),
        cost_estimate=cost(50),
        name="mixer_backward",
    )(
        marks, place, maps, state_grads, start, raw, raw, rim, conv, logits, alpha,
        inv, transfers, states, reads, attn_grad, gate_grad,
    )


def weights_kernel(widths, orders, place, h_one, halo, grad, rim, out_weights, *outs):
    step, count = pl.program_id(0), pl.num_programs(0)
    total = mm(h_one[...], grad[...], TN) + mm(halo[...], rim[...], TN)
    total = jnp.concatenate([total, jnp.transpose(out_weights[...].astype(F32))], axis=1)
    at = 0
    for k, (width, order) in enumerate(zip(widths, orders)):
        value = total[:, at : at + width].astype(BF16)
        at += width
        position = weight_places(step, order)

        @pl.when(position < count // 2)
        def _():
            outs[2 * k][position] = value

        @pl.when(position >= count // 2)
        def _():
            outs[2 * k + 1][position - count // 2] = value


def weight_places(i, bits_in_order):
    position = 0
    for bit in bits_in_order:
        position = 2 * position + lax.rem(i // bit, 2)
    return position


def mixer_weights(place, ranges, h_one, halo, grad, rim, out_weights, widths, orders):
    rows, model = h_one.shape
    deep = model // ranges
    if deep % DK:
        whole = (t_dot(h_one, grad) + t_dot(halo, rim)).astype(BF16)
        whole = jnp.concatenate([whole, out_weights.T], axis=1).reshape(ranges, deep, -1)
        cuts, at = [], 0
        for width, order in zip(widths, orders):
            whole_cut = ordered(whole[:, :, at : at + width], order)
            cuts.append((whole_cut[: ranges // 2], whole_cut[ranges // 2 :]))
            at += width
        return cuts
    outs = pl.pallas_call(
        functools.partial(weights_kernel, widths, orders),
        grid_spec=pltpu.PrefetchScalarGridSpec(
            num_scalar_prefetch=1,
            grid=(ranges,),
            in_specs=[
                block((rows, deep), lambda i, place: (0, i ^ place[0])),
                block((HALO, deep), lambda i, place: (0, i ^ place[0])),
                block(grad.shape, lambda i, place: (0, 0)),
                block(rim.shape, lambda i, place: (0, 0)),
                block((out_weights.shape[0], deep), lambda i, place: (0, i ^ place[0])),
            ],
            out_specs=[
                block((ranges // 2, deep, width), lambda i, place: (0, 0, 0))
                for width in widths
                for _ in range(2)
            ],
        ),
        out_shape=[
            shape((ranges // 2, deep, width), BF16) for width in widths for _ in range(2)
        ],
        compiler_params=params(60),
        cost_estimate=cost(5),
        name="mixer_weights",
    )(place, h_one, halo, grad, rim, out_weights)
    return list(zip(outs[::2], outs[1::2]))


def input_kernel(heads, who, x, gain, grad, w_mixer, w_rates, gain_grad_out, kept, sent):
    step = pl.program_id(0)

    @pl.when(step == 0)
    def _():
        gain_grad_out[...] = jnp.zeros_like(gain_grad_out)
        rows = kept.shape[1] - HALO
        for out in (kept, sent):
            out[:, rows:] = jnp.zeros((out.shape[0], HALO, out.shape[2]), BF16)

    back = mm(grad[:, : heads * MIXW], w_mixer[...], NT) + mm(
        grad[:, heads * MIXW :], w_rates[...], NT
    )
    values = x[...].astype(F32)
    unit = values * rms_scale(values)
    seen = back * unit
    gain_grad_out[...] += fold(seen)
    keep_shares(step, back.astype(BF16), who[0], kept, sent)
    dots = jnp.sum(seen * gain[...], axis=-1, keepdims=True)
    dots = jnp.transpose(jnp.broadcast_to(dots, (ROWS, DK)))[:HALO]
    rows, share = kept.shape[1] - HALO, kept.shape[2]
    per = ROWS // share
    at = iota((HALO, share), 0)
    for k in range(per):
        line = jnp.where(at == step * per + k, dots[:, k * share : (k + 1) * share], 0.0)
        for out in (kept, sent):
            for j in range(out.shape[0]):
                out[j, rows:] = (out[j, rows:].astype(F32) + line).astype(BF16)


def input_backward(heads, count, who, x_all, gain, grad, w_mixer, w_rates):
    rows, model = x_all.shape
    share = model // count
    row = lambda width: block((ROWS, width), lambda i: (i, 0))
    return pl.pallas_call(
        functools.partial(input_kernel, heads),
        grid=(rows // ROWS,),
        in_specs=[
            SCALARS, row(model), fixed(gain.shape), row(grad.shape[1]), once(w_mixer.shape), once(w_rates.shape),
        ],
        out_specs=[fixed((8, model))] + [fixed((count // 2, rows + HALO, share))] * 2,
        out_shape=[shape((8, model))] + [shape((count // 2, rows + HALO, share), BF16)] * 2,
        compiler_params=params(60),
        cost_estimate=cost(6),
        name="input_backward",
    )(who, x_all, gain, grad, w_mixer, w_rates)


def tokens_kernel(model, who, x, gain, resid_grad, own_dots, came_dots, own, came, out):
    share = out.shape[1]
    cols = pl.ds(pl.multiple_of(who[0] * share, share), share)
    scale = rms_scale(x[...].astype(F32))
    unit = x[:, cols].astype(F32) * scale
    dots = own_dots[...].astype(F32) + came_dots[...].astype(F32)
    per = ROWS // share
    at = iota((HALO, share), 0)
    line = jnp.concatenate(
        [
            jnp.sum(jnp.where(at == pl.program_id(0) * per + k, dots, 0.0), axis=0, keepdims=True)
            for k in range(per)
        ],
        axis=1,
    )
    mean = jnp.transpose(jnp.broadcast_to(line, (8, ROWS)))[:, :1] / model
    back = (own[...].astype(F32) + came[...].astype(F32)) * gain[:, cols]
    out[...] = (resid_grad[...] + scale * (back - unit * mean)).astype(BF16)


def tokens_backward(who, x_all, gain, resid_grad, own, came):
    rows, model = x_all.shape
    share = own.shape[1]
    row = lambda width: block((ROWS, width), lambda i: (i, 0))
    extra = block((HALO, share), lambda i: (rows // HALO, 0))
    return pl.pallas_call(
        functools.partial(tokens_kernel, model),
        grid=(rows // ROWS,),
        in_specs=[
            SCALARS, row(model), fixed(gain.shape), row(share), extra, extra, row(share), row(share),
        ],
        out_specs=row(share),
        out_shape=shape((rows, share), BF16),
        compiler_params=params(10),
        cost_estimate=cost(2),
        name="tokens_backward",
    )(who, x_all, gain, resid_grad, own, came, own, came)


def shifted(value, axis, steps):
    count = lax.axis_size(axis)
    first, last = (max(0, -steps), min(count, count - steps))
    return lax.ppermute(value, axis, [(source, source + steps) for source in range(first, last)])


def swap(value, axis, mask):
    return lax.ppermute(value, axis, [(i, i ^ mask) for i in range(lax.axis_size(axis))])


def bits(axis):
    count, bit = lax.axis_size(axis), 1
    while bit < count:
        yield bit
        bit *= 2


def spread(value, axis, order, beside=()):
    found = {0: value}
    for at, bit in enumerate(order):
        came = {m | bit: swap(v, axis, bit) for m, v in list(found.items())}
        if at == 0 and beside:
            came[bit], *beside = tie(came[bit], *beside)
        found.update(came)
    return [found[m] for m in range(len(found))], beside


def spread_seq(value):
    found = {0: value}
    count = lax.axis_size("seq")
    for m in range(2, count, 2):
        found[m] = swap(value, "seq", m)
    for m in range(0, count, 2):
        found[m + 1] = swap(found[m], "seq", 1)
    return jnp.stack([found[m] for m in range(count)])


def tie(*values):
    return lax.optimization_barrier(values)


def core_sum(mine, other):
    return mine + swap(other, "head", 1)


def over_y(total, came):
    total = total + came
    for bit in bits("head"):
        if bit > 2:
            total = total + swap(total, "head", bit)
    return total, swap(total, "head", 1)


def summed_shares(kept, sent):
    for bit in bits("head"):
        came = swap(sent, "head", bit)
        half = kept.shape[0] // 2
        if half:
            sent = kept[half:] + came[half:]
            kept = kept[:half] + came[:half]
    return kept[0], came[0]


def summed(value, axis):
    for bit in bits(axis):
        value = value + swap(value, axis, bit)
    return value


def spread_small(value):
    found = [value] + [swap(value, "seq", m) for m in range(2, lax.axis_size("seq"), 2)]
    here = jnp.stack(found)
    there = swap(here, "seq", 1)
    return jnp.stack([here, there], axis=1).reshape((-1,) + value.shape)


def ordered(value, order):
    place = lax.axis_index("seq")
    positions = [0]
    for bit in order[::-1]:
        positions = positions + [m | bit for m in positions]
    return jnp.take(value, jnp.array(positions) ^ place, axis=0)


def first_exchange(cuts, orders):
    came = []
    for (_, sent), order in zip(cuts, orders):
        if came:
            at = -1 if order[0] == orders[0][0] else 0
            came[at], sent = tie(came[at], sent)
        came.append(swap(sent, "seq", order[0]))
    return came


def scattered(cuts, came, orders):
    kept = [k for k, _ in cuts]
    for stage in range(len(orders[0])):
        if stage:
            came = [swap(value, "seq", order[stage]) for value, order in zip(sent, orders)]
        half = kept[0].shape[0] // 2
        sent = [k[half:] + c[half:] for k, c in zip(kept, came)]
        kept = [k[: max(half, 1)] + c[: max(half, 1)] for k, c in zip(kept, came)]
    return [k[0] for k in kept]


def t_dot(leading, trailing):
    return lax.dot_general(leading, trailing, TN, preferred_element_type=F32)


def local(
    tokens, lengths, norm1_gain, w_mixer, w_rates, decay_log, rates_bias, conv_weight,
    out_gain, w_out, norm2_gain, w_ffn_gate, w_ffn_up, w_ffn_down, out_grad,
):
    rows, share = tokens.shape
    heads = decay_log.shape[0]
    ends = lengths.shape[0]
    model = norm1_gain.shape[0]
    group, ranges = lax.axis_size("head"), lax.axis_size("seq")
    place, member = lax.axis_index("seq"), lax.axis_index("head")
    marks = jnp.concatenate(
        [jnp.reshape(place * rows, (1,)), jnp.cumsum(lengths)]
    ).astype(jnp.int32)
    place_arg = jnp.reshape(place, (1,)).astype(jnp.int32)
    who = jnp.reshape(member, (1,)).astype(jnp.int32)
    down_bits = list(bits("head"))[::-1]
    seq_bits = list(bits("seq"))

    halo = shifted(tokens[rows - HALO :], "seq", 1)
    gain_one, gain_two = norm1_gain[None, :], norm2_gain[None, :]
    gain_out = out_gain[None, :]
    spare = DK - heads * (NH + 1)
    rates_w = jnp.pad(w_rates, ((0, 0), (0, spare)))
    bias = jnp.pad(rates_bias, (0, spare))[None, :]
    none = jnp.zeros((heads,), F32)
    alpha = jnp.stack([none] * NH + [-jnp.exp(decay_log)], axis=-1).reshape(-1)
    alpha = jnp.pad(alpha, (0, spare))[None, :]

    token_parts, (marks, rates_w, bias, alpha) = spread(
        jnp.concatenate([tokens, halo], axis=0), "head", down_bits, (marks, rates_w, bias, alpha)
    )
    (
        x_all, h_one, h_halo, raw, rim, gate_o, logits, inv, transfers, states, reads, own, far, end_state,
    ) = mixer_forward(
        heads, ends, marks, who, token_parts, gain_one, w_mixer, rates_w, bias, alpha, conv_weight
    )
    out_grad, end_state = tie(out_grad, end_state)
    grad_parts, _ = spread(out_grad, "head", down_bits)
    maps = spread_seq(end_state)
    attn, normed, start, *branch = branch_forward(
        heads, place_arg, who, maps, own, far, gate_o, gain_out, w_out, grad_parts
    )
    pieces = len(branch) // 2
    halves = [core_sum(branch[p], branch[pieces + p]) for p in range(pieces)]
    sent_y = [swap(halves[0], "head", 2)]
    for p in range(1, pieces):
        sent_y[-1], halves[p] = tie(sent_y[-1], halves[p])
        sent_y.append(swap(halves[p], "head", 2))
    branch, dh_halves, dh, filled = [], [], [], []
    gate_t, up_t = w_ffn_gate.T, w_ffn_up.T
    for p in range(pieces):
        if p:
            sent_y[p], *filled = tie(sent_y[p], *filled)
        branch.append(over_y(halves[p], sent_y[p]))
        *filled, dh_mine, dh_other = ffn_pass(
            p, who, x_all, *branch[p], grad_parts, gain_two, gate_t, up_t, w_ffn_down, filled
        )
        if p:
            dh_y, dh_other = tie(dh_y, dh_other)
            dh.append(over_y(dh_halves[p - 1], dh_y))
        dh_halves.append(core_sum(dh_mine, dh_other))
        dh_y = swap(dh_halves[p], "head", 2)
    h_two, act, grad_gate, grad_up, grad_full, kept, sent = filled
    dh_halves[-1], act, grad_gate, grad_up = tie(dh_halves[-1], act, grad_gate, grad_up)
    by_owner = lambda value: jnp.swapaxes(
        value.reshape(value.shape[0], ranges, model // ranges), 0, 1
    ).astype(BF16)
    ffn_grads = jnp.concatenate(
        [by_owner(t_dot(act, grad_full)), by_owner(t_dot(grad_gate, h_two)), by_owner(t_dot(grad_up, h_two))],
        axis=1,
    )
    dh_y, ffn_grads = tie(dh_y, ffn_grads)
    ffn_grads = lax.psum_scatter(ffn_grads, "seq", scatter_dimension=0, tiled=False)
    dh.append(over_y(dh_halves[-1], dh_y))
    hidden = act.shape[1]
    (
        out_weights, grad_attn, grad_gate_o, resid_own, gain_two_part, out_gain_part, state_grad,
    ) = resid_backward(
        heads, who, share, x_all, branch, dh, grad_full, gain_two, w_out, normed, attn, gate_o, gain_out, far
    )

    sent, state_grad = tie(sent, state_grad)
    state_grads = spread_small(state_grad.astype(BF16))
    grad_raw, tail, rim_grad, sums, conv_parts = mixer_backward(
        heads, ends, marks, place_arg, maps, state_grads, start, raw, rim, conv_weight, logits, alpha,
        inv, transfers, states, reads, grad_attn, grad_gate_o,
    )
    rim_wide = jnp.pad(rim_grad, ((HALO - 8, 0), (0, 0))).astype(BF16)
    none = jnp.zeros((HALO, MIXW - QKV), BF16)
    rim_wide = jnp.concatenate(
        [b for h in range(heads) for b in (rim_wide[:, h * QKV : (h + 1) * QKV], none)]
        + [jnp.zeros((HALO, DK), BF16)],
        axis=1,
    )
    cut_widths = [MIXW] * (heads - 1) + [512, 256, DK + heads * DV]
    orders = [seq_bits] * (heads + 1) + [seq_bits[1:] + seq_bits[:1]]
    cuts = mixer_weights(
        place_arg, ranges, h_one, h_halo, grad_raw, rim_wide, out_weights, cut_widths, orders
    )
    cuts, ffn_grads, conv_parts, sums, rim_grad, kept = tie(
        cuts, ffn_grads, conv_parts, sums, rim_grad, kept
    )
    grad_down, grad_wgate, grad_wup = (
        ffn_grads[k * hidden : (k + 1) * hidden].astype(F32) for k in range(3)
    )
    came = first_exchange(cuts, orders)
    came[0], grad_raw = tie(came[0], grad_raw)
    first, second = summed_shares(kept, sent)
    own_cols = lambda value: lax.dynamic_slice_in_dim(value, member * share, share, 1)
    even = member % 2 == 0
    branch_own = []
    for mine, other in branch:
        mine, other = own_cols(mine), own_cols(other)
        branch_own += [jnp.where(even, mine, other), jnp.where(even, other, mine)]
    output = (
        tokens.astype(F32)
        + jnp.concatenate(branch_own, axis=0).astype(F32)
        + (first.astype(F32) + second.astype(F32))
    ).astype(BF16)
    tail = tail.at[HALO - 8 :].add(shifted(rim_grad, "seq", -1))
    for h in range(heads):
        grad_raw = lax.dynamic_update_slice(
            grad_raw, tail[:, h * QKV : (h + 1) * QKV].astype(BF16), (rows - HALO, h * MIXW)
        )
    gain_one_part, back_kept, back_sent = input_backward(
        heads, group, who, x_all, gain_one, grad_raw, w_mixer, rates_w
    )
    back_own, back_came = summed_shares(back_kept, back_sent)
    sum_rows = jnp.sum(sums.reshape(2, 8, DK), axis=1)
    small = jnp.concatenate(
        [
            jnp.sum(gain_one_part, axis=0),
            jnp.sum(out_gain_part, axis=0),
            jnp.sum(gain_two_part, axis=0),
            sum_rows[0],
            sum_rows[1],
            jnp.sum(conv_parts.reshape(CONV, 8, heads * QKV), axis=1).reshape(-1),
        ]
    )
    small = small.reshape(-1, DK)
    came[-2], small, back_own = tie(came[-2], small, back_own)
    cuts = scattered(cuts, came, orders)
    tokens_grad = tokens_backward(who, x_all, gain_one, resid_own, back_own, back_came)
    grad_wmixer = jnp.concatenate(cuts[:-1], axis=1).astype(F32)
    grad_wrates = cuts[-1][:, : heads * (NH + 1)].astype(F32)
    grad_wout = cuts[-1][:, DK:].T.astype(F32)

    small = summed(small, "seq").reshape(-1)
    cut = [model, DV, model, DK, DK]
    pieces_of, at = [], 0
    for size in cut:
        pieces_of.append(small[at : at + size])
        at += size
    over_head = summed(small[: model + DV], "head")
    grad_norm1, grad_outgain = over_head[:model], over_head[model:]
    _, _, grad_norm2, bias_row, decay_row = pieces_of
    grad_conv = small[at:].reshape(CONV, heads * QKV)
    grad_bias = bias_row[: heads * (NH + 1)]
    grad_decay = decay_row[: heads * (NH + 1)].reshape(heads, NH + 1)[:, NH]
    return (
        output, tokens_grad, grad_norm1, grad_wmixer, grad_wrates, grad_decay, grad_bias, grad_conv,
        grad_outgain, grad_wout, grad_norm2, grad_wgate.T, grad_wup.T, grad_down,
    )


def solution(mesh):
    placed = (
        P("seq", "head"), P(), P(), P(None, "head"), P(None, "head"), P("head"), P("head"), P(None, "head"),
        P(), P("head", None), P(), P(None, "head"), P(None, "head"), P("head", None), P("seq", "head"),
    )
    return jax.shard_map(
        local,
        mesh=mesh,
        in_specs=placed,
        out_specs=(
            P("seq", "head"), P("seq", "head"), P(), P("seq", "head"), P("seq", "head"), P("head"), P("head"),
            P(None, "head"), P(), P("head", "seq"), P(), P("seq", "head"), P("seq", "head"), P("head", "seq"),
        ),
        check_vma=False,
    )
```

```python
import functools

import jax
import jax.numpy as jnp
from jax import lax
from jax.experimental import pallas as pl
from jax.experimental.pallas import tpu as pltpu
from jax.sharding import PartitionSpec as P

DK = 128
DV = 128
NH = 2
CONV = 4
QKV = 640
MIXW = 768
EPS = 1e-06

CHUNK = 64
TILE = 2 * CHUNK
FWD_SPAN = 256
BWD_SPAN = 128
ROWS = 256
LEVELS = 6
HALO = 16

F32 = jnp.float32
BF16 = jnp.bfloat16

NN = (((1,), (0,)), ((), ()))
NT = (((1,), (1,)), ((), ()))
TN = (((0,), (0,)), ((), ()))

P_INV = 1
P_FWD = 3
P_STATE = 3
P_BWD = 1
P_SOLVE = 3
P_PAIR = 3


def halves(value):
    high = value.astype(BF16)
    return high, (value - high.astype(F32)).astype(BF16)


def mm(left, right, dims=NN, passes=1):
    if passes == 1:
        return lax.dot_general(
            left.astype(BF16), right.astype(BF16), dims, preferred_element_type=F32
        )
    if passes == 6:
        return lax.dot_general(
            left, right, dims, precision=lax.Precision.HIGHEST, preferred_element_type=F32
        )
    left_h, left_l = halves(left)
    right_h, right_l = halves(right)
    dot = functools.partial(lax.dot_general, dimension_numbers=dims, preferred_element_type=F32)
    return dot(left_h, right_h) + (dot(left_h, right_l) + dot(left_l, right_h))


def iota(shape, axis):
    return lax.broadcasted_iota(jnp.int32, shape, axis)


def doc_of(place, marks, ends):
    count = jnp.zeros_like(place)
    for j in range(ends):
        count = count + jnp.where(place >= marks[1 + j], 1, 0)
    return jnp.where(place < 0, -1, count)


def doc_scalar(place, marks, ends):
    count = jnp.int32(0)
    for j in range(ends):
        count = count + (place >= marks[1 + j]).astype(jnp.int32)
    return jnp.where(place < 0, -1, count)


def conv_masks(start, marks, ends, rows, direction):
    place = start + iota((rows, DK), 0)
    edge = jnp.zeros_like(place) if direction < 0 else jnp.full_like(place, 2**30)
    for j in range(ends):
        if direction < 0:
            edge = jnp.maximum(edge, jnp.where(place >= marks[1 + j], marks[1 + j], 0))
        else:
            edge = jnp.minimum(edge, jnp.where(place < marks[1 + j], marks[1 + j], 2**30))
    room = place - edge if direction < 0 else edge - 1 - place
    return [None] + [room >= s for s in range(1, CONV)]


def softplus(v):
    return jnp.maximum(v, 0.0) + jnp.log1p(jnp.exp(-jnp.abs(v)))


def chunk_sum_matrix(upper):
    row, col = iota((TILE, TILE), 0), iota((TILE, TILE), 1)
    keep = (col >= row) if upper else (col <= row)
    keep = keep & ((row // CHUNK) == (col // CHUNK))
    return jnp.where(keep, 1.0, 0.0).astype(F32)


def chunk_sums(upper, value):
    matrix = chunk_sum_matrix(upper)
    return jnp.concatenate(
        [mm(matrix, value[at : at + TILE], NN, 6) for at in range(0, value.shape[0], TILE)], axis=0
    )


def part_columns(h, part):
    begin = h * QKV + part * DK
    return slice(begin, begin + DK)


def convolved(ext, conv, masks, h, part):
    cols = part_columns(h, part)
    span = masks[1].shape[0]
    total = ext[8 : 8 + span, cols] * conv[CONV - 1 : CONV, cols]
    for s in range(1, CONV):
        moved = jnp.where(masks[s], ext[8 - s : 8 - s + span, cols], 0.0)
        total = total + moved * conv[CONV - 1 - s : CONV - s, cols]
    return total


def two(array, c):
    piece = array[c * CHUNK : (c + 1) * CHUNK]
    return jnp.concatenate([piece, piece], axis=0)


def pair(first, second, c):
    at = slice(c * CHUNK, (c + 1) * CHUNK)
    return jnp.concatenate([first[at], second[at]], axis=0)


def unit_rows(v):
    scale = lax.rsqrt(jnp.sum(v * v, axis=-1, keepdims=True) + EPS)
    return v * scale, scale


def token_masks():
    row, col = iota((TILE, TILE), 0), iota((TILE, TILE), 1)
    tok_r, tok_c = row % CHUNK, col % CHUNK
    strict = (tok_c < tok_r) | ((tok_c == tok_r) & (row >= CHUNK) & (col < CHUNK))
    return tok_r ^ tok_c, strict


def gate_tiles(logits, alpha):
    gates = alpha * softplus(logits)
    sums = chunk_sums(False, gates)
    rows = []
    for at in range(0, logits.shape[0], TILE):
        flat = jnp.transpose(sums[at : at + TILE])[:8]
        turned = pltpu.roll(flat, CHUNK, 1)
        lane = iota(flat.shape, 1)
        rows.append(jnp.where(lane < CHUNK, flat, turned))
        rows.append(jnp.where(lane < CHUNK, turned, flat))
    return gates, sums, rows


def spread_column(tile, col):
    return jnp.broadcast_to(tile[:, col : col + 1], (tile.shape[0], DK))


def chunk_gates(span_start, marks, ends, sums, rows, h, c):
    start = span_start + c * CHUNK
    col_place = start + iota((CHUNK, TILE), 0)
    row_place = start + iota((1, TILE), 1) % CHUNK
    col_doc = doc_of(col_place, marks, ends)
    row_doc = doc_of(row_place, marks, ends)
    total = spread_column(sums[c * CHUNK : (c + 1) * CHUNK], 3 * h + 2)
    across = rows[c][3 * h + 2 : 3 * h + 3]
    kept = (col_doc == row_doc) & (row_place <= col_place)
    decay = jnp.exp(jnp.where(kept, total - across, -1e30))
    doc_before = doc_scalar(start - 1, marks, ends)
    doc_last = doc_scalar(start + CHUNK - 1, marks, ends)
    last = total[CHUNK - 1 : CHUNK]
    opening = jnp.where(col_doc == doc_before, jnp.exp(total), 0.0)
    closing = jnp.where(col_doc == doc_last, jnp.exp(last - total), 0.0)
    whole = jnp.where(doc_before == doc_last, jnp.exp(last), 0.0)
    return decay, opening, closing, whole


def inverses(lowers, apart):
    eye = jnp.where(iota((TILE, TILE), 0) == iota((TILE, TILE), 1), 1.0, 0.0)
    result = [eye - jnp.where(apart == 0, lower, 0.0) for lower in lowers]
    for level in range(LEVELS):
        here = (apart >> level) == 1
        steps = [
            mm(inverse, jnp.where(here, lower, 0.0), NN, P_INV)
            for inverse, lower in zip(result, lowers)
        ]
        result = [
            inverse - mm(step, inverse, NN, P_INV) for inverse, step in zip(result, steps)
        ]
    return result


def rms_scale(values):
    return lax.rsqrt(jnp.mean(values * values, axis=-1, keepdims=True) + EPS)


def in_order(parts, me):
    bit = 1
    while bit < len(parts):
        flip = (me // bit) % 2 == 1
        parts = [jnp.where(flip, parts[m ^ bit], parts[m]) for m in range(len(parts))]
        bit *= 2
    return parts


def mixer_kernel(heads, ends, count, marks, who, *refs):
    tokens, halos, refs = refs[:count], refs[count : 2 * count], refs[2 * count :]
    (
        gain, w_mixer, w_rates, bias, alpha, conv,
        x_out, h_out, halo_out, raw_out, rim_out, gate_out, logit_out, inv_out, map_out, state_out,
        read_out, own_out, far_out, end_out, ext, state,
    ) = refs
    step = pl.program_id(0)
    joined = lambda parts: jnp.concatenate(in_order([p[...] for p in parts], who[0]), axis=1)
    span_start = marks[0] + step * FWD_SPAN

    def rounded_norm(rows):
        values = rows.astype(F32)
        return (values * rms_scale(values) * gain[...]).astype(BF16)

    @pl.when(step == 0)
    def _():
        halo_out[...] = rounded_norm(joined(halos))
        halo = jnp.dot(halo_out[...], w_mixer[...], preferred_element_type=F32)
        for h in range(heads):
            ext[0:8, h * QKV : (h + 1) * QKV] = halo[HALO - 8 :, h * MIXW : h * MIXW + QKV]
        rim_out[...] = ext[0:8]
        for h in range(heads):
            state[h, :, :DV] = jnp.zeros((DK, DV), F32)
            state[h, :, DV:] = jnp.where(
                iota((DK, DK), 0) == iota((DK, DK), 1), 1.0, 0.0
            ).astype(F32)

    @pl.when(step > 0)
    def _():
        ext[0:8] = ext[FWD_SPAN : FWD_SPAN + 8]

    x = joined(tokens)
    x_out[...] = x
    h_one = rounded_norm(x)
    h_out[...] = h_one
    raw = jnp.dot(h_one, w_mixer[...], preferred_element_type=F32)
    for h in range(heads):
        ext[8 : 8 + FWD_SPAN, h * QKV : (h + 1) * QKV] = raw[:, h * MIXW : h * MIXW + QKV]
        gate_out[:, h * DV : (h + 1) * DV] = raw[:, h * MIXW + QKV : (h + 1) * MIXW]
    raw_out[...] = ext[8 : 8 + FWD_SPAN]
    logits = jnp.dot(h_one, w_rates[...], preferred_element_type=F32) + bias[...]
    logit_out[...] = logits
    masks = conv_masks(span_start, marks, ends, FWD_SPAN, -1)
    apart, strict = token_masks()
    betas = jax.nn.sigmoid(logits)
    _, sums, rows = gate_tiles(logits, alpha[...])

    units = [(h, c) for h in range(heads) for c in range(FWD_SPAN // CHUNK)]
    parts = {}
    for h in range(heads):
        active = []
        for part in range(5):
            mixed = convolved(ext, conv, masks, h, part)
            active.append(mixed * jax.nn.sigmoid(mixed))
        unit = [unit_rows(active[part])[0] for part in range(3)]
        beta = [spread_column(betas, 3 * h + i) for i in range(NH)]
        parts[h] = (unit, active[3:], beta)

    lowers, reads, sides, lasts, wholes, queries = [], [], [], [], [], []
    for h, c in units:
        (query, key_a, key_b), (value_a, value_b), (beta_a, beta_b) = parts[h]
        keys, values, beta = (
            pair(key_a, key_b, c),
            pair(value_a, value_b, c),
            pair(beta_a, beta_b, c),
        )
        query_c = query[c * CHUNK : (c + 1) * CHUNK]
        decay, opening, closing, whole = chunk_gates(
            span_start, marks, ends, sums, rows, h, c
        )
        decay_two = jnp.concatenate([decay, decay], axis=0)
        opening_two = jnp.concatenate([opening, opening], axis=0)
        closing_two = jnp.concatenate([closing, closing], axis=0)
        lowers.append(
            jnp.where(strict, beta * decay_two * mm(keys, keys, NT, P_FWD), 0.0)
        )
        reads.append(decay * mm(query_c, keys, NT, P_FWD))
        sides.append(
            jnp.concatenate([beta * values, beta * opening_two * keys], axis=1)
        )
        lasts.append(closing_two * keys)
        wholes.append(whole)
        queries.append(opening * query_c)
    solved = inverses(lowers, apart)
    pieces = [mm(inverse, side, NN, P_FWD) for inverse, side in zip(solved, sides)]
    maps = [mm(last, piece, TN, P_FWD) for last, piece in zip(lasts, pieces)]
    seen = [mm(read, piece, NN, P_FWD) for read, piece in zip(reads, pieces)]
    diagonal = iota((DK, DK), 0) == iota((DK, DK), 1)
    for index, (h, c) in enumerate(units):
        inv_out[c, h] = solved[index]
        transfer = jnp.where(diagonal, wholes[index], 0.0) - maps[index][:, DV:]
        map_out[c, h] = transfer
        reader = queries[index] - seen[index][:, DV:]
        at, col = slice(c * CHUNK, (c + 1) * CHUNK), slice(h * DK, (h + 1) * DK)
        read_out[at, col] = reader
        before = state[h]
        state_out[c, h] = before
        both = mm(reader, before, NN, P_STATE)
        own_out[at, col] = seen[index][:, :DV] + both[:, :DV]
        far_out[at, col] = both[:, DV:]
        after = mm(transfer, before, NN, P_STATE)
        state[h, :, :DV] = after[:, :DV] + maps[index][:, :DV]
        state[h, :, DV:] = after[:, DV:]
    end_out[...] = state[...].astype(BF16)


def block(shape, index):
    return pl.BlockSpec(shape, index)


def fixed(shape):
    return pl.BlockSpec(shape, lambda i: (0,) * len(shape))


def once(shape):
    return pl.BlockSpec(
        shape, lambda i: (0,) * len(shape), pipeline_mode=pl.Buffered(buffer_count=1)
    )


SCALARS = pl.BlockSpec(memory_space=pltpu.SMEM)


def shape(dims, kind=F32):
    return jax.ShapeDtypeStruct(dims, kind)


def params(megabytes):
    return pltpu.CompilerParams(
        dimension_semantics=("arbitrary",), vmem_limit_bytes=megabytes << 20
    )


def cost(microseconds):
    return pl.CostEstimate(
        flops=int(microseconds * 1.1e8), bytes_accessed=int(microseconds * 1e5), transcendentals=0
    )


WHOLE = pl.BlockSpec(memory_space=pl.ANY)


def mixer_forward(heads, ends, marks, who, tokens, gain, w_mixer, w_rates, bias, alpha, conv):
    rows, share = tokens[0].shape
    rows = rows - HALO
    model = gain.shape[1]
    steps, chunks, per = rows // FWD_SPAN, rows // CHUNK, FWD_SPAN // CHUNK
    wide = heads * QKV
    row = lambda width: block((FWD_SPAN, width), lambda i: (i, 0))
    cube = lambda last: block((per, heads, TILE, last), lambda i: (i, 0, 0, 0))
    return pl.pallas_call(
        functools.partial(mixer_kernel, heads, ends, len(tokens)),
        grid=(steps,),
        in_specs=[SCALARS, SCALARS]
        + [row(share)] * len(tokens)
        + [block((HALO, share), lambda i: (rows // HALO, 0))] * len(tokens)
        + [
            fixed((1, model)),
            once(w_mixer.shape),
            once(w_rates.shape),
            fixed(bias.shape),
            fixed(alpha.shape),
            fixed(conv.shape),
        ],
        out_specs=[
            row(model),
            row(model),
            fixed((HALO, model)),
            row(wide),
            fixed((8, wide)),
            row(heads * DV),
            row(DK),
            cube(TILE),
            cube(DK),
            cube(DK + DV),
            row(heads * DK),
            row(heads * DV),
            row(heads * DK),
            fixed((heads, DK, DK + DV)),
        ],
        out_shape=[
            shape((rows, model), BF16),
            shape((rows, model), BF16),
            shape((HALO, model), BF16),
            shape((rows, wide)),
            shape((8, wide)),
            shape((rows, heads * DV)),
            shape((rows, DK)),
            shape((chunks, heads, TILE, TILE)),
            shape((chunks, heads, DK, DK)),
            shape((chunks, heads, DK, DK + DV)),
            shape((rows, heads * DK)),
            shape((rows, heads * DV)),
            shape((rows, heads * DK)),
            shape((heads, DK, DK + DV), BF16),
        ],
        scratch_shapes=[
            pltpu.VMEM((8 + FWD_SPAN, wide), F32),
            pltpu.VMEM((heads, DK, DK + DV), F32),
        ],
        compiler_params=params(60),
        cost_estimate=cost(36),
        name="mixer_forward",
    )(marks, who, *tokens, *tokens, gain, w_mixer, w_rates, bias, alpha, conv)


def branch_kernel(heads, pieces, place, who, maps, own, far, gate, gain, w_out, *refs):
    attn_out, normed_out, start_out, *refs, start = refs[-4 - 2 * pieces :]
    mine, other = refs[:pieces], refs[pieces:]
    step = pl.program_id(0)

    @pl.when(step == 0)
    def _():
        start[...] = jnp.zeros_like(start)

        def join(j, carry):
            at = j ^ place[0]
            for h in range(heads):
                start[h] = (
                    mm(maps[at, h, :, DV:].astype(F32), start[h], NN, P_STATE)
                    + maps[at, h, :, :DV].astype(F32)
                )
            return carry

        lax.fori_loop(0, place[0], join, 0)
        start_out[...] = start[...]

    for h in range(heads):
        col = slice(h * DV, (h + 1) * DV)
        attn = own[:, col] + mm(far[:, col], start[h], NN, P_STATE)
        attn_out[:, col] = attn
        gates = gate[:, col]
        normed = attn * rms_scale(attn) * gain[...] * (gates * jax.nn.sigmoid(gates))
        normed_out[:, col] = normed.astype(BF16)
    branch = jnp.dot(normed_out[...], w_out[...], preferred_element_type=F32).astype(BF16)
    keep_half(step, who[0], branch, mine, other)


def keep_half(step, me, value, mine, other):
    for p in range(len(mine)):
        for half in range(2):

            @pl.when(step == 2 * p + half)
            def _():
                @pl.when(lax.rem(me, 2) == half)
                def _():
                    mine[p][...] = value

                @pl.when(lax.rem(me, 2) != half)
                def _():
                    other[p][...] = value


def pick_half(step, me, mine, other, out):
    for p in range(len(mine)):
        for half in range(2):

            @pl.when(step == 2 * p + half)
            def _():
                @pl.when(lax.rem(me, 2) == half)
                def _():
                    out[...] = mine[p][...].astype(F32)

                @pl.when(lax.rem(me, 2) != half)
                def _():
                    out[...] = other[p][...].astype(F32)


def branch_forward(heads, place, who, maps, own, far, gate, gain, w_out, waits):
    rows, model = own.shape[0], w_out.shape[1]
    wide = heads * DV
    pieces = rows // (2 * ROWS)
    row = lambda width: block((ROWS, width), lambda i: (i, 0))
    return pl.pallas_call(
        functools.partial(branch_kernel, heads, pieces),
        grid=(rows // ROWS,),
        in_specs=[
            SCALARS, SCALARS, once(maps.shape), row(wide), row(wide), row(wide), fixed(gain.shape), once(w_out.shape),
        ]
        + [WHOLE] * len(waits),
        out_specs=[row(wide), row(wide), fixed((heads, DK, DV))]
        + [fixed((ROWS, model))] * (2 * pieces),
        out_shape=[shape((rows, wide)), shape((rows, wide), BF16), shape((heads, DK, DV))]
        + [shape((ROWS, model), BF16)] * (2 * pieces),
        scratch_shapes=[pltpu.VMEM((heads, DK, DV), F32)],
        compiler_params=params(14),
        cost_estimate=cost(3),
        name="branch_forward",
    )(place, who, maps, own, far, gate, gain, w_out, *waits)


def share_places(count):
    order, bit = [0], count // 2
    for bit in [1 << k for k in range(count.bit_length() - 1)][::-1]:
        order = order + [m | bit for m in order]
    return order


def keep_shares(step, value, me, kept, sent):
    count = 2 * kept.shape[0]
    width = value.shape[1] // count
    parts = in_order([value[:, m * width : (m + 1) * width] for m in range(count)], me)
    rows = pl.ds(pl.multiple_of(step * ROWS, ROWS), ROWS)
    for position, m in enumerate(share_places(count)):
        if position < count // 2:
            kept[position, rows] = parts[m]
        else:
            sent[position - count // 2, rows] = parts[m]


def ffn_kernel(count, filled, who, x, mine, other, *refs):
    grads, refs = refs[:count], refs[count:]
    gain, w_gate, w_up, w_down = refs[:4]
    (
        h_out, act_out, gg_out, gu_out, grad_out, kept, sent, dh_mine, dh_other, picked,
    ) = refs[4 + filled :]
    step = pl.program_id(0)
    pick_half(step, who[0], [mine], [other], picked)
    resid = x[...].astype(F32) + picked[...]
    h_two = (resid * rms_scale(resid) * gain[...]).astype(BF16)
    h_out[...] = h_two
    grad = jnp.concatenate(in_order([g[...] for g in grads], who[0]), axis=1)
    grad_out[...] = grad
    gate = mm(h_two, w_gate[...], NT)
    up = mm(h_two, w_up[...], NT)
    sig = jax.nn.sigmoid(gate)
    silu = gate * sig
    act = (silu * up).astype(BF16)
    act_out[...] = act
    grad_act = mm(grad, w_down[...], NT)
    grad_gate = (grad_act * up * sig * (1.0 + gate * (1.0 - sig))).astype(BF16)
    grad_up = (grad_act * silu).astype(BF16)
    gg_out[...] = grad_gate
    gu_out[...] = grad_up
    dh = (mm(grad_gate, w_gate[...]) + mm(grad_up, w_up[...])).astype(BF16)
    keep_half(step, who[0], dh, [dh_mine], [dh_other])
    keep_shares(step, mm(act, w_down[...]).astype(BF16), who[0], kept, sent)


def ffn_pass(piece, who, x_all, mine, other, grads, gain, w_gate, w_up, w_down, filled):
    rows, model = x_all.shape
    share, count = grads[0].shape[1], len(grads)
    hidden = w_gate.shape[0]
    row = lambda width: block((ROWS, width), lambda i: (2 * piece + i, 0))
    half = fixed((ROWS, model))
    shares = block((count // 2, 2 * ROWS, share), lambda i: (0, piece, 0))
    first = 8 + count
    return pl.pallas_call(
        functools.partial(ffn_kernel, count, len(filled)),
        grid=(2,),
        in_specs=[SCALARS, row(model), half, half]
        + [row(share)] * count
        + [fixed(gain.shape), once(w_gate.shape), once(w_up.shape), once(w_down.shape)]
        + [WHOLE] * len(filled),
        out_specs=[row(model), row(hidden), row(hidden), row(hidden), row(model)]
        + [shares] * 2
        + [half] * 2,
        out_shape=[
            shape((rows, model), BF16),
            shape((rows, hidden), BF16),
            shape((rows, hidden), BF16),
            shape((rows, hidden), BF16),
            shape((rows, model), BF16),
        ]
        + [shape((count // 2, rows, share), BF16)] * 2
        + [shape((ROWS, model), BF16)] * 2,
        scratch_shapes=[pltpu.VMEM((ROWS, model), F32)],
        input_output_aliases={first + k: k for k in range(len(filled))},
        compiler_params=params(32),
        cost_estimate=cost(10),
        name="ffn_pass",
    )(who, x_all, mine, other, *grads, gain, w_gate, w_up, w_down, *filled)


def fold(value):
    return jnp.sum(value.reshape(value.shape[0] // 8, 8, value.shape[1]), axis=0)


def resid_kernel(
    heads, pieces, who, x, *refs
):
    take = lambda k: refs[k * pieces : (k + 1) * pieces]
    branch_mine, branch_other, dh_mine, dh_other = take(0), take(1), take(2), take(3)
    (
        grad, gain, w_out, normed, attn, gate, out_gain, far,
        weight_out, attn_grad_out, gate_grad_out, resid_out,
        gain_grad_out, out_gain_grad_out, state_grad_out, resid_all, weight_sum, dh,
    ) = refs[4 * pieces :]
    step = pl.program_id(0)
    pick_half(step, who[0], branch_mine, branch_other, resid_all)
    pick_half(step, who[0], dh_mine, dh_other, dh)

    @pl.when(pl.program_id(0) == 0)
    def _():
        for total in (gain_grad_out, out_gain_grad_out, state_grad_out, weight_sum):
            total[...] = jnp.zeros_like(total)

    resid = x[...].astype(F32) + resid_all[...]
    scale = rms_scale(resid)
    unit = resid * scale
    grad_h = dh[...]
    gain_grad_out[...] += fold(grad_h * unit)
    lifted = grad_h * gain[...]
    grad_resid = grad[...].astype(F32) + scale * (
        lifted - unit * jnp.mean(lifted * unit, axis=-1, keepdims=True)
    )
    resid_all[...] = grad_resid
    share = resid_out.shape[1]
    resid_out[...] = resid_all[:, pl.ds(pl.multiple_of(who[0] * share, share), share)]
    grad_branch = grad_resid.astype(BF16)
    weight_sum[...] += mm(normed[...], grad_branch, TN)

    @pl.when(pl.program_id(0) == pl.num_programs(0) - 1)
    def _():
        weight_out[...] = weight_sum[...].astype(BF16)

    grad_normed = mm(grad_branch, w_out[...], NT)
    for h in range(heads):
        col = slice(h * DV, (h + 1) * DV)
        value, gates, back = attn[:, col], gate[:, col], grad_normed[:, col]
        scale_o = rms_scale(value)
        unit_o = value * scale_o
        sig = jax.nn.sigmoid(gates)
        silu = gates * sig
        gate_grad_out[:, col] = (
            back * unit_o * out_gain[...] * sig * (1.0 + gates * (1.0 - sig))
        ).astype(BF16)
        scaled = back * silu
        out_gain_grad_out[...] += fold(scaled * unit_o)
        lifted_o = scaled * out_gain[...]
        grad_attn = scale_o * (
            lifted_o - unit_o * jnp.mean(lifted_o * unit_o, axis=-1, keepdims=True)
        )
        attn_grad_out[:, col] = grad_attn
        state_grad_out[h] += mm(far[:, col], grad_attn, TN, P_STATE)


def resid_backward(heads, who, share, x_all, branch, dh, grad, gain, w_out, normed, attn, gate, out_gain, far):
    rows, model = x_all.shape
    wide = heads * DV
    row = lambda width: block((ROWS, width), lambda i: (i, 0))
    pieces = rows // (2 * ROWS)
    halves = [fixed((ROWS, model))] * (4 * pieces)
    return pl.pallas_call(
        functools.partial(resid_kernel, heads, pieces),
        grid=(rows // ROWS,),
        in_specs=[
            SCALARS, row(model), *halves, row(model), fixed(gain.shape), once(w_out.shape),
            row(wide), row(wide), row(wide), fixed(out_gain.shape), row(wide),
        ],
        out_specs=[fixed(w_out.shape), row(wide), row(wide), row(share)]
        + [fixed((8, model)), fixed((8, DV)), fixed((heads, DK, DV))],
        out_shape=[
            shape(w_out.shape, BF16),
            shape((rows, wide)),
            shape((rows, wide), BF16),
            shape((rows, share)),
            shape((8, model)),
            shape((8, DV)),
            shape((heads, DK, DV)),
        ],
        scratch_shapes=[
            pltpu.VMEM((ROWS, model), F32),
            pltpu.VMEM(w_out.shape, F32),
            pltpu.VMEM((ROWS, model), F32),
        ],
        compiler_params=params(60),
        cost_estimate=cost(9),
        name="resid_backward",
    )(
        who, x_all, *[b[0] for b in branch], *[b[1] for b in branch], *[d[0] for d in dh], *[d[1] for d in dh],
        grad, gain, w_out, normed, attn, gate, out_gain, far,
    )


def mixer_back_kernel(
    heads, ends, steps, marks, place, maps, state_grads, start, raw, raw_before, rim, conv, logits, alpha,
    inv, transfers, states, reads, attn_grad, gate_grad,
    grad_raw_out, tail_out, rim_out, sums_out, conv_out,
    ext, mixed_grad, carry,
):
    step = pl.program_id(0)
    at_step = steps - 1 - step
    span_start = marks[0] + at_step * BWD_SPAN
    wide = heads * QKV
    per = BWD_SPAN // CHUNK

    @pl.when(step == 0)
    def _():
        carry[...] = jnp.zeros_like(carry)
        count = maps.shape[0]

        def join(k, unused):
            at = (count - 1 - k) ^ place[0]
            for h in range(heads):
                carry[h] = (
                    mm(maps[at, h, :, DV:].astype(F32), carry[h], TN, P_STATE)
                    + state_grads[at, h].astype(F32)
                )
            return unused

        lax.fori_loop(0, count - 1 - place[0], join, 0)
        mixed_grad[0:8] = jnp.zeros((8, wide), F32)
        mixed_grad[8 + BWD_SPAN :] = jnp.zeros((8, wide), F32)
        sums_out[...] = jnp.zeros_like(sums_out)
        conv_out[...] = jnp.zeros_like(conv_out)

    @pl.when(step > 0)
    def _():
        mixed_grad[8 + BWD_SPAN :] = mixed_grad[8:16]

    @pl.when(at_step == 0)
    def _():
        ext[0:8] = rim[...]

    @pl.when(at_step > 0)
    def _():
        ext[0:8] = raw_before[...]

    ext[8 : 8 + BWD_SPAN] = raw[...]
    masks = conv_masks(span_start, marks, ends, BWD_SPAN, -1)
    apart, strict = token_masks()
    logit = logits[...]
    betas = jax.nn.sigmoid(logit)
    gates, sums, rows = gate_tiles(logit, alpha[...])

    parts = {}
    for h in range(heads):
        mixed = [convolved(ext, conv, masks, h, part) for part in range(5)]
        active = [m * jax.nn.sigmoid(m) for m in mixed]
        unit, scale = zip(*[unit_rows(active[part]) for part in range(3)])
        beta = [spread_column(betas, 3 * h + i) for i in range(NH)]
        parts[h] = (mixed, unit, scale, active[3:], beta)

    units = [(h, c) for h in range(heads) for c in range(per)]
    befores, grads_after = {}, {}
    for h in range(heads):
        for c in reversed(range(per)):
            at, col = slice(c * CHUNK, (c + 1) * CHUNK), slice(h * DK, (h + 1) * DK)
            befores[h, c] = states[c, h, :, :DV] + mm(
                states[c, h, :, DV:], start[h], NN, P_STATE
            )
        for c in reversed(range(per)):
            at, col = slice(c * CHUNK, (c + 1) * CHUNK), slice(h * DK, (h + 1) * DK)
            grads_after[h, c] = carry[h]
            carry[h] = mm(reads[at, col], attn_grad[at, col], TN, P_STATE) + mm(
                transfers[c, h], carry[h], TN, P_STATE
            )

    work = {}
    for h, c in units:
        _, unit, _, values, beta = parts[h]
        keys = pair(unit[1], unit[2], c)
        value = pair(values[0], values[1], c)
        beta_c = pair(beta[0], beta[1], c)
        query = unit[0][c * CHUNK : (c + 1) * CHUNK]
        decay, opening, closing, chunk_whole = chunk_gates(
            span_start, marks, ends, sums, rows, h, c
        )
        decay_two = jnp.concatenate([decay, decay], axis=0)
        opening_two = jnp.concatenate([opening, opening], axis=0)
        closing_two = jnp.concatenate([closing, closing], axis=0)
        grown = jnp.where(strict, decay_two * mm(keys, keys, NT, P_BWD), 0.0)
        read = decay * mm(query, keys, NT, P_BWD)
        recalled = opening_two * mm(keys, befores[h, c], NN, P_SOLVE)
        missing = value - recalled
        deltas = mm(inv[c, h], beta_c * missing, NN, P_SOLVE)
        at, col = slice(c * CHUNK, (c + 1) * CHUNK), slice(h * DK, (h + 1) * DK)
        out_grad = attn_grad[at, col]
        grad_deltas = mm(read, out_grad, TN, P_SOLVE) + mm(
            closing_two * keys, grads_after[h, c], NN, P_SOLVE
        )
        work[h, c] = [
            keys, query, beta_c, decay, decay_two, opening, opening_two, closing_two,
            grown, missing, deltas, out_grad, grad_deltas, chunk_whole,
        ]
    columns = {}
    for h, c in units:
        (
            keys, query, beta, decay, decay_two, opening, opening_two, closing_two,
            grown, missing, deltas, out_grad, grad_deltas, chunk_whole,
        ) = work[h, c]
        grad_target = mm(inv[c, h], grad_deltas, TN, P_SOLVE)
        grad_lower = jnp.where(strict, -mm(grad_target, deltas, NT, P_PAIR), 0.0)
        grad_beta = jnp.sum(grad_lower * grown, axis=-1, keepdims=True) + jnp.sum(
            grad_target * missing, axis=-1, keepdims=True
        )
        grad_pairs = grad_lower * beta * decay_two
        grad_value = beta * grad_target
        grad_read = decay * mm(out_grad, deltas, NT, P_PAIR)
        left = mm(grad_pairs, keys, NN, P_BWD) - beta * opening_two * mm(
            grad_target, befores[h, c], NT, P_BWD
        )
        closed = closing_two * mm(deltas, grads_after[h, c], NT, P_BWD)
        right = mm(grad_pairs, keys, TN, P_BWD) + closed + mm(grad_read, query, TN, P_BWD)
        grad_query = mm(grad_read, keys, NN, P_BWD) + opening * mm(
            out_grad, befores[h, c], NT, P_BWD
        )
        in_left = jnp.sum(keys * left, axis=-1, keepdims=True)
        in_right = jnp.sum(keys * right, axis=-1, keepdims=True)
        in_query = jnp.sum(query * grad_query, axis=-1, keepdims=True)
        spare = in_left - in_right
        grad_total = spare[:CHUNK] + spare[CHUNK:] + in_query
        whole = jnp.sum(keys * closed) + jnp.sum(
            chunk_whole * jnp.sum(grads_after[h, c] * befores[h, c], axis=0, keepdims=True)
        )
        last_row = iota((CHUNK, 1), 0) == CHUNK - 1
        grad_total = grad_total + jnp.where(last_row, whole, 0.0)
        columns[h, c] = (
            grad_query - query * in_query,
            left + right - keys * (in_left + in_right),
            grad_value,
            grad_beta,
            grad_total,
        )

    lane = iota((BWD_SPAN, DK), 1)
    rates = jnp.zeros((BWD_SPAN, DK), F32)
    for h in range(heads):
        mixed, unit, scale, values, beta = parts[h]
        got = [columns[h, c] for c in range(per)]
        low, high = slice(0, CHUNK), slice(CHUNK, 2 * CHUNK)
        stack = lambda index, part: jnp.concatenate([g[index][part] for g in got], axis=0)
        act_grads = [
            scale[0] * stack(0, low),
            scale[1] * stack(1, low),
            scale[2] * stack(1, high),
            stack(2, low),
            stack(2, high),
        ]
        for i, column in enumerate((stack(3, low), stack(3, high), stack(4, low))):
            rates = rates + jnp.where(lane == 3 * h + i, column, 0.0)
        for part in range(5):
            cols = part_columns(h, part)
            sig = jax.nn.sigmoid(mixed[part])
            grad = act_grads[part] * sig * (1.0 + mixed[part] * (1.0 - sig))
            mixed_grad[8 : 8 + BWD_SPAN, cols] = grad
            conv_out[24:32, cols] += fold(grad * ext[8 : 8 + BWD_SPAN, cols])
            for s in range(1, CONV):
                moved = jnp.where(masks[s], ext[8 - s : 8 - s + BWD_SPAN, cols], 0.0)
                tap = CONV - 1 - s
                conv_out[8 * tap : 8 * tap + 8, cols] += fold(grad * moved)

    ahead = conv_masks(span_start, marks, ends, BWD_SPAN, 1)
    for h in range(heads):
        for part in range(5):
            cols = part_columns(h, part)
            grad = mixed_grad[8 : 8 + BWD_SPAN, cols] * conv[CONV - 1 : CONV, cols]
            for s in range(1, CONV):
                moved = jnp.where(ahead[s], mixed_grad[8 + s : 8 + s + BWD_SPAN, cols], 0.0)
                grad = grad + moved * conv[CONV - 1 - s : CONV - s, cols]
            begin = h * MIXW + part * DK
            grad_raw_out[:, begin : begin + DK] = grad.astype(BF16)

            @pl.when(step == 0)
            def _():
                tail_out[:, cols] = grad[BWD_SPAN - HALO :]

        grad_raw_out[:, h * MIXW + QKV : (h + 1) * MIXW] = gate_grad[:, h * DV : (h + 1) * DV]

    @pl.when(at_step == 0)
    def _():
        rim_masks = conv_masks(marks[0] - 8, marks, ends, 8, 1)
        for h in range(heads):
            for part in range(5):
                cols = part_columns(h, part)
                grad = jnp.zeros((8, DK), F32)
                for s in range(1, CONV):
                    moved = jnp.where(rim_masks[s], mixed_grad[s : s + 8, cols], 0.0)
                    grad = grad + moved * conv[CONV - 1 - s : CONV - s, cols]
                rim_out[:, cols] = grad

    back = chunk_sums(True, rates)
    lanes = iota((1, DK), 1)
    is_gate = (lanes % (NH + 1) == NH) & (lanes < heads * (NH + 1))
    grad_logits = jnp.where(is_gate, back * alpha[...] * betas, rates * betas * (1.0 - betas))
    grad_raw_out[:, heads * MIXW :] = grad_logits.astype(BF16)
    sums_out[0:8] += fold(grad_logits)
    sums_out[8:16] += fold(back * gates)


def mixer_backward(
    heads, ends, marks, place, maps, state_grads, start, raw, rim, conv, logits, alpha,
    inv, transfers, states, reads, attn_grad, gate_grad,
):
    rows, wide = raw.shape
    steps, per = rows // BWD_SPAN, BWD_SPAN // CHUNK
    turn = lambda i: steps - 1 - i
    row = lambda width: block((BWD_SPAN, width), lambda i: (turn(i), 0))
    cube = lambda last: block((per, heads, TILE, last), lambda i: (turn(i), 0, 0, 0))
    return pl.pallas_call(
        functools.partial(mixer_back_kernel, heads, ends, steps),
        grid=(steps,),
        in_specs=[
            SCALARS,
            SCALARS,
            once(maps.shape),
            once(state_grads.shape),
            fixed(start.shape),
            row(wide),
            block((8, wide), lambda i: (jnp.maximum(turn(i) * (BWD_SPAN // 8) - 1, 0), 0)),
            fixed(rim.shape),
            fixed(conv.shape),
            row(DK),
            fixed(alpha.shape),
            cube(TILE),
            cube(DK),
            cube(DK + DV),
            row(heads * DK),
            row(heads * DV),
            row(heads * DV),
        ],
        out_specs=[
            row(heads * MIXW + DK),
            fixed((HALO, wide)),
            fixed((8, wide)),
            fixed((16, DK)),
            fixed((8 * CONV, wide)),
        ],
        out_shape=[
            shape((rows, heads * MIXW + DK), BF16),
            shape((HALO, wide)),
            shape((8, wide)),
            shape((16, DK)),
            shape((8 * CONV, wide)),
        ],
        scratch_shapes=[
            pltpu.VMEM((8 + BWD_SPAN, wide), F32),
            pltpu.VMEM((8 + BWD_SPAN + 8, wide), F32),
            pltpu.VMEM((heads, DK, DV), F32),
        ],
        compiler_params=params(60),
        cost_estimate=cost(50),
        name="mixer_backward",
    )(
        marks, place, maps, state_grads, start, raw, raw, rim, conv, logits, alpha,
        inv, transfers, states, reads, attn_grad, gate_grad,
    )


def weights_kernel(widths, orders, place, h_one, halo, grad, rim, out_weights, *outs):
    step, count = pl.program_id(0), pl.num_programs(0)
    total = mm(h_one[...], grad[...], TN) + mm(halo[...], rim[...], TN)
    total = jnp.concatenate([total, jnp.transpose(out_weights[...].astype(F32))], axis=1)
    at = 0
    for k, (width, order) in enumerate(zip(widths, orders)):
        value = total[:, at : at + width].astype(BF16)
        at += width
        position = weight_places(step, order)

        @pl.when(position < count // 2)
        def _():
            outs[2 * k][position] = value

        @pl.when(position >= count // 2)
        def _():
            outs[2 * k + 1][position - count // 2] = value


def weight_places(i, bits_in_order):
    position = 0
    for bit in bits_in_order:
        position = 2 * position + lax.rem(i // bit, 2)
    return position


def mixer_weights(place, ranges, h_one, halo, grad, rim, out_weights, widths, orders):
    rows, model = h_one.shape
    deep = model // ranges
    if deep % DK:
        whole = (t_dot(h_one, grad) + t_dot(halo, rim)).astype(BF16)
        whole = jnp.concatenate([whole, out_weights.T], axis=1).reshape(ranges, deep, -1)
        cuts, at = [], 0
        for width, order in zip(widths, orders):
            whole_cut = ordered(whole[:, :, at : at + width], order)
            cuts.append((whole_cut[: ranges // 2], whole_cut[ranges // 2 :]))
            at += width
        return cuts
    outs = pl.pallas_call(
        functools.partial(weights_kernel, widths, orders),
        grid_spec=pltpu.PrefetchScalarGridSpec(
            num_scalar_prefetch=1,
            grid=(ranges,),
            in_specs=[
                block((rows, deep), lambda i, place: (0, i ^ place[0])),
                block((HALO, deep), lambda i, place: (0, i ^ place[0])),
                block(grad.shape, lambda i, place: (0, 0)),
                block(rim.shape, lambda i, place: (0, 0)),
                block((out_weights.shape[0], deep), lambda i, place: (0, i ^ place[0])),
            ],
            out_specs=[
                block((ranges // 2, deep, width), lambda i, place: (0, 0, 0))
                for width in widths
                for _ in range(2)
            ],
        ),
        out_shape=[
            shape((ranges // 2, deep, width), BF16) for width in widths for _ in range(2)
        ],
        compiler_params=params(60),
        cost_estimate=cost(5),
        name="mixer_weights",
    )(place, h_one, halo, grad, rim, out_weights)
    return list(zip(outs[::2], outs[1::2]))


def input_kernel(heads, who, x, gain, grad, w_mixer, w_rates, gain_grad_out, kept, sent):
    step = pl.program_id(0)

    @pl.when(step == 0)
    def _():
        gain_grad_out[...] = jnp.zeros_like(gain_grad_out)
        rows = kept.shape[1] - HALO
        for out in (kept, sent):
            out[:, rows:] = jnp.zeros((out.shape[0], HALO, out.shape[2]), BF16)

    back = mm(grad[:, : heads * MIXW], w_mixer[...], NT) + mm(
        grad[:, heads * MIXW :], w_rates[...], NT
    )
    values = x[...].astype(F32)
    unit = values * rms_scale(values)
    seen = back * unit
    gain_grad_out[...] += fold(seen)
    keep_shares(step, back.astype(BF16), who[0], kept, sent)
    dots = jnp.sum(seen * gain[...], axis=-1, keepdims=True)
    dots = jnp.transpose(jnp.broadcast_to(dots, (ROWS, DK)))[:HALO]
    rows, share = kept.shape[1] - HALO, kept.shape[2]
    per = ROWS // share
    at = iota((HALO, share), 0)
    for k in range(per):
        line = jnp.where(at == step * per + k, dots[:, k * share : (k + 1) * share], 0.0)
        for out in (kept, sent):
            for j in range(out.shape[0]):
                out[j, rows:] = (out[j, rows:].astype(F32) + line).astype(BF16)


def input_backward(heads, count, who, x_all, gain, grad, w_mixer, w_rates):
    rows, model = x_all.shape
    share = model // count
    row = lambda width: block((ROWS, width), lambda i: (i, 0))
    return pl.pallas_call(
        functools.partial(input_kernel, heads),
        grid=(rows // ROWS,),
        in_specs=[
            SCALARS, row(model), fixed(gain.shape), row(grad.shape[1]), once(w_mixer.shape), once(w_rates.shape),
        ],
        out_specs=[fixed((8, model))] + [fixed((count // 2, rows + HALO, share))] * 2,
        out_shape=[shape((8, model))] + [shape((count // 2, rows + HALO, share), BF16)] * 2,
        compiler_params=params(60),
        cost_estimate=cost(6),
        name="input_backward",
    )(who, x_all, gain, grad, w_mixer, w_rates)


def tokens_kernel(model, who, x, gain, resid_grad, own_dots, came_dots, own, came, out):
    share = out.shape[1]
    cols = pl.ds(pl.multiple_of(who[0] * share, share), share)
    scale = rms_scale(x[...].astype(F32))
    unit = x[:, cols].astype(F32) * scale
    dots = own_dots[...].astype(F32) + came_dots[...].astype(F32)
    per = ROWS // share
    at = iota((HALO, share), 0)
    line = jnp.concatenate(
        [
            jnp.sum(jnp.where(at == pl.program_id(0) * per + k, dots, 0.0), axis=0, keepdims=True)
            for k in range(per)
        ],
        axis=1,
    )
    mean = jnp.transpose(jnp.broadcast_to(line, (8, ROWS)))[:, :1] / model
    back = (own[...].astype(F32) + came[...].astype(F32)) * gain[:, cols]
    out[...] = (resid_grad[...] + scale * (back - unit * mean)).astype(BF16)


def tokens_backward(who, x_all, gain, resid_grad, own, came):
    rows, model = x_all.shape
    share = own.shape[1]
    row = lambda width: block((ROWS, width), lambda i: (i, 0))
    extra = block((HALO, share), lambda i: (rows // HALO, 0))
    return pl.pallas_call(
        functools.partial(tokens_kernel, model),
        grid=(rows // ROWS,),
        in_specs=[
            SCALARS, row(model), fixed(gain.shape), row(share), extra, extra, row(share), row(share),
        ],
        out_specs=row(share),
        out_shape=shape((rows, share), BF16),
        compiler_params=params(10),
        cost_estimate=cost(2),
        name="tokens_backward",
    )(who, x_all, gain, resid_grad, own, came, own, came)


def shifted(value, axis, steps):
    count = lax.axis_size(axis)
    first, last = (max(0, -steps), min(count, count - steps))
    return lax.ppermute(value, axis, [(source, source + steps) for source in range(first, last)])


def swap(value, axis, mask):
    return lax.ppermute(value, axis, [(i, i ^ mask) for i in range(lax.axis_size(axis))])


def bits(axis):
    count, bit = lax.axis_size(axis), 1
    while bit < count:
        yield bit
        bit *= 2


def spread(value, axis, order, beside=()):
    found = {0: value}
    for at, bit in enumerate(order):
        came = {m | bit: swap(v, axis, bit) for m, v in list(found.items())}
        if at == 0 and beside:
            came[bit], *beside = tie(came[bit], *beside)
        found.update(came)
    return [found[m] for m in range(len(found))], beside


def spread_seq(value):
    found = {0: value}
    count = lax.axis_size("seq")
    for m in range(2, count, 2):
        found[m] = swap(value, "seq", m)
    for m in range(0, count, 2):
        found[m + 1] = swap(found[m], "seq", 1)
    return jnp.stack([found[m] for m in range(count)])


def tie(*values):
    return lax.optimization_barrier(values)


def core_sum(mine, other):
    return mine + swap(other, "head", 1)


def over_y(total, came):
    total = total + came
    for bit in bits("head"):
        if bit > 2:
            total = total + swap(total, "head", bit)
    return total, swap(total, "head", 1)


def summed_shares(kept, sent):
    for bit in bits("head"):
        came = swap(sent, "head", bit)
        half = kept.shape[0] // 2
        if half:
            sent = kept[half:] + came[half:]
            kept = kept[:half] + came[:half]
    return kept[0], came[0]


def summed(value, axis):
    for bit in bits(axis):
        value = value + swap(value, axis, bit)
    return value


def spread_small(value):
    found = [value] + [swap(value, "seq", m) for m in range(2, lax.axis_size("seq"), 2)]
    here = jnp.stack(found)
    there = swap(here, "seq", 1)
    return jnp.stack([here, there], axis=1).reshape((-1,) + value.shape)


def ordered(value, order):
    place = lax.axis_index("seq")
    positions = [0]
    for bit in order[::-1]:
        positions = positions + [m | bit for m in positions]
    return jnp.take(value, jnp.array(positions) ^ place, axis=0)


def first_exchange(cuts, orders):
    came = []
    for (_, sent), order in zip(cuts, orders):
        if came and order[0] == orders[0][0]:
            came[-1], sent = tie(came[-1], sent)
        came.append(swap(sent, "seq", order[0]))
    return came


def scattered(cuts, came, orders):
    kept = [k for k, _ in cuts]
    for stage in range(len(orders[0])):
        if stage:
            came = [swap(value, "seq", order[stage]) for value, order in zip(sent, orders)]
        half = kept[0].shape[0] // 2
        sent = [k[half:] + c[half:] for k, c in zip(kept, came)]
        kept = [k[: max(half, 1)] + c[: max(half, 1)] for k, c in zip(kept, came)]
    return [k[0] for k in kept]


def t_dot(leading, trailing):
    return lax.dot_general(leading, trailing, TN, preferred_element_type=F32)


def local(
    tokens, lengths, norm1_gain, w_mixer, w_rates, decay_log, rates_bias, conv_weight,
    out_gain, w_out, norm2_gain, w_ffn_gate, w_ffn_up, w_ffn_down, out_grad,
):
    rows, share = tokens.shape
    heads = decay_log.shape[0]
    ends = lengths.shape[0]
    model = norm1_gain.shape[0]
    group, ranges = lax.axis_size("head"), lax.axis_size("seq")
    place, member = lax.axis_index("seq"), lax.axis_index("head")
    marks = jnp.concatenate(
        [jnp.reshape(place * rows, (1,)), jnp.cumsum(lengths)]
    ).astype(jnp.int32)
    place_arg = jnp.reshape(place, (1,)).astype(jnp.int32)
    who = jnp.reshape(member, (1,)).astype(jnp.int32)
    down_bits = list(bits("head"))[::-1]
    seq_bits = list(bits("seq"))

    halo = shifted(tokens[rows - HALO :], "seq", 1)
    gain_one, gain_two = norm1_gain[None, :], norm2_gain[None, :]
    gain_out = out_gain[None, :]
    spare = DK - heads * (NH + 1)
    rates_w = jnp.pad(w_rates, ((0, 0), (0, spare)))
    bias = jnp.pad(rates_bias, (0, spare))[None, :]
    none = jnp.zeros((heads,), F32)
    alpha = jnp.stack([none] * NH + [-jnp.exp(decay_log)], axis=-1).reshape(-1)
    alpha = jnp.pad(alpha, (0, spare))[None, :]

    token_parts, (marks, rates_w, bias, alpha) = spread(
        jnp.concatenate([tokens, halo], axis=0), "head", down_bits, (marks, rates_w, bias, alpha)
    )
    (
        x_all, h_one, h_halo, raw, rim, gate_o, logits, inv, transfers, states, reads, own, far, end_state,
    ) = mixer_forward(
        heads, ends, marks, who, token_parts, gain_one, w_mixer, rates_w, bias, alpha, conv_weight
    )
    out_grad, end_state = tie(out_grad, end_state)
    grad_parts, _ = spread(out_grad, "head", down_bits)
    maps = spread_seq(end_state)
    attn, normed, start, *branch = branch_forward(
        heads, place_arg, who, maps, own, far, gate_o, gain_out, w_out, grad_parts
    )
    pieces = len(branch) // 2
    halves = [core_sum(branch[p], branch[pieces + p]) for p in range(pieces)]
    sent_y = [swap(halves[0], "head", 2)]
    for p in range(1, pieces):
        sent_y[-1], halves[p] = tie(sent_y[-1], halves[p])
        sent_y.append(swap(halves[p], "head", 2))
    branch, dh_halves, dh, filled = [], [], [], []
    gate_t, up_t = w_ffn_gate.T, w_ffn_up.T
    for p in range(pieces):
        if p:
            sent_y[p], *filled = tie(sent_y[p], *filled)
        branch.append(over_y(halves[p], sent_y[p]))
        *filled, dh_mine, dh_other = ffn_pass(
            p, who, x_all, *branch[p], grad_parts, gain_two, gate_t, up_t, w_ffn_down, filled
        )
        if p:
            dh_y, dh_other = tie(dh_y, dh_other)
            dh.append(over_y(dh_halves[p - 1], dh_y))
        dh_halves.append(core_sum(dh_mine, dh_other))
        dh_y = swap(dh_halves[p], "head", 2)
    h_two, act, grad_gate, grad_up, grad_full, kept, sent = filled
    dh_halves[-1], act, grad_gate, grad_up = tie(dh_halves[-1], act, grad_gate, grad_up)
    by_owner = lambda value: jnp.swapaxes(
        value.reshape(value.shape[0], ranges, model // ranges), 0, 1
    ).astype(BF16)
    ffn_grads = jnp.concatenate(
        [by_owner(t_dot(act, grad_full)), by_owner(t_dot(grad_gate, h_two)), by_owner(t_dot(grad_up, h_two))],
        axis=1,
    )
    dh_y, ffn_grads = tie(dh_y, ffn_grads)
    ffn_grads = lax.psum_scatter(ffn_grads, "seq", scatter_dimension=0, tiled=False)
    dh.append(over_y(dh_halves[-1], dh_y))
    hidden = act.shape[1]
    (
        out_weights, grad_attn, grad_gate_o, resid_own, gain_two_part, out_gain_part, state_grad,
    ) = resid_backward(
        heads, who, share, x_all, branch, dh, grad_full, gain_two, w_out, normed, attn, gate_o, gain_out, far
    )

    sent, state_grad = tie(sent, state_grad)
    state_grads = spread_small(state_grad.astype(BF16))
    grad_raw, tail, rim_grad, sums, conv_parts = mixer_backward(
        heads, ends, marks, place_arg, maps, state_grads, start, raw, rim, conv_weight, logits, alpha,
        inv, transfers, states, reads, grad_attn, grad_gate_o,
    )
    rim_wide = jnp.pad(rim_grad, ((HALO - 8, 0), (0, 0))).astype(BF16)
    none = jnp.zeros((HALO, MIXW - QKV), BF16)
    rim_wide = jnp.concatenate(
        [b for h in range(heads) for b in (rim_wide[:, h * QKV : (h + 1) * QKV], none)]
        + [jnp.zeros((HALO, DK), BF16)],
        axis=1,
    )
    cut_widths = [MIXW] * (heads - 1) + [512, 256, DK + heads * DV]
    orders = [seq_bits] * (heads + 1) + [seq_bits[1:] + seq_bits[:1]]
    cuts = mixer_weights(
        place_arg, ranges, h_one, h_halo, grad_raw, rim_wide, out_weights, cut_widths, orders
    )
    cuts, ffn_grads, conv_parts, sums, rim_grad, kept = tie(
        cuts, ffn_grads, conv_parts, sums, rim_grad, kept
    )
    grad_down, grad_wgate, grad_wup = (
        ffn_grads[k * hidden : (k + 1) * hidden].astype(F32) for k in range(3)
    )
    came = first_exchange(cuts, orders)
    came[0], grad_raw = tie(came[0], grad_raw)
    first, second = summed_shares(kept, sent)
    own_cols = lambda value: lax.dynamic_slice_in_dim(value, member * share, share, 1)
    even = member % 2 == 0
    branch_own = []
    for mine, other in branch:
        mine, other = own_cols(mine), own_cols(other)
        branch_own += [jnp.where(even, mine, other), jnp.where(even, other, mine)]
    output = (
        tokens.astype(F32)
        + jnp.concatenate(branch_own, axis=0).astype(F32)
        + (first.astype(F32) + second.astype(F32))
    ).astype(BF16)
    tail = tail.at[HALO - 8 :].add(shifted(rim_grad, "seq", -1))
    for h in range(heads):
        grad_raw = lax.dynamic_update_slice(
            grad_raw, tail[:, h * QKV : (h + 1) * QKV].astype(BF16), (rows - HALO, h * MIXW)
        )
    gain_one_part, back_kept, back_sent = input_backward(
        heads, group, who, x_all, gain_one, grad_raw, w_mixer, rates_w
    )
    back_own, back_came = summed_shares(back_kept, back_sent)
    sum_rows = jnp.sum(sums.reshape(2, 8, DK), axis=1)
    small = jnp.concatenate(
        [
            jnp.sum(gain_one_part, axis=0),
            jnp.sum(out_gain_part, axis=0),
            jnp.sum(gain_two_part, axis=0),
            sum_rows[0],
            sum_rows[1],
            jnp.sum(conv_parts.reshape(CONV, 8, heads * QKV), axis=1).reshape(-1),
        ]
    )
    small = small.reshape(-1, DK)
    came[-2], small, back_own = tie(came[-2], small, back_own)
    cuts = scattered(cuts, came, orders)
    tokens_grad = tokens_backward(who, x_all, gain_one, resid_own, back_own, back_came)
    grad_wmixer = jnp.concatenate(cuts[:-1], axis=1).astype(F32)
    grad_wrates = cuts[-1][:, : heads * (NH + 1)].astype(F32)
    grad_wout = cuts[-1][:, DK:].T.astype(F32)

    small = summed(small, "seq").reshape(-1)
    cut = [model, DV, model, DK, DK]
    pieces_of, at = [], 0
    for size in cut:
        pieces_of.append(small[at : at + size])
        at += size
    over_head = summed(small[: model + DV], "head")
    grad_norm1, grad_outgain = over_head[:model], over_head[model:]
    _, _, grad_norm2, bias_row, decay_row = pieces_of
    grad_conv = small[at:].reshape(CONV, heads * QKV)
    grad_bias = bias_row[: heads * (NH + 1)]
    grad_decay = decay_row[: heads * (NH + 1)].reshape(heads, NH + 1)[:, NH]
    return (
        output, tokens_grad, grad_norm1, grad_wmixer, grad_wrates, grad_decay, grad_bias, grad_conv,
        grad_outgain, grad_wout, grad_norm2, grad_wgate.T, grad_wup.T, grad_down,
    )


def solution(mesh):
    placed = (
        P("seq", "head"), P(), P(), P(None, "head"), P(None, "head"), P("head"), P("head"), P(None, "head"),
        P(), P("head", None), P(), P(None, "head"), P(None, "head"), P("head", None), P("seq", "head"),
    )
    return jax.shard_map(
        local,
        mesh=mesh,
        in_specs=placed,
        out_specs=(
            P("seq", "head"), P("seq", "head"), P(), P("seq", "head"), P("seq", "head"), P("head"), P("head"),
            P(None, "head"), P(), P("head", "seq"), P(), P("seq", "head"), P("seq", "head"), P("head", "seq"),
        ),
        check_vma=False,
    )
```
